32 devices in a mesh: grp: 4 (over y, core), tile: 8 (over z, x).
Axes of the slice: x: 2, y: 2, z: 4, core: 2. Of those that a mesh axis runs over, the one named last changes fastest.
Arguments:
- material: int32 [6, 1536, 2048], P(None, 'grp', 'tile'), may hold values from 0 to 7
- conduct_table: float32 [8], replicated, may hold values from 1 to 20
- heat_sink: float32 [1536, 2048], P('grp', 'tile'), may hold values from 1 to 10
- heat_source: float32 [6, 1536, 2048], P(None, 'grp', 'tile'), may hold values from -120 to 120
- die_power: float32 [192, 128, 128], P(('grp', 'tile')), may hold values from -60 to 60
- die_conduct: float32 [192], P(('grp', 'tile')), may hold values from 1 to 8
- bond_conductance: float32 [192], P(('grp', 'tile')), may hold values from 0.5 to 4
- tile_place: int32 [192], P(('grp', 'tile')), may hold values from -1 to 191, as said below
Outputs:
- interposer_temp: float32 [6, 1536, 2048], P(None, 'grp', 'tile')
- die_temp: float32 [192, 128, 128], P(('grp', 'tile'))
The draws below stay inside these ranges and needn't reach their ends.
Inputs may be any that keep to these rules, and one draw needn't show every extreme that they name: `tile_place`: -1 marks an empty slot; the other entries are distinct tile positions; one device holds all 6 of its slots filled and every device at least one.
All inputs are finite; a program needn't handle non-finite values.
Results may differ from the reference program's by a relative error of at most 0.0003.
Values sent between devices are 32-bit elements; how exact they have to be, the bound alone decides.
A program may use at most 192 MiB of HBM per device.

```python
import math
import jax
import jax.numpy as jnp

LAYERS = 6
MATS = 8
TS = 128
RATIO = 8
NU = 2
NC = 4
TILE_DEV = 6
TILES = 192
NX = 1536
NY = 2048


def draw_tile_place(key, part):
    device_count = TILES // TILE_DEV
    keys = jax.random.split(jax.random.fold_in(key, 17), 5)
    full_device = jax.random.randint(keys[0], (), 0, device_count)
    counts = 1 + jax.random.randint(keys[1], (device_count,), 0, TILE_DEV // 2)
    counts = jnp.where(jnp.arange(device_count) == full_device, TILE_DEV, counts)
    scores = jax.random.randint(keys[2], (device_count, TILE_DEV), 0, 1 << 20) * TILE_DEV + jnp.arange(TILE_DEV)[None, :]
    rank_local = jnp.argsort(jnp.argsort(scores, axis=1), axis=1)
    filled = (rank_local < counts[:, None]).reshape(TILES)
    slot_keys = jnp.where(filled, 0, 1) * TILES + jax.random.permutation(keys[3], TILES)
    slot_order = jnp.argsort(slot_keys)
    position_order = jax.random.permutation(keys[4], TILES)
    total = jnp.sum(filled.astype(jnp.int32))
    placed = jnp.where(jnp.arange(TILES) < total, position_order, -1).astype(jnp.int32)
    return jnp.zeros((TILES,), jnp.int32).at[slot_order].set(placed).astype(jnp.int32)


def with_ends(array, own_key, low, largest):
    longest = array.shape.index(max(array.shape))
    spots = []
    for shift in (0, 1):
        where = [jax.random.randint(jax.random.fold_in(own_key, axis), (), 0, length) for axis, length in enumerate(array.shape)]
        where[longest] = (where[longest] + shift) % array.shape[longest]
        spots.append(tuple(where))
    return array.at[spots[0]].set(low).at[spots[1]].set(largest)


def steps_of(stream_key, dims, pieces, least, top_value):
    def one(dim, shards_of):
        heights = jax.random.uniform(jax.random.fold_in(jax.random.fold_in(stream_key, 6), dim), (shards_of,), jnp.float32, least / len(pieces), top_value / len(pieces))
        return jnp.repeat(jnp.exp(heights), dims[dim] // shards_of).reshape((-1,) + (1,) * (len(dims) - dim - 1))

    level = one(*pieces[0])
    for cut in pieces[1:]:
        level = level * one(*cut)
    return level


def normal_values(stream_key, dims, width, bound, cuts=(), kind=jnp.bfloat16):
    level = steps_of(stream_key, dims, cuts, -0.22, 0.18) if cuts else 1.0
    values = jax.random.normal(stream_key, dims, jnp.float32) * width * level
    return jnp.minimum(jnp.maximum(values, -bound), bound).astype(kind)


def setup_inputs(seed: int = 0) -> dict:
    key_list = jax.random.split(jax.random.key(seed), 9)
    return {
        "material": with_ends(jax.random.randint(key_list[0], (LAYERS, NX, NY), 0, MATS), jax.random.fold_in(key_list[0], 1), 0, MATS - 1).astype(jnp.int32),
        "conduct_table": jnp.clip(jnp.exp(jax.random.uniform(key_list[1], (MATS,), jnp.float32, math.log(1.0), math.log(20.0))), 1.0, 20.0),
        "heat_sink": jnp.clip(jnp.exp(math.log(10.0) - 2.3025851 * jax.random.uniform(key_list[2], (NX, NY), jnp.float32) ** steps_of(key_list[2], (NX, NY), ((0, 4), (1, 8)), -0.2, 0.2)), 1.0, 10.0),
        "heat_source": normal_values(key_list[3], (LAYERS, NX, NY), 20.0, 120.0, ((1, 4), (2, 8)), jnp.float32),
        "die_power": normal_values(key_list[4], (TILES, TS, TS), 10.0, 60.0, ((0, 32),), jnp.float32),
        "die_conduct": jnp.clip(jnp.exp(math.log(8.0) - 2.0794415 * jax.random.uniform(key_list[5], (TILES,), jnp.float32) ** steps_of(key_list[5], (TILES,), ((0, 32),), -0.2, 0.2)), 1.0, 8.0),
        "bond_conductance": jnp.clip(jnp.exp(math.log(4.0) - 2.0794415 * jax.random.uniform(key_list[6], (TILES,), jnp.float32) ** steps_of(key_list[6], (TILES,), ((0, 32),), -0.2, 0.2)), 0.5, 4.0),
        "tile_place": draw_tile_place(jax.random.fold_in(key_list[8], 71), 0),
    }


relax_weight = 0.8


def harmonic(lower_side, upper_side):
    total = lower_side + upper_side
    return 2.0 * lower_side * upper_side / jnp.where(total > 0, total, 1.0)


def neighbours(padded):
    return (padded[:-2, 1:-1, 1:-1], padded[2:, 1:-1, 1:-1], padded[1:-1, :-2, 1:-1],
            padded[1:-1, 2:, 1:-1], padded[1:-1, 1:-1, :-2], padded[1:-1, 1:-1, 2:])


def grid_faces(padded, vertical):
    centre = padded[1:-1, 1:-1, 1:-1]
    scales = (vertical, vertical, 1.0, 1.0, 1.0, 1.0)
    return tuple(harmonic(centre, other) * weight_value for other, weight_value in zip(neighbours(padded), scales))


def grid_residual(padded, faces, extra, source):
    centre = padded[1:-1, 1:-1, 1:-1]
    flux_sum = extra * centre
    diagonal = extra
    for face, other in zip(faces, neighbours(padded)):
        flux_sum = flux_sum + face * (centre - other)
        diagonal = diagonal + face
    return source - flux_sum, diagonal


def grid_sweep(padded, faces, extra, source):
    residual_part, diagonal = grid_residual(padded, faces, extra, source)
    centre = padded[1:-1, 1:-1, 1:-1]
    return centre + relax_weight * residual_part / jnp.where(diagonal > 0, diagonal, 1.0)


def in_block(length, block_size, offset):
    relative = (jnp.arange(length) - offset) % block_size
    return (relative != 0).astype(jnp.float32), (relative != block_size - 1).astype(jnp.float32)


def die_faces(conduct, block_size, offset):
    lower_x, upper_x = in_block(conduct.shape[-2], block_size, offset)
    lower_y, upper_y = in_block(conduct.shape[-1], block_size, offset)
    return (conduct * lower_x[:, None], conduct * upper_x[:, None], conduct * lower_y[None, :], conduct * upper_y[None, :])


def die_residual(field, faces, couple, top_field, source):
    widths = [(0, 0)] * (field.ndim - 2) + [(1, 1), (1, 1)]
    padded = jnp.pad(field, widths)
    views = (padded[..., :-2, 1:-1], padded[..., 2:, 1:-1], padded[..., 1:-1, :-2], padded[..., 1:-1, 2:])
    flux_sum = couple * field
    diagonal = couple
    for face, other in zip(faces, views):
        flux_sum = flux_sum + face * (field - other)
        diagonal = diagonal + face
    return source + couple * top_field - flux_sum, diagonal


def die_sweep(field, faces, couple, top_field, source):
    residual_part, diagonal = die_residual(field, faces, couple, top_field, source)
    return field + relax_weight * residual_part / jnp.where(diagonal > 0, diagonal, 1.0)


def coarsen(field, factor):
    shape = field.shape
    split = field.reshape(shape[:-2] + (shape[-2] // factor, factor, shape[-1] // factor, factor))
    return split.sum(axis=(-3, -1))


def refine(field, factor):
    return jnp.repeat(jnp.repeat(field, factor, axis=-2), factor, axis=-1)


def on_layers(bottom, top_layer, layer_count):
    middle = jnp.zeros((layer_count - 2,) + bottom.shape, jnp.float32)
    return jnp.concatenate([bottom[None], middle, top_layer[None]], 0)


def cell_conduct(material, conduct_table):
    values = jnp.zeros(material.shape, jnp.float32)
    for kind in range(conduct_table.shape[0]):
        values = values + jnp.where(material == kind, conduct_table[kind], 0.0)
    return values


def blocks_to_field(blocks, blocks_down, blocks_across):
    edge_cells = blocks.shape[-1]
    shaped = blocks.reshape(blocks_down, blocks_across, edge_cells, edge_cells)
    return shaped.transpose(0, 2, 1, 3).reshape(blocks_down * edge_cells, blocks_across * edge_cells)


def field_to_blocks(field, blocks_down, blocks_across, edge_cells):
    shaped = field.reshape(blocks_down, edge_cells, blocks_across, edge_cells)
    return shaped.transpose(0, 2, 1, 3).reshape(blocks_down * blocks_across, edge_cells, edge_cells)


def reference(material, conduct_table, heat_sink, heat_source, die_power, die_conduct, bond_conductance, tile_place):
    layer_count, row_count, col_count = material.shape
    block_edge = die_power.shape[1]
    coarse_block = block_edge // RATIO
    blocks_down = row_count // block_edge
    blocks_across = col_count // block_edge
    area = float(RATIO * RATIO)
    cell_values = cell_conduct(material, conduct_table)
    fine_faces = grid_faces(jnp.pad(cell_values, 1), 1.0)
    fine_extra = on_layers(heat_sink, jnp.zeros_like(heat_sink), layer_count)
    interposer = jnp.zeros_like(heat_source)
    for repeat_index in range(NU):
        interposer = grid_sweep(jnp.pad(interposer, 1), fine_faces, fine_extra, heat_source)
    fine_resid = grid_residual(jnp.pad(interposer, 1), fine_faces, fine_extra, heat_source)[0]

    filled = (tile_place >= 0).astype(jnp.float32)
    ones_block = jnp.ones((1, block_edge, block_edge), jnp.float32)
    slot_faces = die_faces(die_conduct[:, None, None] * ones_block, block_edge, 0)
    slot_couple = bond_conductance[:, None, None] * ones_block
    zero_top = jnp.zeros_like(die_power)
    die_field = jnp.zeros_like(die_power)
    for repeat_index in range(NU):
        die_field = die_sweep(die_field, slot_faces, slot_couple, zero_top, die_power)
    die_resid = die_residual(die_field, slot_faces, slot_couple, zero_top, die_power)[0] * filled[:, None, None]

    coarse_rhs = coarsen(fine_resid, RATIO)
    die_coarse = coarsen(die_resid, RATIO)
    index_safe = jnp.maximum(tile_place, 0).astype(jnp.int32)
    pos_rhs = jnp.zeros_like(die_coarse).at[index_safe].add(die_coarse)
    pos_conduct = jnp.zeros(tile_place.shape, jnp.float32).at[index_safe].add(die_conduct * filled)
    pos_couple = jnp.zeros(tile_place.shape, jnp.float32).at[index_safe].add(bond_conductance * area * filled)
    coarse_ones = jnp.ones((1, coarse_block, coarse_block), jnp.float32)
    top_rhs = blocks_to_field(pos_rhs, blocks_down, blocks_across)
    top_conduct = blocks_to_field(pos_conduct[:, None, None] * coarse_ones, blocks_down, blocks_across)
    top_couple = blocks_to_field(pos_couple[:, None, None] * coarse_ones, blocks_down, blocks_across)

    coarse_k = coarsen(cell_values, RATIO) / area
    coarse_sink = coarsen(heat_sink, RATIO)
    coarse_faces = grid_faces(jnp.pad(coarse_k, 1), area)
    top_faces = die_faces(top_conduct, coarse_block, 0)
    coarse_extra = on_layers(coarse_sink, top_couple, layer_count)
    coarse_error = jnp.zeros_like(coarse_rhs)
    top_error = jnp.zeros_like(top_rhs)
    for repeat_index in range(NC):
        pull_term = on_layers(jnp.zeros_like(coarse_sink), top_couple * top_error, layer_count)
        next_error = grid_sweep(jnp.pad(coarse_error, 1), coarse_faces, coarse_extra, coarse_rhs + pull_term)
        top_error = die_sweep(top_error, top_faces, top_couple, coarse_error[-1], top_rhs)
        coarse_error = next_error

    interposer = interposer + refine(coarse_error, RATIO)
    slot_error = field_to_blocks(top_error, blocks_down, blocks_across, coarse_block)[index_safe] * filled[:, None, None]
    die_field = die_field + refine(slot_error, RATIO)
    for repeat_index in range(NU):
        interposer = grid_sweep(jnp.pad(interposer, 1), fine_faces, fine_extra, heat_source)
    for repeat_index in range(NU):
        die_field = die_sweep(die_field, slot_faces, slot_couple, zero_top, die_power)
    return interposer, die_field * filled[:, None, None]
```

```python
import functools
import jax
import jax.numpy as jnp
from jax import lax
from jax.experimental import pallas as pl
from jax.experimental.pallas import tpu as pltpu
from jax.sharding import PartitionSpec as P

RATIO = 8
NU = 2
NC = 4
RELAX = 0.8
HALO = 4
TOP = 16
LANES = 128
FAR = 1e30
TINY = 1e-25
UNROLL = 2
MESH = pl.DeviceIdType.MESH
HIGHEST = lax.Precision.HIGHEST
DIRECTIONS = ((-1, 0), (1, 0), (0, -1), (0, 1), (-1, -1), (-1, 1), (1, -1), (1, 1), (-1, 0), (1, 0))
N_ROUGH = 8


def inverse(x):
    return pltpu.reciprocal(x, approx=True)


def harmonic(a, b):
    total = a + b
    return 2.0 * a * b * inverse(jnp.where(total > 0, total, 1.0))


def guarded_weight(d):
    return RELAX * inverse(jnp.where(d > TINY, d, 1.0))


def iota(shape, dim):
    return lax.broadcasted_iota(jnp.int32, shape, dim)


def shift(x, amount, axis):
    return pltpu.roll(x, amount % x.shape[axis], axis)


def row_sums(fields):
    shape = fields[0].shape
    row = lax.broadcasted_iota(jnp.int32, shape, 0)
    xs = list(fields) + [jnp.zeros(shape, jnp.float32)] * (8 - len(fields))

    def merge(x, y, start, run):
        first = ((row - start + 8) % 8) % (2 * run) < run
        return jnp.where(first, x, y) + shift(jnp.where(first, y, x), -run, 0)

    z = [merge(xs[j], xs[j + 4], j, 4) for j in range(4)]
    y = [merge(z[j], z[j + 2], j, 2) for j in range(2)]
    return merge(y[0], y[1], 0, 1)


def two_part_dot(a, b):
    high = a.astype(jnp.bfloat16)
    low = (a - high.astype(jnp.float32)).astype(jnp.bfloat16)
    b = b.astype(jnp.bfloat16)
    return jnp.dot(high, b, preferred_element_type=jnp.float32) + jnp.dot(
        low, b, preferred_element_type=jnp.float32
    )


def dot(a, b):
    return jnp.dot(a, b, precision=HIGHEST, preferred_element_type=jnp.float32)


def kernel(
    grp_count,
    tile_count,
    material,
    table,
    heat_sink,
    source,
    die_power,
    die_conduct,
    bond,
    place,
    out,
    die_out,
    field,
    zx,
    zy,
    zz,
    diag,
    weight,
    ua,
    ub,
    packed,
    turned,
    from_side,
    outer,
    strip,
    sx,
    sy,
    sz,
    sw,
    su,
    lines,
    sums,
    folded,
    rough,
    rough_side,
    rough_row,
    rough_corner,
    dies,
    die_message,
    all_dies,
    die_fix,
    all_fixes,
    wide,
    spread,
    send_sem,
    recv_sem,
    gather_send,
    gather_recv,
):
    layers, rows, cols = material.shape
    slots, edge, _ = die_power.shape
    cell = edge // RATIO
    down, across = rows // edge, cols // edge
    crows, ccols = rows // RATIO, cols // RATIO
    panes = cols // LANES
    long = rows + LANES
    height = rows + 2 * TOP
    n_fields = 2 * layers + 1
    area = float(RATIO * RATIO)
    per = LANES // ccols
    count = grp_count * tile_count
    g = lax.axis_index("grp")
    t = lax.axis_index("tile")
    me = g * tile_count + t

    def peer(offset):
        other = lax.rem(me + offset, count)
        return other, (other // tile_count, lax.rem(other, tile_count))

    def exists(dy, dx):
        ok = jnp.bool_(True)
        if dy:
            ok = jnp.logical_and(ok, g > 0 if dy < 0 else g < grp_count - 1)
        if dx:
            ok = jnp.logical_and(ok, t > 0 if dx < 0 else t < tile_count - 1)
        return ok

    for top in (0, height - TOP):
        field[0:layers, :, top : top + TOP, :] = jnp.full((layers, panes, TOP, LANES), FAR, jnp.float32)
        field[layers:n_fields, :, top : top + TOP, :] = jnp.zeros(
            (n_fields - layers, panes, TOP, LANES), jnp.float32
        )
    cut = HALO * layers
    from_side[:, 0:cut, :] = jnp.full((2, cut, rows), FAR, jnp.float32)
    from_side[:, cut:, :] = jnp.zeros((2, from_side.shape[1] - cut, rows), jnp.float32)
    outer[...] = jnp.where(iota(outer.shape, 2) % 64 < cut, FAR, 0.0)
    rough_side[...] = jnp.zeros_like(rough_side)
    rough_row[...] = jnp.zeros_like(rough_row)
    rough_corner[...] = jnp.zeros_like(rough_corner)
    zx[:, :, 0:8, :] = jnp.zeros((layers, panes, 8, LANES), jnp.float32)

    barrier = pltpu.get_barrier_semaphore()

    @pl.loop(1, count)
    def _(offset):
        pl.semaphore_signal(barrier, inc=1, device_id=peer(offset)[1], device_id_type=MESH)

    lane8 = iota((8, LANES), 1)
    sub8 = iota((8, LANES), 0)

    def right_lane(f):
        return HALO * f

    def left_lane(f):
        return 64 + 8 * (f // 2) + HALO * (1 - f % 2)

    doubled = [jnp.full((8, LANES), 2.0 * table[m], jnp.float32) for m in range(table.shape[0])]

    @pl.loop(0, rows // 8)
    def _(i):
        r = pl.multiple_of(i * 8, 8)
        edges = jnp.zeros((8, LANES), jnp.float32)
        summed = [[] for _ in range(panes)]
        for f in range(n_fields):
            xs = []
            for p in range(panes):
                part = slice(p * LANES, (p + 1) * LANES)
                if f < layers:
                    kind = material[f, pl.ds(r, 8), part]
                    values = list(doubled)
                    bit = 1
                    while len(values) > 1:
                        odd = (kind & bit) != 0
                        values = [
                            jnp.where(odd, values[m + 1], values[m]) if m + 1 < len(values) else values[m]
                            for m in range(0, len(values), 2)
                        ]
                        bit *= 2
                    summed[p].append(values[0])
                    x = inverse(values[0])
                elif f < 2 * layers:
                    x = source[f - layers, pl.ds(r, 8), part]
                else:
                    x = heat_sink[pl.ds(r, 8), part]
                    summed[p].append(x)
                field[f, p, pl.ds(TOP + r, 8), :] = x
                xs.append(x)
            a, b = right_lane(f), left_lane(f)
            right = shift(xs[-1], HALO + a, 1)
            left = shift(xs[0], b, 1)
            edges = jnp.where((lane8 >= a) & (lane8 < a + HALO), right, edges)
            edges = jnp.where((lane8 >= b) & (lane8 < b + HALO), left, edges)
        packed[pl.ds(r, 8), :] = edges
        for p in range(panes):
            sums[pl.ds(r, 8), p * LANES : (p + 1) * LANES] = row_sums(summed[p])

    turned[...] = packed[...].T

    pl.semaphore_wait(barrier, count - 1)

    depth = from_side.shape[1]

    def halo_copy(k):
        dy, dx = DIRECTIONS[k]
        if k < 2:
            src = field.at[:, :, pl.ds(TOP if dy < 0 else height - TOP - 8, 8), :]
            dst = field.at[:, :, pl.ds(height - TOP if dy < 0 else TOP - 8, 8), :]
        elif dy == 0:
            src = turned.at[pl.ds(0 if dx > 0 else 64, depth), :]
            dst = from_side.at[0 if dx > 0 else 1]
        else:
            src = packed.at[pl.ds(0 if dy < 0 else rows - 8, 8), :]
            which = 2 if dx == 0 else (0 if dx > 0 else 1)
            dst = outer.at[which, pl.ds(0 if dy < 0 else LANES - 8, 8), :]
        return pltpu.make_async_remote_copy(
            src_ref=src, dst_ref=dst, send_sem=send_sem.at[k], recv_sem=recv_sem.at[k],
            device_id=(g + dy, t + dx), device_id_type=MESH,
        )

    def rough_copy(k, phase):
        dy, dx = DIRECTIONS[k]
        half = pl.ds(2 * phase, 2)
        if dy == 0:
            src = rough.at[half]
            dst = rough_side.at[k - 2, half]
        else:
            src = rough.at[half, pl.ds(0 if dy < 0 else crows - 8, 8), :]
            dst = (rough_row.at[k, half] if dx == 0 else rough_corner.at[k - 4, half])
        s = len(DIRECTIONS) + N_ROUGH * phase + k
        return pltpu.make_async_remote_copy(
            src_ref=src, dst_ref=dst, send_sem=send_sem.at[s], recv_sem=recv_sem.at[s],
            device_id=(g + dy, t + dx), device_id_type=MESH,
        )

    def start_all(make, n):
        for k, (dy, dx) in enumerate(DIRECTIONS[:n]):
            pl.when(exists(dy, dx))(lambda k=k: make(k).start())

    def wait_all_recv(make, n):
        for k, (dy, dx) in enumerate(DIRECTIONS[:n]):
            pl.when(exists(-dy, -dx))(lambda k=k: make(k).wait_recv())

    def wait_all_send(make, n):
        for k, (dy, dx) in enumerate(DIRECTIONS[:n]):
            pl.when(exists(dy, dx))(lambda k=k: make(k).wait_send())

    start_all(halo_copy, len(DIRECTIONS))

    srow, scol = iota((edge, edge), 0), iota((edge, edge), 1)
    one, none = jnp.float32(1.0), jnp.float32(0.0)
    sides = (
        jnp.where(srow > 0, one, none) + jnp.where(srow < edge - 1, one, none)
        + jnp.where(scol > 0, one, none) + jnp.where(scol < edge - 1, one, none)
    )

    def around(v):
        return (
            jnp.where(srow > 0, shift(v, 1, 0), 0.0)
            + jnp.where(srow < edge - 1, shift(v, -1, 0), 0.0)
            + jnp.where(scol > 0, shift(v, 1, 1), 0.0)
            + jnp.where(scol < edge - 1, shift(v, -1, 1), 0.0)
        )

    rows_in = (iota((cell, edge), 0) == iota((cell, edge), 1) // RATIO).astype(jnp.float32)
    message = jnp.zeros((cell, LANES), jnp.float32)
    row_m = iota((8, LANES), 0)
    params = jnp.full((8, LANES), -1.0, jnp.float32)
    for s in range(slots):
        c, b = die_conduct[s], bond[s]
        live = jnp.where(place[s] >= 0, 1.0, 0.0)
        p = die_power[s]
        d = c * sides + b
        wt = guarded_weight(d)
        v = wt * p
        v = (1.0 - RELAX) * v + wt * (p + c * around(v))
        dies[s] = v
        resid = live * (p + c * around(v) - d * v)
        cols_in = (
            iota((edge, LANES), 0) // RATIO + cell * s == iota((edge, LANES), 1)
        ).astype(jnp.float32)
        message = message + dot(dot(rows_in, resid), cols_in)
        mine = lane8 // cell == s
        value = jnp.where(
            row_m == 0, c, jnp.where(row_m == 1, b * area, place[s].astype(jnp.float32))
        )
        params = jnp.where(mine, value, params)
    die_message[0:cell, :] = message
    die_message[cell : cell + 8, :] = params
    all_dies[me] = die_message[...]

    def gather_copy(phase, other, slot, where):
        src, dst = (die_message, all_dies) if phase == 0 else (die_fix, all_fixes)
        return pltpu.make_async_remote_copy(
            src_ref=src, dst_ref=dst.at[slot],
            send_sem=gather_send.at[phase, other], recv_sem=gather_recv.at[phase, slot],
            device_id=where, device_id_type=MESH,
        )

    def gather_start(phase):
        @pl.loop(1, count)
        def _(offset):
            other, where = peer(offset)
            gather_copy(phase, other, me, where).start()

    def gather_wait(phase):
        @pl.loop(1, count)
        def _(offset):
            other, where = peer(offset)
            gather_copy(phase, other, other, where).wait()

    gather_start(0)

    def gathered(total, first_tile):
        pick = (iota((cols, LANES), 0) // RATIO == iota((cols, LANES), 1)).astype(jnp.float32)
        folded[...] = two_part_dot(sums[...], pick)
        for tile in range(2):
            result = jnp.zeros((crows, LANES), jnp.float32)
            for q in range(per):
                f = tile * per + q
                if f < total:
                    result = result + shift(folded[pl.ds(f, crows, stride=8), :], q * ccols, 1)
            rough[first_tile + tile] = result

    gathered(layers + 1, 0)
    start_all(lambda k: rough_copy(k, 0), N_ROUGH)

    wait_all_recv(halo_copy, len(DIRECTIONS))
    extra = [outer[j].T for j in range(3)]

    def woven(near, far, f, first):
        size = near.shape[1]
        lower = iota((8, size), 0) < HALO
        m = f // 2 * 8
        a = (far if first else near)[m : m + 8]
        b = (near if first else far)[m : m + 8]
        return (
            jnp.where(lower, a, b) if f % 2 == 0 else shift(jnp.where(lower, b, a), HALO, 0)
        )

    for f in range(n_fields):
        for side in range(2):
            at = 64 if side == 0 else 0
            strip[side, f, :, 0:rows] = woven(
                turned[at : at + depth, :], from_side[side], f, side == 0
            )
            strip[side, f, :, rows:long] = woven(
                extra[2][at : at + depth], extra[side][64 - at : 64 - at + depth], f, side == 0
            )

    def strip_total(side, l, us):
        u, fx, fy = us[l], sx[side, l], sy[side, l]
        total = strip[side, layers + l] + fx * shift(u, -1, 1) + shift(fx * u, 1, 1)
        total = total + fy * shift(u, -1, 0) + shift(fy * u, 1, 0)
        if l > 0:
            total = total + sz[side, l - 1] * us[l - 1]
        if l < layers - 1:
            total = total + sz[side, l] * us[l + 1]
        return total

    def strip_sweep(side, us):
        return [
            (1.0 - RELAX) * us[l] + sw[side, l] * strip_total(side, l, us) for l in range(layers)
        ]

    def lay_lines(k, rows_of):
        x = jnp.concatenate(
            rows_of + [jnp.zeros((LANES - 8 * layers, long), jnp.float32)], axis=0
        ).T
        lines[k, TOP : TOP + rows + 8, :] = x[0 : rows + 8]
        lines[k, TOP - 8 : TOP, :] = x[long - 8 : long]

    sub_long = iota((8, long), 0)

    def line_rows(l, fields, has_face):
        parts = []
        if has_face:
            parts = [shift(sy[1, l], -3, 0), shift(sy[0, l], -2, 0)]
        for left, right in fields:
            q = len(parts)
            parts.append(shift(right[l], q - 4, 0))
            parts.append(shift(sy[0, l] * left[l], q - 2, 0))
        x = parts[0]
        for q in range(1, len(parts)):
            x = jnp.where(sub_long == q, parts[q], x)
        return x

    smooth = []
    for side in range(2):
        below = None
        us = []
        for l in range(layers):
            k = strip[side, l]
            fx = inverse(k + shift(k, -1, 1))
            fy = inverse(k + shift(k, -1, 0))
            sx[side, l] = fx
            sy[side, l] = fy
            d = fx + shift(fx, 1, 1) + fy + shift(fy, 1, 0)
            d = d + (strip[side, 2 * layers] if l == 0 else below)
            if l < layers - 1:
                below = inverse(k + strip[side, l + 1])
                sz[side, l] = below
                d = d + below
            wt = guarded_weight(d)
            sw[side, l] = wt
            us.append(wt * strip[side, layers + l])
        new = strip_sweep(side, us)
        for l in range(layers):
            su[side, l] = new[l]
        smooth.append((us, new))
    fields = list(zip(*smooth))
    lay_lines(0, [line_rows(l, fields, True) for l in range(layers)])

    first8, last8 = lane8 == 0, lane8 == LANES - 1

    def from_right(xs, p, end):
        turn = shift(xs[p], -1, 1)
        if p < panes - 1:
            return jnp.where(last8, shift(xs[p + 1], -1, 1), turn)
        return turn if end is None else jnp.where(last8, end, turn)

    def from_left(xs, p, end):
        return jnp.where(first8, end if p == 0 else shift(xs[p - 1], 1, 1), shift(xs[p], 1, 1))

    def line_ends(line, l, q):
        return shift(line, -(8 * l + 2 * q + 1), 1)

    @pl.loop(1, height // 8 - 1, unroll=UNROLL)
    def _(i):
        r = pl.multiple_of(i * 8, 8)
        here = pl.ds(r, 8)
        line = lines[0, here, :]
        ks = [[field[l, p, here, :] for p in range(panes)] for l in range(layers)]
        fxs = []
        for l in range(layers):
            fxs.append([])
            for p in range(panes):
                fx = inverse(ks[l][p] + field[l, p, pl.ds(r + 1, 8), :])
                zx[l, p, here, :] = fx
                fxs[l].append(fx)
        below = [None] * panes
        for l in range(layers):
            k = ks[l]
            ends = line_ends(line, l, 0)
            fys = [inverse(k[p] + from_right(k, p, None)) for p in range(panes)]
            fys[-1] = jnp.where(last8, ends, fys[-1])
            for p in range(panes):
                fy = fys[p]
                zy[l, p, here, :] = fy
                d = fxs[l][p] + zx[l, p, pl.ds(r - 1, 8), :] + fy + from_left(fys, p, ends)
                d = d + (field[2 * layers, p, here, :] if l == 0 else below[p])
                if l < layers - 1:
                    below[p] = inverse(k[p] + ks[l + 1][p])
                    zz[l, p, here, :] = below[p]
                    d = d + below[p]
                diag[l, p, here, :] = d
                wt = guarded_weight(d)
                weight[l, p, here, :] = wt
                ua[l, p, here, :] = wt * field[layers + l, p, here, :]

    def pulled(u, r, l, us, line, q):
        here = pl.ds(r, 8)
        fys = [zy[l, p, here, :] for p in range(panes)]
        flows = [fys[p] * us[l][p] for p in range(panes)]
        ends = line_ends(line, l, q)
        totals = []
        for p in range(panes):
            total = field[layers + l, p, here, :]
            total = total + zx[l, p, here, :] * u[l, p, pl.ds(r + 1, 8), :]
            total = total + zx[l, p, pl.ds(r - 1, 8), :] * u[l, p, pl.ds(r - 1, 8), :]
            total = total + fys[p] * from_right(us[l], p, ends) + from_left(flows, p, ends)
            if l > 0:
                total = total + zz[l - 1, p, here, :] * us[l - 1][p]
            if l < layers - 1:
                total = total + zz[l, p, here, :] * us[l + 1][p]
            totals.append(total)
        return totals

    def layers_at(u, r):
        return [[u[l, p, pl.ds(r, 8), :] for p in range(panes)] for l in range(layers)]

    def sweep(u, store, first, last, k, q):
        @pl.loop(first, last, unroll=UNROLL)
        def _(i):
            r = pl.multiple_of(i * 8, 8)
            us = layers_at(u, r)
            line = lines[k, pl.ds(r, 8), :]
            for l in range(layers):
                totals = pulled(u, r, l, us, line, q)
                for p in range(panes):
                    store(
                        l, p, r,
                        (1.0 - RELAX) * us[l][p] + weight[l, p, pl.ds(r, 8), :] * totals[p],
                    )

    def into(ref):
        def store(l, p, r, new):
            ref[l, p, pl.ds(r, 8), :] = new

        return store

    sweep(ua, into(ub), 1, height // 8 - 1, 0, 1)

    @pl.loop(0, crows, unroll=UNROLL)
    def _(i):
        r = pl.multiple_of(i * 8 + TOP, 8)
        us = layers_at(ub, r)
        line = lines[0, pl.ds(r, 8), :]
        resids = [[] for _ in range(panes)]
        for l in range(layers):
            totals = pulled(ub, r, l, us, line, 2)
            for p in range(panes):
                resids[p].append(totals[p] - diag[l, p, pl.ds(r, 8), :] * us[l][p])
        for p in range(panes):
            sums[pl.ds(pl.multiple_of(i * 8, 8), 8), p * LANES : (p + 1) * LANES] = row_sums(
                resids[p]
            )

    gathered(layers, 2)
    start_all(lambda k: rough_copy(k, 1), N_ROUGH)

    gather_wait(0)
    span = tile_count * across
    chigh = crows + 16
    parts = cell + 8
    spots = [(a, b) for a in range(-1, down + 1) for b in range(-1, across + 1)]
    wanted = []
    for a, b in spots:
        pr, pc = g * down + a, t * across + b
        inside = (pr >= 0) & (pr < grp_count * down) & (pc >= 0) & (pc < span)
        wanted.append(jnp.where(inside, pr * span + pc, -2).astype(jnp.float32))

    for lo in range(0, len(spots), across + 2):

        def add(d, acc, lo=lo):
            block = all_dies[d]
            where = block[cell + 2 : cell + 3, :]
            return tuple(
                a + jnp.where(where == wanted[lo + j], block, 0.0) for j, a in enumerate(acc)
            )

        acc = lax.fori_loop(
            0, count, add, tuple(jnp.zeros((parts, LANES), jnp.float32) for _ in range(across + 2))
        )
        lane_p = iota((parts, LANES), 1)
        line = jnp.zeros((parts, LANES), jnp.float32)
        for j in range(across + 2):
            x = acc[j]
            step = LANES // 2
            while step >= cell:
                x = x + shift(x, step, 1)
                step //= 2
            line = jnp.where(lane_p // cell == j, x, line)
        line = shift(line, 8 - cell, 1)
        a = lo // (across + 2) - 1
        if a == -1:
            first, size, off = 0, 8, cell - 8
        elif a == down:
            first, size, off = 8 + crows, 8, 0
        else:
            first, size, off = 8 + a * cell, cell, 0
        n = 2 * layers + 1
        wide[n, first : first + size, :] = line[off : off + size]
        wide[n + 1, first : first + size, :] = jnp.broadcast_to(
            line[cell : cell + 1], (size, LANES)
        )
        wide[n + 2, first : first + size, :] = jnp.broadcast_to(
            line[cell + 1 : cell + 2], (size, LANES)
        )

    for phase in range(2):
        wait_all_recv(lambda k: rough_copy(k, phase), N_ROUGH)
        for f in range(layers + 1 if phase == 0 else layers):
            tile, q = 2 * phase + f // per, f % per
            target = f if phase == 0 else layers + 1 + f

            def joined(left, middle, right, size):
                lane = iota((size, LANES), 1)
                x = shift(middle, 8 - ccols * q, 1)
                x = jnp.where((lane >= 8) & (lane < 8 + ccols), x, 0.0)
                x = jnp.where(lane < 8, shift(left, 8 - ccols - ccols * q, 1), x)
                return jnp.where(
                    (lane >= 8 + ccols) & (lane < 16 + ccols),
                    shift(right, 8 + ccols - ccols * q, 1),
                    x,
                )

            wide[target, 8 : 8 + crows, :] = joined(
                rough_side[1, tile], rough[tile], rough_side[0, tile], crows
            )
            wide[target, 0:8, :] = joined(
                rough_corner[3, tile], rough_row[1, tile], rough_corner[2, tile], 8
            )
            wide[target, 8 + crows : chigh, :] = joined(
                rough_corner[1, tile], rough_row[0, tile], rough_corner[0, tile], 8
            )

    kc = [wide[l] * (0.5 / area) for l in range(layers)]
    cx = [harmonic(k, shift(k, -1, 0)) for k in kc]
    cy = [harmonic(k, shift(k, -1, 1)) for k in kc]
    cz = [harmonic(kc[l], kc[l + 1]) * area for l in range(layers - 1)]
    top_rhs, top_c, top_b = (wide[2 * layers + 1 + j] for j in range(3))
    weights = []
    for l in range(layers):
        d = cx[l] + shift(cx[l], 1, 0) + cy[l] + shift(cy[l], 1, 1)
        if l == 0:
            d = d + wide[layers]
        else:
            d = d + cz[l - 1]
        d = d + (cz[l] if l < layers - 1 else top_b)
        weights.append(guarded_weight(d))
    crow = (iota((chigh, LANES), 0) + (cell - 8)) % cell
    ccol = (iota((chigh, LANES), 1) + (cell - 8)) % cell
    low_x, high_x = crow != 0, crow != cell - 1
    low_y, high_y = ccol != 0, ccol != cell - 1
    near = sum(jnp.where(m, one, none) for m in (low_x, high_x, low_y, high_y))
    top_d = top_c * near + top_b
    top_w = guarded_weight(top_d)
    errors = [weights[l] * wide[layers + 1 + l] for l in range(layers)]
    top = top_w * top_rhs
    for _ in range(NC - 1):
        new = []
        for l in range(layers):
            e = errors[l]
            total = wide[layers + 1 + l]
            total = total + cx[l] * shift(e, -1, 0) + shift(cx[l] * e, 1, 0)
            total = total + cy[l] * shift(e, -1, 1) + shift(cy[l] * e, 1, 1)
            if l > 0:
                total = total + cz[l - 1] * errors[l - 1]
            total = total + (cz[l] * errors[l + 1] if l < layers - 1 else top_b * top)
            new.append((1.0 - RELAX) * e + weights[l] * total)
        nearby = (
            jnp.where(low_x, shift(top, 1, 0), 0.0)
            + jnp.where(high_x, shift(top, -1, 0), 0.0)
            + jnp.where(low_y, shift(top, 1, 1), 0.0)
            + jnp.where(high_y, shift(top, -1, 1), 0.0)
        )
        top = top + top_w * (
            top_rhs + top_b * errors[layers - 1] + top_c * nearby - top_d * top
        )
        errors = new
    lane_c = iota((cell, LANES), 1)
    fix = jnp.zeros((cell, LANES), jnp.float32)
    for a in range(down):
        piece = shift(top[8 + a * cell : 8 + (a + 1) * cell], a * ccols - 8, 1)
        fix = jnp.where(lane_c // ccols == a, piece, fix)
    die_fix[...] = fix
    all_fixes[me] = die_fix[...]
    gather_start(1)

    pick = (iota((LANES, cols), 0) == 8 + iota((LANES, cols), 1) // RATIO).astype(jnp.float32)
    fine = two_part_dot(jnp.concatenate(errors, axis=0), pick)
    for l in range(layers):
        for p in range(panes):
            spread[l, p] = fine[l * chigh : (l + 1) * chigh, p * LANES : (p + 1) * LANES]
    lane_s = iota((LANES, LANES), 1)
    wanted_lane = jnp.where(lane_s % 8 < HALO, 7, 8) + jnp.where(lane_s % 16 < 8, 0, ccols)
    wanted_lane = jnp.where(
        iota((LANES, LANES), 0) == wanted_lane, lane_s // 16, -1
    )
    sides_of = jnp.zeros((chigh, LANES), jnp.float32)
    for l in range(layers):
        sides_of = sides_of + two_part_dot(errors[l], (wanted_lane == l).astype(jnp.float32))
    along = iota((chigh, long), 1)
    coarse_row = jnp.where(along < rows + 64, along // RATIO + 8, 7)
    side_fix = two_part_dot(
        sides_of.T, (iota((chigh, long), 0) == coarse_row).astype(jnp.float32)
    )
    smooth = []
    for side in range(2):
        us = []
        for l in range(layers):
            at = 16 * l + 8 * side
            us.append(su[side, l] + side_fix[at : at + 8])
        smooth.append((us, strip_sweep(side, us)))
    fields = list(zip(*smooth))
    lay_lines(1, [line_rows(l, fields, False) for l in range(layers)])

    @pl.loop(1, height // 8 - 1)
    def _(i):
        r = pl.multiple_of(i * 8, 8)
        for l in range(layers):
            for p in range(panes):
                ub[l, p, pl.ds(r, 8), :] = ub[l, p, pl.ds(r, 8), :] + spread[l, p, pl.ds(i + 6, 1), :]

    sweep(ub, into(ua), 1, height // 8 - 1, 1, 0)

    def finish(l, p, r, new):
        out[l, pl.ds(r - TOP, 8), p * LANES : (p + 1) * LANES] = new

    sweep(ua, finish, TOP // 8, (height - TOP) // 8, 1, 1)

    gather_wait(1)
    codes = []
    for s in range(slots):
        spot = jnp.maximum(place[s], 0)
        pr, pc = spot // span, lax.rem(spot, span)
        target = (pr // down) * tile_count + pc // across
        local = lax.rem(pr, down) * across + lax.rem(pc, across)
        codes.append(jnp.where(place[s] >= 0, target * 8 + local, -1))
    group = lane_c // cell

    def collect(d, acc):
        block = all_fixes[d]
        code = group + d * 8
        return tuple(a + jnp.where(code == codes[s], block, 0.0) for s, a in enumerate(acc))

    fixes = lax.fori_loop(
        0, count, collect, tuple(jnp.zeros((cell, LANES), jnp.float32) for _ in range(slots))
    )
    rows_out = (iota((edge, cell), 0) // RATIO == iota((edge, cell), 1)).astype(jnp.float32)
    cols_out = (iota((LANES, edge), 0) == iota((LANES, edge), 1) // RATIO).astype(jnp.float32)
    for s in range(slots):
        x = fixes[s]
        step = LANES // 2
        while step >= cell:
            x = x + shift(x, step, 1)
            step //= 2
        c, b = die_conduct[s], bond[s]
        live = jnp.where(place[s] >= 0, 1.0, 0.0)
        p = die_power[s]
        wt = guarded_weight(c * sides + b)
        v = dies[s] + live * dot(rows_out, dot(x, cols_out))
        for _ in range(NU):
            v = (1.0 - RELAX) * v + wt * (p + c * around(v))
        die_out[s] = live * v

    wait_all_send(halo_copy, len(DIRECTIONS))
    for phase in range(2):
        wait_all_send(lambda k: rough_copy(k, phase), N_ROUGH)


def per_device(grp_count, tile_count, *args):
    material, die_power = args[0], args[4]
    layers, rows, cols = material.shape
    slots, edge, _ = die_power.shape
    cell = edge // RATIO
    crows = rows // RATIO
    panes, long, height = cols // LANES, rows + LANES, rows + 2 * TOP
    count = grp_count * tile_count
    n_fields = 2 * layers + 1
    depth = -(-n_fields * HALO // 8) * 8
    vmem = pl.BlockSpec(memory_space=pltpu.VMEM)
    smem = pl.BlockSpec(memory_space=pltpu.SMEM)
    f32 = jnp.float32

    def scratch(*shape):
        return pltpu.VMEM(shape, f32)

    grid = (layers, panes, height, LANES)
    return pl.pallas_call(
        functools.partial(kernel, grp_count, tile_count),
        out_shape=(
            jax.ShapeDtypeStruct((layers, rows, cols), f32),
            jax.ShapeDtypeStruct((slots, edge, edge), f32),
        ),
        in_specs=[vmem, smem, vmem, vmem, vmem, smem, smem, smem],
        out_specs=(vmem, vmem),
        scratch_shapes=[
            scratch(n_fields, panes, height, LANES),
            scratch(*grid),
            scratch(*grid),
            scratch(layers - 1, panes, height, LANES),
            scratch(*grid),
            scratch(*grid),
            scratch(*grid),
            scratch(*grid),
            scratch(rows, LANES),
            scratch(LANES, rows),
            scratch(2, depth, rows),
            scratch(3, LANES, LANES),
            scratch(2, n_fields, 8, long),
            scratch(2, layers, 8, long),
            scratch(2, layers, 8, long),
            scratch(2, layers - 1, 8, long),
            scratch(2, layers, 8, long),
            scratch(2, layers, 8, long),
            scratch(2, height, LANES),
            scratch(rows, cols),
            scratch(rows, LANES),
            scratch(4, crows, LANES),
            scratch(2, 4, crows, LANES),
            scratch(2, 4, 8, LANES),
            scratch(4, 4, 8, LANES),
            scratch(slots, edge, edge),
            scratch(cell + 8, LANES),
            scratch(count, cell + 8, LANES),
            scratch(cell, LANES),
            scratch(count, cell, LANES),
            scratch(n_fields + 3, crows + 16, LANES),
            scratch(layers, panes, crows + 16, LANES),
            pltpu.SemaphoreType.DMA((len(DIRECTIONS) + 2 * N_ROUGH,)),
            pltpu.SemaphoreType.DMA((len(DIRECTIONS) + 2 * N_ROUGH,)),
            pltpu.SemaphoreType.DMA((2, count)),
            pltpu.SemaphoreType.DMA((2, count)),
        ],
        compiler_params=pltpu.CompilerParams(
            collective_id=0, has_side_effects=True, vmem_limit_bytes=60 * 1024 * 1024
        ),
    )(*args)


def solution(mesh):
    placed = (
        P(None, "grp", "tile"),
        P(),
        P("grp", "tile"),
        P(None, "grp", "tile"),
        P(("grp", "tile"), None, None),
        P(("grp", "tile")),
        P(("grp", "tile")),
        P(("grp", "tile")),
    )
    return jax.shard_map(
        functools.partial(per_device, mesh.shape["grp"], mesh.shape["tile"]),
        mesh=mesh,
        in_specs=placed,
        out_specs=(P(None, "grp", "tile"), P(("grp", "tile"), None, None)),
        check_vma=False,
    )
```

```python
import functools
import jax
import jax.numpy as jnp
from jax import lax
from jax.experimental import pallas as pl
from jax.experimental.pallas import tpu as pltpu
from jax.sharding import PartitionSpec as P

RATIO = 8
NU = 2
NC = 4
RELAX = 0.8
HALO = 4
TOP = 16
LANES = 128
FAR = 1e30
TINY = 1e-25
UNROLL = 5
MESH = pl.DeviceIdType.MESH
DIRECTIONS = ((-1, 0), (1, 0), (0, -1), (0, 1), (-1, -1), (-1, 1), (1, -1), (1, 1), (-1, 0), (1, 0))
N_ROUGH = 8


def inverse(x):
    return pltpu.reciprocal(x, approx=True)


def harmonic(a, b):
    total = a + b
    return 2.0 * a * b * inverse(jnp.where(total > 0, total, 1.0))


def guarded_weight(d):
    return RELAX * inverse(jnp.where(d > TINY, d, 1.0))


def unroll_of(n, most=UNROLL):
    return max(u for u in range(1, most + 1) if n % u == 0)


def iota(shape, dim):
    return lax.broadcasted_iota(jnp.int32, shape, dim)


def shift(x, amount, axis):
    return pltpu.roll(x, amount % x.shape[axis], axis)


def row_sums(fields):
    shape = fields[0].shape
    row = lax.broadcasted_iota(jnp.int32, shape, 0)
    xs = list(fields) + [jnp.zeros(shape, jnp.float32)] * (8 - len(fields))

    def merge(x, y, start, run):
        first = ((row - start + 8) % 8) % (2 * run) < run
        return jnp.where(first, x, y) + shift(jnp.where(first, y, x), -run, 0)

    z = [merge(xs[j], xs[j + 4], j, 4) for j in range(4)]
    y = [merge(z[j], z[j + 2], j, 2) for j in range(2)]
    return merge(y[0], y[1], 0, 1)


def halves(a):
    high = a.astype(jnp.bfloat16)
    return high, (a - high.astype(jnp.float32)).astype(jnp.bfloat16)


def two_part_dot(a, b):
    b = b.astype(jnp.bfloat16)
    return jnp.dot(
        jnp.concatenate(halves(a), axis=1),
        jnp.concatenate([b, b], axis=0),
        preferred_element_type=jnp.float32,
    )


def kernel(
    grp_count,
    tile_count,
    material,
    table,
    heat_sink,
    source,
    die_power,
    die_conduct,
    bond,
    place,
    out,
    die_out,
    field,
    zx,
    zy,
    zz,
    diag,
    weight,
    ua,
    ub,
    packed,
    turned,
    from_side,
    outer,
    strip,
    sx,
    sy,
    sz,
    sw,
    su,
    lines,
    sums,
    folded,
    rough,
    rough_side,
    rough_row,
    rough_corner,
    dies,
    fixed,
    all_dies,
    all_fixes,
    wide,
    spread,
    send_sem,
    recv_sem,
    gather_send,
    gather_recv,
):
    layers, rows, cols = material.shape
    slots, edge, _ = die_power.shape
    cell = edge // RATIO
    down, across = rows // edge, cols // edge
    crows, ccols = rows // RATIO, cols // RATIO
    panes = cols // LANES
    long = rows + LANES
    height = rows + 2 * TOP
    n_fields = 2 * layers + 1
    area = float(RATIO * RATIO)
    per = LANES // ccols
    count = grp_count * tile_count
    g = lax.axis_index("grp")
    t = lax.axis_index("tile")
    me = g * tile_count + t

    def each_peer(act):
        for dg in range(grp_count):
            for dt in range(tile_count):
                if dg or dt:
                    act((lax.rem(g + dg, grp_count), lax.rem(t + dt, tile_count)))

    def exists(dy, dx):
        ok = jnp.bool_(True)
        if dy:
            ok = jnp.logical_and(ok, g > 0 if dy < 0 else g < grp_count - 1)
        if dx:
            ok = jnp.logical_and(ok, t > 0 if dx < 0 else t < tile_count - 1)
        return ok

    for top in (0, height - TOP):
        field[0:layers, :, top : top + TOP, :] = jnp.full((layers, panes, TOP, LANES), FAR, jnp.float32)
        field[layers:n_fields, :, top : top + TOP, :] = jnp.zeros(
            (n_fields - layers, panes, TOP, LANES), jnp.float32
        )
    cut = HALO * layers
    from_side[:, 0:cut, :] = jnp.full((2, cut, rows), FAR, jnp.float32)
    from_side[:, cut:, :] = jnp.zeros((2, from_side.shape[1] - cut, rows), jnp.float32)
    outer[...] = jnp.where(iota(outer.shape, 2) % 64 < cut, FAR, 0.0)
    for n in range(2):
        for at in (0, edge + 8):
            dies[n, :, pl.ds(at, 8), :] = jnp.zeros((slots, 8, edge), jnp.float32)
    rough_side[...] = jnp.zeros_like(rough_side)
    rough_row[...] = jnp.zeros_like(rough_row)
    rough_corner[...] = jnp.zeros_like(rough_corner)
    zx[:, :, 0:8, :] = jnp.zeros((layers, panes, 8, LANES), jnp.float32)

    barrier = pltpu.get_barrier_semaphore()

    each_peer(
        lambda where: pl.semaphore_signal(barrier, inc=1, device_id=where, device_id_type=MESH)
    )

    lane8 = iota((8, LANES), 1)
    sub8 = iota((8, LANES), 0)

    def right_lane(f):
        return HALO * f

    def left_lane(f):
        return 64 + 8 * (f // 2) + HALO * (1 - f % 2)

    doubled = [jnp.full((8, LANES), 2.0 * table[m], jnp.float32) for m in range(table.shape[0])]

    @pl.loop(0, rows // 8, unroll=unroll_of(rows // 8, 4))
    def _(i):
        r = pl.multiple_of(i * 8, 8)
        edges = jnp.zeros((8, LANES), jnp.float32)
        summed = [[] for _ in range(panes)]
        for f in range(n_fields):
            xs = []
            for p in range(panes):
                part = slice(p * LANES, (p + 1) * LANES)
                if f < layers:
                    kind = material[f, pl.ds(r, 8), part]
                    values = list(doubled)
                    bit = 1
                    while len(values) > 1:
                        odd = (kind & bit) != 0
                        values = [
                            jnp.where(odd, values[m + 1], values[m]) if m + 1 < len(values) else values[m]
                            for m in range(0, len(values), 2)
                        ]
                        bit *= 2
                    summed[p].append(values[0])
                    x = inverse(values[0])
                elif f < 2 * layers:
                    x = source[f - layers, pl.ds(r, 8), part]
                else:
                    x = heat_sink[pl.ds(r, 8), part]
                    summed[p].append(x)
                field[f, p, pl.ds(TOP + r, 8), :] = x
                xs.append(x)
            a, b = right_lane(f), left_lane(f)
            right = shift(xs[-1], HALO + a, 1)
            left = shift(xs[0], b, 1)
            edges = jnp.where((lane8 >= a) & (lane8 < a + HALO), right, edges)
            edges = jnp.where((lane8 >= b) & (lane8 < b + HALO), left, edges)
        packed[pl.ds(r, 8), :] = edges
        for p in range(panes):
            sums[pl.ds(r, 8), p * LANES : (p + 1) * LANES] = row_sums(summed[p])

    turned[...] = packed[...].T

    pl.semaphore_wait(barrier, count - 1)

    depth = from_side.shape[1]

    def halo_copy(k):
        dy, dx = DIRECTIONS[k]
        if k < 2:
            src = field.at[:, :, pl.ds(TOP if dy < 0 else height - TOP - 8, 8), :]
            dst = field.at[:, :, pl.ds(height - TOP if dy < 0 else TOP - 8, 8), :]
        elif dy == 0:
            src = turned.at[pl.ds(0 if dx > 0 else 64, depth), :]
            dst = from_side.at[0 if dx > 0 else 1]
        else:
            src = packed.at[pl.ds(0 if dy < 0 else rows - 8, 8), :]
            which = 2 if dx == 0 else (0 if dx > 0 else 1)
            dst = outer.at[which, pl.ds(0 if dy < 0 else LANES - 8, 8), :]
        return pltpu.make_async_remote_copy(
            src_ref=src, dst_ref=dst, send_sem=send_sem.at[k], recv_sem=recv_sem.at[k],
            device_id=(g + dy, t + dx), device_id_type=MESH,
        )

    def rough_copy(k, phase):
        dy, dx = DIRECTIONS[k]
        half = pl.ds(2 * phase, 2)
        if dy == 0:
            src = rough.at[half]
            dst = rough_side.at[k - 2, half]
        else:
            src = rough.at[half, pl.ds(0 if dy < 0 else crows - 8, 8), :]
            dst = (rough_row.at[k, half] if dx == 0 else rough_corner.at[k - 4, half])
        s = len(DIRECTIONS) + N_ROUGH * phase + k
        return pltpu.make_async_remote_copy(
            src_ref=src, dst_ref=dst, send_sem=send_sem.at[s], recv_sem=recv_sem.at[s],
            device_id=(g + dy, t + dx), device_id_type=MESH,
        )

    def start_all(make, n):
        for k, (dy, dx) in enumerate(DIRECTIONS[:n]):
            pl.when(exists(dy, dx))(lambda k=k: make(k).start())

    def wait_all_recv(make, n):
        for k, (dy, dx) in enumerate(DIRECTIONS[:n]):
            pl.when(exists(-dy, -dx))(lambda k=k: make(k).wait_recv())

    def wait_all_send(make, n):
        for k, (dy, dx) in enumerate(DIRECTIONS[:n]):
            pl.when(exists(dy, dx))(lambda k=k: make(k).wait_send())

    start_all(halo_copy, len(DIRECTIONS))

    col_d = iota((8, LANES), 1)
    one, none = jnp.float32(1.0), jnp.float32(0.0)
    inner = jnp.where(col_d > 0, one, none) + jnp.where(col_d < edge - 1, one, none) + 1.0
    first_row = jnp.where(sub8 > 0, one, none)
    last_row = jnp.where(sub8 < 7, one, none)
    beside = (
        jnp.abs(iota((edge, edge), 0) - iota((edge, edge), 1)) == 1
    ).astype(jnp.float32)
    body = pl.ds(8, edge)
    tall = edge // 8

    def die_diagonal(c, b):
        tops = [c * (inner + first_row) + b, c * (inner + 1.0) + b, c * (inner + last_row) + b]
        ws = [guarded_weight(d) for d in tops]

        def full(x):
            return jnp.concatenate([x[0]] + [x[1]] * (tall - 2) + [x[2]], axis=0)

        return full(tops), full(ws)

    def around(n, s):
        v = dies[n, s, body, :]
        return (
            dies[n, s, pl.ds(7, edge), :] + dies[n, s, pl.ds(9, edge), :] + two_part_dot(v, beside)
        )

    rows_in = (iota((cell, edge), 0) == iota((cell, edge), 1) // RATIO).astype(jnp.bfloat16)
    rows_in = jnp.concatenate([rows_in, rows_in], axis=1)
    message = jnp.zeros((cell, LANES), jnp.float32)
    params = jnp.full((8, LANES), -1.0, jnp.float32)
    for s in range(slots):
        c, b = die_conduct[s], bond[s]
        live = jnp.where(place[s] >= 0, 1.0, 0.0)
        p = die_power[s]
        d, wt = die_diagonal(c, b)
        dies[0, s, body, :] = wt * p
        dies[1, s, body, :] = (1.0 - RELAX) * dies[0, s, body, :] + wt * (p + c * around(0, s))
        resid = p + c * around(1, s) - d * dies[1, s, body, :]
        cols_in = (
            iota((edge, LANES), 0) // RATIO + cell * s == iota((edge, LANES), 1)
        ).astype(jnp.float32)
        by_row = jnp.dot(
            rows_in, jnp.concatenate(halves(resid), axis=0), preferred_element_type=jnp.float32
        )
        message = message + live * two_part_dot(by_row, cols_in)
        mine = lane8 // cell == s
        value = jnp.where(
            sub8 == 0, c, jnp.where(sub8 == 1, b * area, place[s].astype(jnp.float32))
        )
        params = jnp.where(mine, value, params)
    all_dies[me, 0:cell, :] = message
    all_dies[me, cell : cell + 8, :] = params

    def gather_start(phase):
        every = (all_dies, all_fixes)[phase]
        each_peer(
            lambda where: pltpu.make_async_remote_copy(
                src_ref=every.at[me], dst_ref=every.at[me],
                send_sem=gather_send.at[phase], recv_sem=gather_recv.at[phase],
                device_id=where, device_id_type=MESH,
            ).start()
        )

    def gather_wait(phase):
        others = (all_dies, all_fixes)[phase].at[pl.ds(0, count - 1)]
        for sem in (gather_send, gather_recv):
            pltpu.make_async_copy(others, others, sem.at[phase]).wait()

    gather_start(0)

    def gathered(total, first_tile):
        pick = (iota((cols, LANES), 0) // RATIO == iota((cols, LANES), 1)).astype(jnp.float32)
        folded[...] = two_part_dot(sums[...], pick)
        for tile in range(2):
            result = jnp.zeros((crows, LANES), jnp.float32)
            for q in range(per):
                f = tile * per + q
                if f < total:
                    result = result + shift(folded[pl.ds(f, crows, stride=8), :], q * ccols, 1)
            rough[first_tile + tile] = result

    gathered(layers + 1, 0)
    start_all(lambda k: rough_copy(k, 0), N_ROUGH)

    wait_all_recv(halo_copy, len(DIRECTIONS))
    extra = [outer[j].T for j in range(3)]

    def woven(near, far, f, first):
        size = near.shape[1]
        lower = iota((8, size), 0) < HALO
        m = f // 2 * 8
        a = (far if first else near)[m : m + 8]
        b = (near if first else far)[m : m + 8]
        return (
            jnp.where(lower, a, b) if f % 2 == 0 else shift(jnp.where(lower, b, a), HALO, 0)
        )

    for f in range(n_fields):
        for side in range(2):
            at = 64 if side == 0 else 0
            strip[side, f, :, 0:rows] = woven(
                turned[at : at + depth, :], from_side[side], f, side == 0
            )
            strip[side, f, :, rows:long] = woven(
                extra[2][at : at + depth], extra[side][64 - at : 64 - at + depth], f, side == 0
            )

    def strip_total(side, l, us):
        u, fx, fy = us[l], sx[side, l], sy[side, l]
        total = strip[side, layers + l] + fx * shift(u, -1, 1) + shift(fx * u, 1, 1)
        total = total + fy * shift(u, -1, 0) + shift(fy * u, 1, 0)
        if l > 0:
            total = total + sz[side, l - 1] * us[l - 1]
        if l < layers - 1:
            total = total + sz[side, l] * us[l + 1]
        return total

    def strip_sweep(side, us):
        return [
            (1.0 - RELAX) * us[l] + sw[side, l] * strip_total(side, l, us) for l in range(layers)
        ]

    def lay_lines(k, rows_of):
        x = jnp.concatenate(
            rows_of + [jnp.zeros((LANES - 8 * layers, long), jnp.float32)], axis=0
        ).T
        lines[k, TOP : TOP + rows + 8, :] = x[0 : rows + 8]
        lines[k, TOP - 8 : TOP, :] = x[long - 8 : long]

    sub_long = iota((8, long), 0)

    def line_rows(l, fields, has_face):
        parts = []
        if has_face:
            parts = [shift(sy[1, l], -3, 0), shift(sy[0, l], -2, 0)]
        for left, right in fields:
            q = len(parts)
            parts.append(shift(right[l], q - 4, 0))
            parts.append(shift(sy[0, l] * left[l], q - 2, 0))
        x = parts[0]
        for q in range(1, len(parts)):
            x = jnp.where(sub_long == q, parts[q], x)
        return x

    smooth = []
    for side in range(2):
        below = None
        us = []
        for l in range(layers):
            k = strip[side, l]
            fx = inverse(k + shift(k, -1, 1))
            fy = inverse(k + shift(k, -1, 0))
            sx[side, l] = fx
            sy[side, l] = fy
            d = fx + shift(fx, 1, 1) + fy + shift(fy, 1, 0)
            d = d + (strip[side, 2 * layers] if l == 0 else below)
            if l < layers - 1:
                below = inverse(k + strip[side, l + 1])
                sz[side, l] = below
                d = d + below
            wt = guarded_weight(d)
            sw[side, l] = wt
            us.append(wt * strip[side, layers + l])
        new = strip_sweep(side, us)
        for l in range(layers):
            su[side, l] = new[l]
        smooth.append((us, new))
    fields = list(zip(*smooth))
    lay_lines(0, [line_rows(l, fields, True) for l in range(layers)])

    first8, last8 = lane8 == 0, lane8 == LANES - 1

    def from_right(xs, p, end):
        turn = shift(xs[p], -1, 1)
        if p < panes - 1:
            return jnp.where(last8, shift(xs[p + 1], -1, 1), turn)
        return turn if end is None else jnp.where(last8, end, turn)

    def from_left(xs, p, end):
        return jnp.where(first8, end if p == 0 else shift(xs[p - 1], 1, 1), shift(xs[p], 1, 1))

    def line_ends(line, l, q):
        return shift(line, -(8 * l + 2 * q + 1), 1)

    @pl.loop(1, height // 8 - 1, unroll=unroll_of(height // 8 - 2))
    def _(i):
        r = pl.multiple_of(i * 8, 8)
        here = pl.ds(r, 8)
        line = lines[0, here, :]
        ks = [[field[l, p, here, :] for p in range(panes)] for l in range(layers)]
        fxs = []
        for l in range(layers):
            fxs.append([])
            for p in range(panes):
                fx = inverse(ks[l][p] + field[l, p, pl.ds(r + 1, 8), :])
                zx[l, p, here, :] = fx
                fxs[l].append(fx)
        below = [None] * panes
        for l in range(layers):
            k = ks[l]
            ends = line_ends(line, l, 0)
            fys = [inverse(k[p] + from_right(k, p, None)) for p in range(panes)]
            fys[-1] = jnp.where(last8, ends, fys[-1])
            for p in range(panes):
                fy = fys[p]
                zy[l, p, here, :] = fy
                d = fxs[l][p] + zx[l, p, pl.ds(r - 1, 8), :] + fy + from_left(fys, p, ends)
                d = d + (field[2 * layers, p, here, :] if l == 0 else below[p])
                if l < layers - 1:
                    below[p] = inverse(k[p] + ks[l + 1][p])
                    zz[l, p, here, :] = below[p]
                    d = d + below[p]
                diag[l, p, here, :] = d
                wt = guarded_weight(d)
                weight[l, p, here, :] = wt
                ua[l, p, here, :] = wt * field[layers + l, p, here, :]

    def pulled(u, r, l, us, line, q):
        here = pl.ds(r, 8)
        fys = [zy[l, p, here, :] for p in range(panes)]
        flows = [fys[p] * us[l][p] for p in range(panes)]
        ends = line_ends(line, l, q)
        totals = []
        for p in range(panes):
            total = field[layers + l, p, here, :]
            total = total + zx[l, p, here, :] * u[l, p, pl.ds(r + 1, 8), :]
            total = total + zx[l, p, pl.ds(r - 1, 8), :] * u[l, p, pl.ds(r - 1, 8), :]
            total = total + fys[p] * from_right(us[l], p, ends) + from_left(flows, p, ends)
            if l > 0:
                total = total + zz[l - 1, p, here, :] * us[l - 1][p]
            if l < layers - 1:
                total = total + zz[l, p, here, :] * us[l + 1][p]
            totals.append(total)
        return totals

    def layers_at(u, r):
        return [[u[l, p, pl.ds(r, 8), :] for p in range(panes)] for l in range(layers)]

    def sweep(u, store, first, last, k, q):
        @pl.loop(first, last, unroll=unroll_of(last - first))
        def _(i):
            r = pl.multiple_of(i * 8, 8)
            us = layers_at(u, r)
            line = lines[k, pl.ds(r, 8), :]
            for l in range(layers):
                totals = pulled(u, r, l, us, line, q)
                for p in range(panes):
                    store(
                        l, p, r,
                        (1.0 - RELAX) * us[l][p] + weight[l, p, pl.ds(r, 8), :] * totals[p],
                    )

    def into(ref):
        def store(l, p, r, new):
            ref[l, p, pl.ds(r, 8), :] = new

        return store

    sweep(ua, into(ub), 1, height // 8 - 1, 0, 1)

    @pl.loop(0, crows, unroll=unroll_of(crows))
    def _(i):
        r = pl.multiple_of(i * 8 + TOP, 8)
        us = layers_at(ub, r)
        line = lines[0, pl.ds(r, 8), :]
        resids = [[] for _ in range(panes)]
        for l in range(layers):
            totals = pulled(ub, r, l, us, line, 2)
            for p in range(panes):
                resids[p].append(totals[p] - diag[l, p, pl.ds(r, 8), :] * us[l][p])
        for p in range(panes):
            sums[pl.ds(pl.multiple_of(i * 8, 8), 8), p * LANES : (p + 1) * LANES] = row_sums(
                resids[p]
            )

    gathered(layers, 2)
    start_all(lambda k: rough_copy(k, 1), N_ROUGH)

    gather_wait(0)
    span = tile_count * across
    chigh = crows + 16
    parts = cell + 8
    spots = [(a, b) for a in range(-1, down + 1) for b in range(-1, across + 1)]
    wanted = []
    for a, b in spots:
        pr, pc = g * down + a, t * across + b
        inside = (pr >= 0) & (pr < grp_count * down) & (pc >= 0) & (pc < span)
        wanted.append(jnp.where(inside, pr * span + pc, -2).astype(jnp.float32))

    for lo in range(0, len(spots), across + 2):

        def add(d, acc, lo=lo):
            block = all_dies[d]
            where = all_dies[d, pl.ds(cell + 2, 1), :]
            return tuple(
                jnp.where(where == wanted[lo + j], block, a) for j, a in enumerate(acc)
            )

        acc = lax.fori_loop(
            0, count, add, tuple(jnp.zeros((parts, LANES), jnp.float32) for _ in range(across + 2)),
            unroll=unroll_of(count, 8),
        )
        lane_p = iota((parts, LANES), 1)
        line = jnp.zeros((parts, LANES), jnp.float32)
        for j in range(across + 2):
            x = acc[j]
            step = LANES // 2
            while step >= cell:
                x = x + shift(x, step, 1)
                step //= 2
            line = jnp.where(lane_p // cell == j, x, line)
        line = shift(line, 8 - cell, 1)
        a = lo // (across + 2) - 1
        if a == -1:
            first, size, off = 0, 8, cell - 8
        elif a == down:
            first, size, off = 8 + crows, 8, 0
        else:
            first, size, off = 8 + a * cell, cell, 0
        n = 2 * layers + 1
        wide[n, first : first + size, :] = line[off : off + size]
        wide[n + 1, first : first + size, :] = jnp.broadcast_to(
            line[cell : cell + 1], (size, LANES)
        )
        wide[n + 2, first : first + size, :] = jnp.broadcast_to(
            line[cell + 1 : cell + 2], (size, LANES)
        )

    for phase in range(2):
        wait_all_recv(lambda k: rough_copy(k, phase), N_ROUGH)
        for f in range(layers + 1 if phase == 0 else layers):
            tile, q = 2 * phase + f // per, f % per
            target = f if phase == 0 else layers + 1 + f

            def joined(left, middle, right, size):
                lane = iota((size, LANES), 1)
                x = shift(middle, 8 - ccols * q, 1)
                x = jnp.where((lane >= 8) & (lane < 8 + ccols), x, 0.0)
                x = jnp.where(lane < 8, shift(left, 8 - ccols - ccols * q, 1), x)
                return jnp.where(
                    (lane >= 8 + ccols) & (lane < 16 + ccols),
                    shift(right, 8 + ccols - ccols * q, 1),
                    x,
                )

            wide[target, 8 : 8 + crows, :] = joined(
                rough_side[1, tile], rough[tile], rough_side[0, tile], crows
            )
            wide[target, 0:8, :] = joined(
                rough_corner[3, tile], rough_row[1, tile], rough_corner[2, tile], 8
            )
            wide[target, 8 + crows : chigh, :] = joined(
                rough_corner[1, tile], rough_row[0, tile], rough_corner[0, tile], 8
            )

    kc = [wide[l] * (0.5 / area) for l in range(layers)]
    cx = [harmonic(k, shift(k, -1, 0)) for k in kc]
    cy = [harmonic(k, shift(k, -1, 1)) for k in kc]
    cz = [harmonic(kc[l], kc[l + 1]) * area for l in range(layers - 1)]
    top_rhs, top_c, top_b = (wide[2 * layers + 1 + j] for j in range(3))
    weights = []
    for l in range(layers):
        d = cx[l] + shift(cx[l], 1, 0) + cy[l] + shift(cy[l], 1, 1)
        if l == 0:
            d = d + wide[layers]
        else:
            d = d + cz[l - 1]
        d = d + (cz[l] if l < layers - 1 else top_b)
        weights.append(guarded_weight(d))
    crow = (iota((chigh, LANES), 0) + (cell - 8)) % cell
    ccol = (iota((chigh, LANES), 1) + (cell - 8)) % cell
    low_x, high_x = crow != 0, crow != cell - 1
    low_y, high_y = ccol != 0, ccol != cell - 1
    near = sum(jnp.where(m, one, none) for m in (low_x, high_x, low_y, high_y))
    top_d = top_c * near + top_b
    top_w = guarded_weight(top_d)
    errors = [weights[l] * wide[layers + 1 + l] for l in range(layers)]
    top = top_w * top_rhs
    for _ in range(NC - 1):
        new = []
        for l in range(layers):
            e = errors[l]
            total = wide[layers + 1 + l]
            total = total + cx[l] * shift(e, -1, 0) + shift(cx[l] * e, 1, 0)
            total = total + cy[l] * shift(e, -1, 1) + shift(cy[l] * e, 1, 1)
            if l > 0:
                total = total + cz[l - 1] * errors[l - 1]
            total = total + (cz[l] * errors[l + 1] if l < layers - 1 else top_b * top)
            new.append((1.0 - RELAX) * e + weights[l] * total)
        nearby = (
            jnp.where(low_x, shift(top, 1, 0), 0.0)
            + jnp.where(high_x, shift(top, -1, 0), 0.0)
            + jnp.where(low_y, shift(top, 1, 1), 0.0)
            + jnp.where(high_y, shift(top, -1, 1), 0.0)
        )
        top = top + top_w * (
            top_rhs + top_b * errors[layers - 1] + top_c * nearby - top_d * top
        )
        errors = new
    lane_c = iota((cell, LANES), 1)
    fix = jnp.zeros((cell, LANES), jnp.float32)
    for a in range(down):
        piece = shift(top[8 + a * cell : 8 + (a + 1) * cell], a * ccols - 8, 1)
        fix = jnp.where(lane_c // ccols == a, piece, fix)
    all_fixes[me] = fix
    gather_start(1)

    pick = (iota((LANES, cols), 0) == 8 + iota((LANES, cols), 1) // RATIO).astype(jnp.float32)
    fine = two_part_dot(jnp.concatenate(errors, axis=0), pick)
    for l in range(layers):
        for p in range(panes):
            spread[l, p] = fine[l * chigh : (l + 1) * chigh, p * LANES : (p + 1) * LANES]
    lane_s = iota((LANES, LANES), 1)
    wanted_lane = jnp.where(lane_s % 8 < HALO, 7, 8) + jnp.where(lane_s % 16 < 8, 0, ccols)
    wanted_lane = jnp.where(
        iota((LANES, LANES), 0) == wanted_lane, lane_s // 16, -1
    )
    sides_of = jnp.zeros((chigh, LANES), jnp.float32)
    for l in range(layers):
        sides_of = sides_of + two_part_dot(errors[l], (wanted_lane == l).astype(jnp.float32))
    along = iota((chigh, long), 1)
    coarse_row = jnp.where(along < rows + 64, along // RATIO + 8, 7)
    side_fix = two_part_dot(
        sides_of.T, (iota((chigh, long), 0) == coarse_row).astype(jnp.float32)
    )
    smooth = []
    for side in range(2):
        us = []
        for l in range(layers):
            at = 16 * l + 8 * side
            us.append(su[side, l] + side_fix[at : at + 8])
        smooth.append((us, strip_sweep(side, us)))
    fields = list(zip(*smooth))
    lay_lines(1, [line_rows(l, fields, False) for l in range(layers)])

    @pl.loop(1, height // 8 - 1)
    def _(i):
        r = pl.multiple_of(i * 8, 8)
        for l in range(layers):
            for p in range(panes):
                ub[l, p, pl.ds(r, 8), :] = ub[l, p, pl.ds(r, 8), :] + spread[l, p, pl.ds(i + 6, 1), :]

    sweep(ub, into(ua), 1, height // 8 - 1, 1, 0)

    def finish(l, p, r, new):
        out[l, pl.ds(r - TOP, 8), p * LANES : (p + 1) * LANES] = new

    sweep(ua, finish, TOP // 8, (height - TOP) // 8, 1, 1)

    gather_wait(1)
    group = lane_c // cell
    cols_out = (iota((LANES, edge), 0) == iota((LANES, edge), 1) // RATIO).astype(jnp.float32)
    for s in range(slots):
        spot = jnp.maximum(place[s], 0)
        pr, pc = spot // span, lax.rem(spot, span)
        target = (pr // down) * tile_count + pc // across
        local = lax.rem(pr, down) * across + lax.rem(pc, across)
        x = jnp.where(group == local, all_fixes[target], 0.0)
        step = LANES // 2
        while step >= cell:
            x = x + shift(x, step, 1)
            step //= 2
        c, b = die_conduct[s], bond[s]
        live = jnp.where(place[s] >= 0, 1.0, 0.0)
        p = die_power[s]
        wt = die_diagonal(c, b)[1]
        fixed[s] = live * two_part_dot(x, cols_out)
        for k in range(tall):
            dies[0, s, pl.ds(8 + 8 * k, 8), :] = (
                dies[1, s, pl.ds(8 + 8 * k, 8), :] + fixed[s, pl.ds(k, 1), :]
            )
        for n in range(NU):
            v = (1.0 - RELAX) * dies[n % 2, s, body, :] + wt * (p + c * around(n % 2, s))
            if n < NU - 1:
                dies[(n + 1) % 2, s, body, :] = v
        die_out[s] = live * v

    wait_all_send(halo_copy, len(DIRECTIONS))
    for phase in range(2):
        wait_all_send(lambda k: rough_copy(k, phase), N_ROUGH)


def per_device(grp_count, tile_count, *args):
    material, die_power = args[0], args[4]
    layers, rows, cols = material.shape
    slots, edge, _ = die_power.shape
    cell = edge // RATIO
    crows = rows // RATIO
    panes, long, height = cols // LANES, rows + LANES, rows + 2 * TOP
    count = grp_count * tile_count
    n_fields = 2 * layers + 1
    depth = -(-n_fields * HALO // 8) * 8
    vmem = pl.BlockSpec(memory_space=pltpu.VMEM)
    smem = pl.BlockSpec(memory_space=pltpu.SMEM)
    f32 = jnp.float32

    def scratch(*shape):
        return pltpu.VMEM(shape, f32)

    grid = (layers, panes, height, LANES)
    return pl.pallas_call(
        functools.partial(kernel, grp_count, tile_count),
        out_shape=(
            jax.ShapeDtypeStruct((layers, rows, cols), f32),
            jax.ShapeDtypeStruct((slots, edge, edge), f32),
        ),
        in_specs=[vmem, smem, vmem, vmem, vmem, smem, smem, smem],
        out_specs=(vmem, vmem),
        scratch_shapes=[
            scratch(n_fields, panes, height, LANES),
            scratch(*grid),
            scratch(*grid),
            scratch(layers - 1, panes, height, LANES),
            scratch(*grid),
            scratch(*grid),
            scratch(*grid),
            scratch(*grid),
            scratch(rows, LANES),
            scratch(LANES, rows),
            scratch(2, depth, rows),
            scratch(3, LANES, LANES),
            scratch(2, n_fields, 8, long),
            scratch(2, layers, 8, long),
            scratch(2, layers, 8, long),
            scratch(2, layers - 1, 8, long),
            scratch(2, layers, 8, long),
            scratch(2, layers, 8, long),
            scratch(2, height, LANES),
            scratch(rows, cols),
            scratch(rows, LANES),
            scratch(4, crows, LANES),
            scratch(2, 4, crows, LANES),
            scratch(2, 4, 8, LANES),
            scratch(4, 4, 8, LANES),
            scratch(2, slots, edge + 16, edge),
            scratch(slots, cell, edge),
            scratch(count, cell + 8, LANES),
            scratch(count, cell, LANES),
            scratch(n_fields + 3, crows + 16, LANES),
            scratch(layers, panes, crows + 16, LANES),
            pltpu.SemaphoreType.DMA((len(DIRECTIONS) + 2 * N_ROUGH,)),
            pltpu.SemaphoreType.DMA((len(DIRECTIONS) + 2 * N_ROUGH,)),
            pltpu.SemaphoreType.DMA((2,)),
            pltpu.SemaphoreType.DMA((2,)),
        ],
        compiler_params=pltpu.CompilerParams(
            collective_id=0, has_side_effects=True, vmem_limit_bytes=60 * 1024 * 1024
        ),
    )(*args)


def solution(mesh):
    placed = (
        P(None, "grp", "tile"),
        P(),
        P("grp", "tile"),
        P(None, "grp", "tile"),
        P(("grp", "tile"), None, None),
        P(("grp", "tile")),
        P(("grp", "tile")),
        P(("grp", "tile")),
    )
    return jax.shard_map(
        functools.partial(per_device, mesh.shape["grp"], mesh.shape["tile"]),
        mesh=mesh,
        in_specs=placed,
        out_specs=(P(None, "grp", "tile"), P(("grp", "tile"), None, None)),
        check_vma=False,
    )
```

```python
import functools
import jax
import jax.numpy as jnp
from jax import lax
from jax.experimental import pallas as pl
from jax.experimental.pallas import tpu as pltpu
from jax.sharding import PartitionSpec as P

RATIO = 8
NU = 2
NC = 4
RELAX = 0.8
HALO = 4
TOP = 16
LANES = 128
FAR = 1e30
TINY = 1e-25
UNROLL = 5
MESH = pl.DeviceIdType.MESH
DIRECTIONS = ((-1, 0), (1, 0), (0, -1), (0, 1), (-1, -1), (-1, 1), (1, -1), (1, 1), (-1, 0), (1, 0))
N_ROUGH = 8


def inverse(x):
    return pltpu.reciprocal(x, approx=True)


def harmonic(a, b):
    total = a + b
    return 2.0 * a * b * inverse(jnp.where(total > 0, total, 1.0))


def guarded_weight(d):
    return RELAX * inverse(jnp.where(d > TINY, d, 1.0))


def unroll_of(n, most=UNROLL):
    return max(u for u in range(1, most + 1) if n % u == 0)


def iota(shape, dim):
    return lax.broadcasted_iota(jnp.int32, shape, dim)


def shift(x, amount, axis):
    return pltpu.roll(x, amount % x.shape[axis], axis)


def row_sums(fields):
    shape = fields[0].shape
    row = lax.broadcasted_iota(jnp.int32, shape, 0)
    xs = list(fields) + [jnp.zeros(shape, jnp.float32)] * (8 - len(fields))

    def merge(x, y, start, run):
        first = ((row - start + 8) % 8) % (2 * run) < run
        return jnp.where(first, x, y) + shift(jnp.where(first, y, x), -run, 0)

    z = [merge(xs[j], xs[j + 4], j, 4) for j in range(4)]
    y = [merge(z[j], z[j + 2], j, 2) for j in range(2)]
    return merge(y[0], y[1], 0, 1)


def halves(a):
    high = a.astype(jnp.bfloat16)
    return high, (a - high.astype(jnp.float32)).astype(jnp.bfloat16)


def two_part_dot(a, b):
    b = b.astype(jnp.bfloat16)
    return jnp.dot(
        jnp.concatenate(halves(a), axis=1),
        jnp.concatenate([b, b], axis=0),
        preferred_element_type=jnp.float32,
    )


def kernel(
    grp_count,
    tile_count,
    material_far,
    table,
    heat_sink_far,
    source_far,
    die_power_far,
    die_conduct,
    bond,
    place,
    out,
    die_out,
    material,
    heat_sink,
    source,
    die_power,
    field,
    zx,
    zy,
    zz,
    diag,
    weight,
    ua,
    ub,
    packed,
    turned,
    from_side,
    outer,
    strip,
    sx,
    sy,
    sz,
    sw,
    su,
    lines,
    sums,
    folded,
    rough,
    rough_side,
    rough_row,
    rough_corner,
    dies,
    fixed,
    all_dies,
    all_fixes,
    wide,
    spread,
    send_sem,
    recv_sem,
    gather_send,
    gather_recv,
    load_sem,
    die_sem,
):
    layers, rows, cols = material.shape
    slots, edge, _ = die_power.shape
    cell = edge // RATIO
    down, across = rows // edge, cols // edge
    crows, ccols = rows // RATIO, cols // RATIO
    panes = cols // LANES
    long = rows + LANES
    height = rows + 2 * TOP
    n_fields = 2 * layers + 1
    area = float(RATIO * RATIO)
    per = LANES // ccols
    count = grp_count * tile_count
    g = lax.axis_index("grp")
    t = lax.axis_index("tile")
    me = g * tile_count + t

    def each_peer(act):
        for dg in range(grp_count):
            for dt in range(tile_count):
                if dg or dt:
                    act((lax.rem(g + dg, grp_count), lax.rem(t + dt, tile_count)))

    def exists(dy, dx):
        ok = jnp.bool_(True)
        if dy:
            ok = jnp.logical_and(ok, g > 0 if dy < 0 else g < grp_count - 1)
        if dx:
            ok = jnp.logical_and(ok, t > 0 if dx < 0 else t < tile_count - 1)
        return ok

    pieces = unroll_of(rows // 8, 4)
    piece = rows // pieces

    def loads(n):
        some = pl.ds(pl.multiple_of(n * piece, 8), piece)
        pairs = (
            (material_far.at[:, some, :], material.at[:, some, :]),
            (source_far.at[:, some, :], source.at[:, some, :]),
            (heat_sink_far.at[some, :], heat_sink.at[some, :]),
        )
        return [
            pltpu.make_async_copy(a, b, load_sem.at[j, n]) for j, (a, b) in enumerate(pairs)
        ]

    die_load = pltpu.make_async_copy(die_power_far, die_power, die_sem)
    for n in range(pieces):
        for load in loads(n):
            load.start()
    die_load.start()

    for top in (0, height - TOP):
        field[0:layers, :, top : top + TOP, :] = jnp.full((layers, panes, TOP, LANES), FAR, jnp.float32)
        field[layers:n_fields, :, top : top + TOP, :] = jnp.zeros(
            (n_fields - layers, panes, TOP, LANES), jnp.float32
        )
    cut = HALO * layers
    from_side[:, 0:cut, :] = jnp.full((2, cut, rows), FAR, jnp.float32)
    from_side[:, cut:, :] = jnp.zeros((2, from_side.shape[1] - cut, rows), jnp.float32)
    outer[...] = jnp.where(iota(outer.shape, 2) % 64 < cut, FAR, 0.0)
    for n in range(2):
        for at in (0, edge + 8):
            dies[n, :, pl.ds(at, 8), :] = jnp.zeros((slots, 8, edge), jnp.float32)
    rough_side[...] = jnp.zeros_like(rough_side)
    rough_row[...] = jnp.zeros_like(rough_row)
    rough_corner[...] = jnp.zeros_like(rough_corner)
    zx[:, :, 0:8, :] = jnp.zeros((layers, panes, 8, LANES), jnp.float32)

    barrier = pltpu.get_barrier_semaphore()

    each_peer(
        lambda where: pl.semaphore_signal(barrier, inc=1, device_id=where, device_id_type=MESH)
    )

    lane8 = iota((8, LANES), 1)
    sub8 = iota((8, LANES), 0)

    def right_lane(f):
        return HALO * f

    def left_lane(f):
        return 64 + 8 * (f // 2) + HALO * (1 - f % 2)

    doubled = [jnp.full((8, LANES), 2.0 * table[m], jnp.float32) for m in range(table.shape[0])]

    @pl.loop(0, pieces)
    def _(n):
        for load in loads(n):
            load.wait()

        @pl.loop(0, piece // 8, unroll=unroll_of(piece // 8, 4))
        def _(i):
            r = pl.multiple_of(n * piece + i * 8, 8)
            edges = jnp.zeros((8, LANES), jnp.float32)
            summed = [[] for _ in range(panes)]
            for f in range(n_fields):
                xs = []
                for p in range(panes):
                    part = slice(p * LANES, (p + 1) * LANES)
                    if f < layers:
                        kind = material[f, pl.ds(r, 8), part]
                        values = list(doubled)
                        bit = 1
                        while len(values) > 1:
                            odd = (kind & bit) != 0
                            values = [
                                jnp.where(odd, values[m + 1], values[m]) if m + 1 < len(values) else values[m]
                                for m in range(0, len(values), 2)
                            ]
                            bit *= 2
                        summed[p].append(values[0])
                        x = inverse(values[0])
                    elif f < 2 * layers:
                        x = source[f - layers, pl.ds(r, 8), part]
                    else:
                        x = heat_sink[pl.ds(r, 8), part]
                        summed[p].append(x)
                    field[f, p, pl.ds(TOP + r, 8), :] = x
                    xs.append(x)
                a, b = right_lane(f), left_lane(f)
                right = shift(xs[-1], HALO + a, 1)
                left = shift(xs[0], b, 1)
                edges = jnp.where((lane8 >= a) & (lane8 < a + HALO), right, edges)
                edges = jnp.where((lane8 >= b) & (lane8 < b + HALO), left, edges)
            packed[pl.ds(r, 8), :] = edges
            for p in range(panes):
                sums[pl.ds(r, 8), p * LANES : (p + 1) * LANES] = row_sums(summed[p])

    turned[...] = packed[...].T

    pl.semaphore_wait(barrier, count - 1)

    depth = from_side.shape[1]

    def halo_copy(k):
        dy, dx = DIRECTIONS[k]
        if k < 2:
            src = field.at[:, :, pl.ds(TOP if dy < 0 else height - TOP - 8, 8), :]
            dst = field.at[:, :, pl.ds(height - TOP if dy < 0 else TOP - 8, 8), :]
        elif dy == 0:
            src = turned.at[pl.ds(0 if dx > 0 else 64, depth), :]
            dst = from_side.at[0 if dx > 0 else 1]
        else:
            src = packed.at[pl.ds(0 if dy < 0 else rows - 8, 8), :]
            which = 2 if dx == 0 else (0 if dx > 0 else 1)
            dst = outer.at[which, pl.ds(0 if dy < 0 else LANES - 8, 8), :]
        return pltpu.make_async_remote_copy(
            src_ref=src, dst_ref=dst, send_sem=send_sem.at[k], recv_sem=recv_sem.at[k],
            device_id=(g + dy, t + dx), device_id_type=MESH,
        )

    def rough_copy(k, phase):
        dy, dx = DIRECTIONS[k]
        half = pl.ds(2 * phase, 2)
        if dy == 0:
            src = rough.at[half]
            dst = rough_side.at[k - 2, half]
        else:
            src = rough.at[half, pl.ds(0 if dy < 0 else crows - 8, 8), :]
            dst = (rough_row.at[k, half] if dx == 0 else rough_corner.at[k - 4, half])
        s = len(DIRECTIONS) + N_ROUGH * phase + k
        return pltpu.make_async_remote_copy(
            src_ref=src, dst_ref=dst, send_sem=send_sem.at[s], recv_sem=recv_sem.at[s],
            device_id=(g + dy, t + dx), device_id_type=MESH,
        )

    def start_all(make, n):
        for k, (dy, dx) in enumerate(DIRECTIONS[:n]):
            pl.when(exists(dy, dx))(lambda k=k: make(k).start())

    def wait_all_recv(make, n):
        for k, (dy, dx) in enumerate(DIRECTIONS[:n]):
            pl.when(exists(-dy, -dx))(lambda k=k: make(k).wait_recv())

    def wait_all_send(make, n):
        for k, (dy, dx) in enumerate(DIRECTIONS[:n]):
            pl.when(exists(dy, dx))(lambda k=k: make(k).wait_send())

    start_all(halo_copy, len(DIRECTIONS))

    first8, last8 = lane8 == 0, lane8 == LANES - 1

    def from_right(xs, p, end):
        turn = shift(xs[p], -1, 1)
        if p < panes - 1:
            return jnp.where(last8, shift(xs[p + 1], -1, 1), turn)
        return turn if end is None else jnp.where(last8, end, turn)

    def from_left(xs, p, end):
        return jnp.where(first8, end if p == 0 else shift(xs[p - 1], 1, 1), shift(xs[p], 1, 1))

    def line_ends(line, l, q):
        return shift(line, -(8 * l + 2 * q + 1), 1)

    early, late = TOP // 8 + 2, (height - TOP) // 8 - 1

    def across_down(r, l, p):
        fx = inverse(field[l, p, pl.ds(r, 8), :] + field[l, p, pl.ds(r + 1, 8), :])
        zx[l, p, pl.ds(r, 8), :] = fx
        return fx

    def faces(i, line):
        r = pl.multiple_of(i * 8, 8)
        here = pl.ds(r, 8)
        ks = [[field[l, p, here, :] for p in range(panes)] for l in range(layers)]
        fxs = [[across_down(r, l, p) for p in range(panes)] for l in range(layers)]
        below = [None] * panes
        for l in range(layers):
            k = ks[l]
            ends = 0.0 if line is None else line_ends(line, l, 0)
            fys = [inverse(k[p] + from_right(k, p, None)) for p in range(panes)]
            fys[-1] = jnp.where(last8, ends, fys[-1])
            for p in range(panes):
                fy = fys[p]
                zy[l, p, here, :] = fy
                d = fxs[l][p] + zx[l, p, pl.ds(r - 1, 8), :] + fy + from_left(fys, p, ends)
                d = d + (field[2 * layers, p, here, :] if l == 0 else below[p])
                if l < layers - 1:
                    below[p] = inverse(k[p] + ks[l + 1][p])
                    zz[l, p, here, :] = below[p]
                    d = d + below[p]
                diag[l, p, here, :] = d
                if line is not None:
                    first_sweep(here, l, p, d)

    def first_sweep(here, l, p, d):
        wt = guarded_weight(d)
        weight[l, p, here, :] = wt
        ua[l, p, here, :] = wt * field[layers + l, p, here, :]

    for l in range(layers):
        for p in range(panes):
            across_down((early - 1) * 8, l, p)

    @pl.loop(early, late, unroll=unroll_of(late - early))
    def _(i):
        faces(i, None)

    col_d = iota((8, LANES), 1)
    one, none = jnp.float32(1.0), jnp.float32(0.0)
    inner = jnp.where(col_d > 0, one, none) + jnp.where(col_d < edge - 1, one, none) + 1.0
    first_row = jnp.where(sub8 > 0, one, none)
    last_row = jnp.where(sub8 < 7, one, none)
    beside = (
        jnp.abs(iota((edge, edge), 0) - iota((edge, edge), 1)) == 1
    ).astype(jnp.float32)
    body = pl.ds(8, edge)
    tall = edge // 8

    def die_diagonal(c, b):
        tops = [c * (inner + first_row) + b, c * (inner + 1.0) + b, c * (inner + last_row) + b]
        ws = [guarded_weight(d) for d in tops]

        def full(x):
            return jnp.concatenate([x[0]] + [x[1]] * (tall - 2) + [x[2]], axis=0)

        return full(tops), full(ws)

    def around(n, s):
        v = dies[n, s, body, :]
        return (
            dies[n, s, pl.ds(7, edge), :] + dies[n, s, pl.ds(9, edge), :] + two_part_dot(v, beside)
        )

    rows_in = (iota((cell, edge), 0) == iota((cell, edge), 1) // RATIO).astype(jnp.bfloat16)
    rows_in = jnp.concatenate([rows_in, rows_in], axis=1)
    message = jnp.zeros((cell, LANES), jnp.float32)
    die_load.wait()
    params = jnp.full((8, LANES), -1.0, jnp.float32)
    for s in range(slots):
        c, b = die_conduct[s], bond[s]
        live = jnp.where(place[s] >= 0, 1.0, 0.0)
        p = die_power[s]
        d, wt = die_diagonal(c, b)
        dies[0, s, body, :] = wt * p
        dies[1, s, body, :] = (1.0 - RELAX) * dies[0, s, body, :] + wt * (p + c * around(0, s))
        resid = p + c * around(1, s) - d * dies[1, s, body, :]
        cols_in = (
            iota((edge, LANES), 0) // RATIO + cell * s == iota((edge, LANES), 1)
        ).astype(jnp.float32)
        by_row = jnp.dot(
            rows_in, jnp.concatenate(halves(resid), axis=0), preferred_element_type=jnp.float32
        )
        message = message + live * two_part_dot(by_row, cols_in)
        mine = lane8 // cell == s
        value = jnp.where(
            sub8 == 0, c, jnp.where(sub8 == 1, b * area, place[s].astype(jnp.float32))
        )
        params = jnp.where(mine, value, params)
    all_dies[me, 0:cell, :] = message
    all_dies[me, cell : cell + 8, :] = params

    def gather_start(phase):
        every = (all_dies, all_fixes)[phase]
        each_peer(
            lambda where: pltpu.make_async_remote_copy(
                src_ref=every.at[me], dst_ref=every.at[me],
                send_sem=gather_send.at[phase], recv_sem=gather_recv.at[phase],
                device_id=where, device_id_type=MESH,
            ).start()
        )

    def gather_wait(phase):
        others = (all_dies, all_fixes)[phase].at[pl.ds(0, count - 1)]
        for sem in (gather_send, gather_recv):
            pltpu.make_async_copy(others, others, sem.at[phase]).wait()

    def gathered(total, first_tile):
        pick = (iota((cols, LANES), 0) // RATIO == iota((cols, LANES), 1)).astype(jnp.float32)
        folded[...] = two_part_dot(sums[...], pick)
        for tile in range(2):
            result = jnp.zeros((crows, LANES), jnp.float32)
            for q in range(per):
                f = tile * per + q
                if f < total:
                    result = result + shift(folded[pl.ds(f, crows, stride=8), :], q * ccols, 1)
            rough[first_tile + tile] = result

    gathered(layers + 1, 0)

    wait_all_recv(halo_copy, len(DIRECTIONS))
    gather_start(0)
    start_all(lambda k: rough_copy(k, 0), N_ROUGH)
    extra = [outer[j].T for j in range(3)]

    def woven(near, far, f, first):
        size = near.shape[1]
        lower = iota((8, size), 0) < HALO
        m = f // 2 * 8
        a = (far if first else near)[m : m + 8]
        b = (near if first else far)[m : m + 8]
        return (
            jnp.where(lower, a, b) if f % 2 == 0 else shift(jnp.where(lower, b, a), HALO, 0)
        )

    for f in range(n_fields):
        for side in range(2):
            at = 64 if side == 0 else 0
            strip[side, f, :, 0:rows] = woven(
                turned[at : at + depth, :], from_side[side], f, side == 0
            )
            strip[side, f, :, rows:long] = woven(
                extra[2][at : at + depth], extra[side][64 - at : 64 - at + depth], f, side == 0
            )

    def strip_total(side, l, us):
        u, fx, fy = us[l], sx[side, l], sy[side, l]
        total = strip[side, layers + l] + fx * shift(u, -1, 1) + shift(fx * u, 1, 1)
        total = total + fy * shift(u, -1, 0) + shift(fy * u, 1, 0)
        if l > 0:
            total = total + sz[side, l - 1] * us[l - 1]
        if l < layers - 1:
            total = total + sz[side, l] * us[l + 1]
        return total

    def strip_sweep(side, us):
        return [
            (1.0 - RELAX) * us[l] + sw[side, l] * strip_total(side, l, us) for l in range(layers)
        ]

    def lay_lines(k, rows_of):
        x = jnp.concatenate(
            rows_of + [jnp.zeros((LANES - 8 * layers, long), jnp.float32)], axis=0
        ).T
        lines[k, TOP : TOP + rows + 8, :] = x[0 : rows + 8]
        lines[k, TOP - 8 : TOP, :] = x[long - 8 : long]

    sub_long = iota((8, long), 0)

    def line_rows(l, fields, has_face):
        parts = []
        if has_face:
            parts = [shift(sy[1, l], -3, 0), shift(sy[0, l], -2, 0)]
        for left, right in fields:
            q = len(parts)
            parts.append(shift(right[l], q - 4, 0))
            parts.append(shift(sy[0, l] * left[l], q - 2, 0))
        x = parts[0]
        for q in range(1, len(parts)):
            x = jnp.where(sub_long == q, parts[q], x)
        return x

    smooth = []
    for side in range(2):
        below = None
        us = []
        for l in range(layers):
            k = strip[side, l]
            fx = inverse(k + shift(k, -1, 1))
            fy = inverse(k + shift(k, -1, 0))
            sx[side, l] = fx
            sy[side, l] = fy
            d = fx + shift(fx, 1, 1) + fy + shift(fy, 1, 0)
            d = d + (strip[side, 2 * layers] if l == 0 else below)
            if l < layers - 1:
                below = inverse(k + strip[side, l + 1])
                sz[side, l] = below
                d = d + below
            wt = guarded_weight(d)
            sw[side, l] = wt
            us.append(wt * strip[side, layers + l])
        new = strip_sweep(side, us)
        for l in range(layers):
            su[side, l] = new[l]
        smooth.append((us, new))
    fields = list(zip(*smooth))
    lay_lines(0, [line_rows(l, fields, True) for l in range(layers)])

    def whole(i):
        faces(i, lines[0, pl.ds(pl.multiple_of(i * 8, 8), 8), :])

    pl.loop(1, early, unroll=early - 1)(whole)

    @pl.loop(early, late, unroll=unroll_of(late - early))
    def _(i):
        here = pl.ds(pl.multiple_of(i * 8, 8), 8)
        line = lines[0, here, :]
        for l in range(layers):
            ends = line_ends(line, l, 0)
            zy[l, panes - 1, here, :] = jnp.where(last8, ends, zy[l, panes - 1, here, :])
            for p in range(panes):
                d = diag[l, p, here, :]
                if p == 0:
                    d = d + jnp.where(first8, ends, 0.0)
                if p == panes - 1:
                    d = d + jnp.where(last8, ends, 0.0)
                if p in (0, panes - 1):
                    diag[l, p, here, :] = d
                first_sweep(here, l, p, d)

    pl.loop(late, height // 8 - 1, unroll=height // 8 - 1 - late)(whole)

    def pulled(u, r, l, us, line, q):
        here = pl.ds(r, 8)
        fys = [zy[l, p, here, :] for p in range(panes)]
        flows = [fys[p] * us[l][p] for p in range(panes)]
        ends = line_ends(line, l, q)
        totals = []
        for p in range(panes):
            total = field[layers + l, p, here, :]
            total = total + zx[l, p, here, :] * u[l, p, pl.ds(r + 1, 8), :]
            total = total + zx[l, p, pl.ds(r - 1, 8), :] * u[l, p, pl.ds(r - 1, 8), :]
            total = total + fys[p] * from_right(us[l], p, ends) + from_left(flows, p, ends)
            if l > 0:
                total = total + zz[l - 1, p, here, :] * us[l - 1][p]
            if l < layers - 1:
                total = total + zz[l, p, here, :] * us[l + 1][p]
            totals.append(total)
        return totals

    def layers_at(u, r):
        return [[u[l, p, pl.ds(r, 8), :] for p in range(panes)] for l in range(layers)]

    def sweep(u, store, first, last, k, q):
        @pl.loop(first, last, unroll=unroll_of(last - first))
        def _(i):
            r = pl.multiple_of(i * 8, 8)
            us = layers_at(u, r)
            line = lines[k, pl.ds(r, 8), :]
            for l in range(layers):
                totals = pulled(u, r, l, us, line, q)
                for p in range(panes):
                    store(
                        l, p, r,
                        (1.0 - RELAX) * us[l][p] + weight[l, p, pl.ds(r, 8), :] * totals[p],
                    )

    def into(ref):
        def store(l, p, r, new):
            ref[l, p, pl.ds(r, 8), :] = new

        return store

    sweep(ua, into(ub), 1, height // 8 - 1, 0, 1)

    @pl.loop(0, crows, unroll=unroll_of(crows))
    def _(i):
        r = pl.multiple_of(i * 8 + TOP, 8)
        us = layers_at(ub, r)
        line = lines[0, pl.ds(r, 8), :]
        resids = [[] for _ in range(panes)]
        for l in range(layers):
            totals = pulled(ub, r, l, us, line, 2)
            for p in range(panes):
                resids[p].append(totals[p] - diag[l, p, pl.ds(r, 8), :] * us[l][p])
        for p in range(panes):
            sums[pl.ds(pl.multiple_of(i * 8, 8), 8), p * LANES : (p + 1) * LANES] = row_sums(
                resids[p]
            )

    gathered(layers, 2)
    start_all(lambda k: rough_copy(k, 1), N_ROUGH)

    chigh = crows + 16

    def join(phase):
        wait_all_recv(lambda k: rough_copy(k, phase), N_ROUGH)
        for f in range(layers + 1 if phase == 0 else layers):
            tile, q = 2 * phase + f // per, f % per
            target = f if phase == 0 else layers + 1 + f

            def joined(left, middle, right, size):
                lane = iota((size, LANES), 1)
                x = shift(middle, 8 - ccols * q, 1)
                x = jnp.where((lane >= 8) & (lane < 8 + ccols), x, 0.0)
                x = jnp.where(lane < 8, shift(left, 8 - ccols - ccols * q, 1), x)
                return jnp.where(
                    (lane >= 8 + ccols) & (lane < 16 + ccols),
                    shift(right, 8 + ccols - ccols * q, 1),
                    x,
                )

            wide[target, 8 : 8 + crows, :] = joined(
                rough_side[1, tile], rough[tile], rough_side[0, tile], crows
            )
            wide[target, 0:8, :] = joined(
                rough_corner[3, tile], rough_row[1, tile], rough_corner[2, tile], 8
            )
            wide[target, 8 + crows : chigh, :] = joined(
                rough_corner[1, tile], rough_row[0, tile], rough_corner[0, tile], 8
            )

    join(0)
    kc = [wide[l] * (0.5 / area) for l in range(layers)]
    cx = [harmonic(k, shift(k, -1, 0)) for k in kc]
    cy = [harmonic(k, shift(k, -1, 1)) for k in kc]
    cz = [harmonic(kc[l], kc[l + 1]) * area for l in range(layers - 1)]
    sums_of = []
    for l in range(layers):
        d = cx[l] + shift(cx[l], 1, 0) + cy[l] + shift(cy[l], 1, 1)
        if l == 0:
            d = d + wide[layers]
        else:
            d = d + cz[l - 1]
        sums_of.append(d + cz[l] if l < layers - 1 else d)

    gather_wait(0)
    span = tile_count * across
    parts = cell + 8
    spots = [(a, b) for a in range(-1, down + 1) for b in range(-1, across + 1)]
    wanted = []
    for a, b in spots:
        pr, pc = g * down + a, t * across + b
        inside = (pr >= 0) & (pr < grp_count * down) & (pc >= 0) & (pc < span)
        wanted.append(jnp.where(inside, pr * span + pc, -2).astype(jnp.float32))

    for lo in range(0, len(spots), across + 2):

        def add(d, acc, lo=lo):
            block = all_dies[d]
            where = all_dies[d, pl.ds(cell + 2, 1), :]
            return tuple(
                jnp.where(where == wanted[lo + j], block, a) for j, a in enumerate(acc)
            )

        acc = lax.fori_loop(
            0, count, add, tuple(jnp.zeros((parts, LANES), jnp.float32) for _ in range(across + 2)),
            unroll=unroll_of(count, 8),
        )
        lane_p = iota((parts, LANES), 1)
        line = jnp.zeros((parts, LANES), jnp.float32)
        for j in range(across + 2):
            x = acc[j]
            step = LANES // 2
            while step >= cell:
                x = x + shift(x, step, 1)
                step //= 2
            line = jnp.where(lane_p // cell == j, x, line)
        line = shift(line, 8 - cell, 1)
        a = lo // (across + 2) - 1
        if a == -1:
            first, size, off = 0, 8, cell - 8
        elif a == down:
            first, size, off = 8 + crows, 8, 0
        else:
            first, size, off = 8 + a * cell, cell, 0
        n = 2 * layers + 1
        wide[n, first : first + size, :] = line[off : off + size]
        wide[n + 1, first : first + size, :] = jnp.broadcast_to(
            line[cell : cell + 1], (size, LANES)
        )
        wide[n + 2, first : first + size, :] = jnp.broadcast_to(
            line[cell + 1 : cell + 2], (size, LANES)
        )

    top_rhs, top_c, top_b = (wide[2 * layers + 1 + j] for j in range(3))
    weights = [guarded_weight(d) for d in sums_of[:-1]] + [guarded_weight(sums_of[-1] + top_b)]
    crow = (iota((chigh, LANES), 0) + (cell - 8)) % cell
    ccol = (iota((chigh, LANES), 1) + (cell - 8)) % cell
    low_x, high_x = crow != 0, crow != cell - 1
    low_y, high_y = ccol != 0, ccol != cell - 1
    near = sum(jnp.where(m, one, none) for m in (low_x, high_x, low_y, high_y))
    top_d = top_c * near + top_b
    top_w = guarded_weight(top_d)
    join(1)
    errors = [weights[l] * wide[layers + 1 + l] for l in range(layers)]
    top = top_w * top_rhs
    for _ in range(NC - 1):
        new = []
        for l in range(layers):
            e = errors[l]
            total = wide[layers + 1 + l]
            total = total + cx[l] * shift(e, -1, 0) + shift(cx[l] * e, 1, 0)
            total = total + cy[l] * shift(e, -1, 1) + shift(cy[l] * e, 1, 1)
            if l > 0:
                total = total + cz[l - 1] * errors[l - 1]
            total = total + (cz[l] * errors[l + 1] if l < layers - 1 else top_b * top)
            new.append((1.0 - RELAX) * e + weights[l] * total)
        nearby = (
            jnp.where(low_x, shift(top, 1, 0), 0.0)
            + jnp.where(high_x, shift(top, -1, 0), 0.0)
            + jnp.where(low_y, shift(top, 1, 1), 0.0)
            + jnp.where(high_y, shift(top, -1, 1), 0.0)
        )
        top = top + top_w * (
            top_rhs + top_b * errors[layers - 1] + top_c * nearby - top_d * top
        )
        errors = new
    lane_c = iota((cell, LANES), 1)
    fix = jnp.zeros((cell, LANES), jnp.float32)
    for a in range(down):
        piece = shift(top[8 + a * cell : 8 + (a + 1) * cell], a * ccols - 8, 1)
        fix = jnp.where(lane_c // ccols == a, piece, fix)
    all_fixes[me] = fix
    gather_start(1)

    pick = (iota((LANES, cols), 0) == 8 + iota((LANES, cols), 1) // RATIO).astype(jnp.float32)
    fine = two_part_dot(jnp.concatenate(errors, axis=0), pick)
    for l in range(layers):
        for p in range(panes):
            spread[l, p] = fine[l * chigh : (l + 1) * chigh, p * LANES : (p + 1) * LANES]
    lane_s = iota((LANES, LANES), 1)
    wanted_lane = jnp.where(lane_s % 8 < HALO, 7, 8) + jnp.where(lane_s % 16 < 8, 0, ccols)
    wanted_lane = jnp.where(
        iota((LANES, LANES), 0) == wanted_lane, lane_s // 16, -1
    )
    sides_of = jnp.zeros((chigh, LANES), jnp.float32)
    for l in range(layers):
        sides_of = sides_of + two_part_dot(errors[l], (wanted_lane == l).astype(jnp.float32))
    along = iota((chigh, long), 1)
    coarse_row = jnp.where(along < rows + 64, along // RATIO + 8, 7)
    side_fix = two_part_dot(
        sides_of.T, (iota((chigh, long), 0) == coarse_row).astype(jnp.float32)
    )
    smooth = []
    for side in range(2):
        us = []
        for l in range(layers):
            at = 16 * l + 8 * side
            us.append(su[side, l] + side_fix[at : at + 8])
        smooth.append((us, strip_sweep(side, us)))
    fields = list(zip(*smooth))
    lay_lines(1, [line_rows(l, fields, False) for l in range(layers)])

    @pl.loop(1, height // 8 - 1)
    def _(i):
        r = pl.multiple_of(i * 8, 8)
        for l in range(layers):
            for p in range(panes):
                ub[l, p, pl.ds(r, 8), :] = ub[l, p, pl.ds(r, 8), :] + spread[l, p, pl.ds(i + 6, 1), :]

    sweep(ub, into(ua), 1, height // 8 - 1, 1, 0)

    def finish(l, p, r, new):
        out[l, pl.ds(r - TOP, 8), p * LANES : (p + 1) * LANES] = new

    sweep(ua, finish, TOP // 8, (height - TOP) // 8, 1, 1)

    gather_wait(1)
    group = lane_c // cell
    cols_out = (iota((LANES, edge), 0) == iota((LANES, edge), 1) // RATIO).astype(jnp.float32)
    for s in range(slots):
        spot = jnp.maximum(place[s], 0)
        pr, pc = spot // span, lax.rem(spot, span)
        target = (pr // down) * tile_count + pc // across
        local = lax.rem(pr, down) * across + lax.rem(pc, across)
        x = jnp.where(group == local, all_fixes[target], 0.0)
        step = LANES // 2
        while step >= cell:
            x = x + shift(x, step, 1)
            step //= 2
        c, b = die_conduct[s], bond[s]
        live = jnp.where(place[s] >= 0, 1.0, 0.0)
        p = die_power[s]
        wt = die_diagonal(c, b)[1]
        fixed[s] = live * two_part_dot(x, cols_out)
        for k in range(tall):
            dies[0, s, pl.ds(8 + 8 * k, 8), :] = (
                dies[1, s, pl.ds(8 + 8 * k, 8), :] + fixed[s, pl.ds(k, 1), :]
            )
        for n in range(NU):
            v = (1.0 - RELAX) * dies[n % 2, s, body, :] + wt * (p + c * around(n % 2, s))
            if n < NU - 1:
                dies[(n + 1) % 2, s, body, :] = v
        die_out[s] = live * v

    wait_all_send(halo_copy, len(DIRECTIONS))
    for phase in range(2):
        wait_all_send(lambda k: rough_copy(k, phase), N_ROUGH)


def per_device(grp_count, tile_count, *args):
    material, die_power = args[0], args[4]
    layers, rows, cols = material.shape
    slots, edge, _ = die_power.shape
    cell = edge // RATIO
    crows = rows // RATIO
    panes, long, height = cols // LANES, rows + LANES, rows + 2 * TOP
    count = grp_count * tile_count
    n_fields = 2 * layers + 1
    depth = -(-n_fields * HALO // 8) * 8
    vmem = pl.BlockSpec(memory_space=pltpu.VMEM)
    smem = pl.BlockSpec(memory_space=pltpu.SMEM)
    far = pl.BlockSpec(memory_space=pl.ANY)
    f32 = jnp.float32

    def scratch(*shape):
        return pltpu.VMEM(shape, f32)

    grid = (layers, panes, height, LANES)
    return pl.pallas_call(
        functools.partial(kernel, grp_count, tile_count),
        out_shape=(
            pltpu.VMEM((layers, rows, cols), f32),
            pltpu.VMEM((slots, edge, edge), f32),
        ),
        in_specs=[far, smem, far, far, far, smem, smem, smem],
        out_specs=(vmem, vmem),
        scratch_shapes=[
            pltpu.VMEM(material.shape, material.dtype),
            scratch(rows, cols),
            scratch(layers, rows, cols),
            scratch(slots, edge, edge),
            scratch(n_fields, panes, height, LANES),
            scratch(*grid),
            scratch(*grid),
            scratch(layers - 1, panes, height, LANES),
            scratch(*grid),
            scratch(*grid),
            scratch(*grid),
            scratch(*grid),
            scratch(rows, LANES),
            scratch(LANES, rows),
            scratch(2, depth, rows),
            scratch(3, LANES, LANES),
            scratch(2, n_fields, 8, long),
            scratch(2, layers, 8, long),
            scratch(2, layers, 8, long),
            scratch(2, layers - 1, 8, long),
            scratch(2, layers, 8, long),
            scratch(2, layers, 8, long),
            scratch(2, height, LANES),
            scratch(rows, cols),
            scratch(rows, LANES),
            scratch(4, crows, LANES),
            scratch(2, 4, crows, LANES),
            scratch(2, 4, 8, LANES),
            scratch(4, 4, 8, LANES),
            scratch(2, slots, edge + 16, edge),
            scratch(slots, cell, edge),
            scratch(count, cell + 8, LANES),
            scratch(count, cell, LANES),
            scratch(n_fields + 3, crows + 16, LANES),
            scratch(layers, panes, crows + 16, LANES),
            pltpu.SemaphoreType.DMA((len(DIRECTIONS) + 2 * N_ROUGH,)),
            pltpu.SemaphoreType.DMA((len(DIRECTIONS) + 2 * N_ROUGH,)),
            pltpu.SemaphoreType.DMA((2,)),
            pltpu.SemaphoreType.DMA((2,)),
            pltpu.SemaphoreType.DMA((3, unroll_of(rows // 8, 4))),
            pltpu.SemaphoreType.DMA,
        ],
        compiler_params=pltpu.CompilerParams(
            collective_id=0, has_side_effects=True, vmem_limit_bytes=60 * 1024 * 1024
        ),
    )(*args)


def solution(mesh):
    placed = (
        P(None, "grp", "tile"),
        P(),
        P("grp", "tile"),
        P(None, "grp", "tile"),
        P(("grp", "tile"), None, None),
        P(("grp", "tile")),
        P(("grp", "tile")),
        P(("grp", "tile")),
    )
    return jax.shard_map(
        functools.partial(per_device, mesh.shape["grp"], mesh.shape["tile"]),
        mesh=mesh,
        in_specs=placed,
        out_specs=(P(None, "grp", "tile"), P(("grp", "tile"), None, None)),
        check_vma=False,
    )
```

```python
import functools
import jax
import jax.numpy as jnp
from jax import lax
from jax.experimental import pallas as pl
from jax.experimental.pallas import tpu as pltpu
from jax.sharding import PartitionSpec as P

RATIO = 8
NU = 2
NC = 4
RELAX = 0.8
HALO = 4
TOP = 16
LANES = 128
FAR = 1e30
TINY = 1e-25
UNROLL = 5
MESH = pl.DeviceIdType.MESH
DIRECTIONS = ((-1, 0), (1, 0), (0, -1), (0, 1), (-1, -1), (-1, 1), (1, -1), (1, 1), (-1, 0), (1, 0))
N_ROUGH = 8


def inverse(x):
    return pltpu.reciprocal(x, approx=True)


def harmonic(a, b):
    total = a + b
    return 2.0 * a * b * inverse(jnp.where(total > 0, total, 1.0))


def guarded_weight(d):
    return RELAX * inverse(jnp.where(d > TINY, d, 1.0))


def unroll_of(n, most=UNROLL):
    return max(u for u in range(1, most + 1) if n % u == 0)


def iota(shape, dim):
    return lax.broadcasted_iota(jnp.int32, shape, dim)


def shift(x, amount, axis):
    return pltpu.roll(x, amount % x.shape[axis], axis)


def row_sums(fields):
    shape = fields[0].shape
    row = lax.broadcasted_iota(jnp.int32, shape, 0)
    xs = list(fields) + [jnp.zeros(shape, jnp.float32)] * (8 - len(fields))

    def merge(x, y, start, run):
        first = ((row - start + 8) % 8) % (2 * run) < run
        return jnp.where(first, x, y) + shift(jnp.where(first, y, x), -run, 0)

    z = [merge(xs[j], xs[j + 4], j, 4) for j in range(4)]
    y = [merge(z[j], z[j + 2], j, 2) for j in range(2)]
    return merge(y[0], y[1], 0, 1)


def halves(a):
    high = a.astype(jnp.bfloat16)
    return high, (a - high.astype(jnp.float32)).astype(jnp.bfloat16)


def two_part_dot(a, b):
    b = b.astype(jnp.bfloat16)
    return jnp.dot(
        jnp.concatenate(halves(a), axis=1),
        jnp.concatenate([b, b], axis=0),
        preferred_element_type=jnp.float32,
    )


def kernel(
    grp_count,
    tile_count,
    material_far,
    table,
    heat_sink_far,
    source_far,
    die_power_far,
    die_conduct,
    bond,
    place,
    out,
    die_out,
    material,
    heat_sink,
    source,
    die_power,
    field,
    zx,
    zu,
    zy,
    zz,
    diag,
    weight,
    ua,
    ub,
    packed,
    turned,
    from_side,
    outer,
    strip,
    sx,
    sy,
    sz,
    sw,
    su,
    lines,
    sums,
    folded,
    rough,
    rough_side,
    rough_row,
    rough_corner,
    rim,
    rim_side,
    dies,
    fixed,
    all_dies,
    all_fixes,
    wide,
    spread,
    send_sem,
    recv_sem,
    gather_send,
    gather_recv,
    load_sem,
    die_sem,
):
    layers, rows, cols = material.shape
    slots, edge, _ = die_power.shape
    cell = edge // RATIO
    down, across = rows // edge, cols // edge
    crows, ccols = rows // RATIO, cols // RATIO
    panes = cols // LANES
    long = rows + LANES
    height = rows + 2 * TOP
    n_fields = 2 * layers + 1
    area = float(RATIO * RATIO)
    per = LANES // ccols
    count = grp_count * tile_count
    g = lax.axis_index("grp")
    t = lax.axis_index("tile")
    me = g * tile_count + t

    def each_peer(act):
        for dg in range(grp_count):
            for dt in range(tile_count):
                if dg or dt:
                    act((lax.rem(g + dg, grp_count), lax.rem(t + dt, tile_count)))

    def exists(dy, dx):
        ok = jnp.bool_(True)
        if dy:
            ok = jnp.logical_and(ok, g > 0 if dy < 0 else g < grp_count - 1)
        if dx:
            ok = jnp.logical_and(ok, t > 0 if dx < 0 else t < tile_count - 1)
        return ok

    pieces = unroll_of(rows // 8, 4)
    piece = rows // pieces

    def loads(n):
        some = pl.ds(pl.multiple_of(n * piece, 8), piece)
        pairs = (
            (material_far.at[:, some, :], material.at[:, some, :]),
            (source_far.at[:, some, :], source.at[:, some, :]),
            (heat_sink_far.at[some, :], heat_sink.at[some, :]),
        )
        return [
            pltpu.make_async_copy(a, b, load_sem.at[j, n]) for j, (a, b) in enumerate(pairs)
        ]

    die_load = pltpu.make_async_copy(die_power_far, die_power, die_sem)
    for n in range(pieces):
        for load in loads(n):
            load.start()
    die_load.start()

    for top in (0, height - TOP):
        field[0:layers, :, top : top + TOP, :] = jnp.full((layers, panes, TOP, LANES), FAR, jnp.float32)
        field[layers:n_fields, :, top : top + TOP, :] = jnp.zeros(
            (n_fields - layers, panes, TOP, LANES), jnp.float32
        )
    cut = HALO * layers
    from_side[:, 0:cut, :] = jnp.full((2, cut, rows), FAR, jnp.float32)
    from_side[:, cut:, :] = jnp.zeros((2, from_side.shape[1] - cut, rows), jnp.float32)
    outer[...] = jnp.where(iota(outer.shape, 2) % 64 < cut, FAR, 0.0)
    for n in range(2):
        for at in (0, edge + 8):
            dies[n, :, pl.ds(at, 8), :] = jnp.zeros((slots, 8, edge), jnp.float32)
    rough_side[...] = jnp.zeros_like(rough_side)
    rim_side[...] = jnp.zeros_like(rim_side)
    rough_row[...] = jnp.zeros_like(rough_row)
    rough_corner[...] = jnp.zeros_like(rough_corner)
    zx[:, :, 0:8, :] = jnp.zeros((layers, panes, 8, LANES), jnp.float32)

    barrier = pltpu.get_barrier_semaphore()

    each_peer(
        lambda where: pl.semaphore_signal(barrier, inc=1, device_id=where, device_id_type=MESH)
    )

    lane8 = iota((8, LANES), 1)
    sub8 = iota((8, LANES), 0)

    def right_lane(f):
        return HALO * f

    def left_lane(f):
        return 64 + 8 * (f // 2) + HALO * (1 - f % 2)

    doubled = [jnp.full((8, LANES), 2.0 * table[m], jnp.float32) for m in range(table.shape[0])]

    @pl.loop(0, pieces)
    def _(n):
        for load in loads(n):
            load.wait()

        @pl.loop(0, piece // 8, unroll=unroll_of(piece // 8, 4))
        def _(i):
            r = pl.multiple_of(n * piece + i * 8, 8)
            edges = jnp.zeros((8, LANES), jnp.float32)
            summed = [[] for _ in range(panes)]
            for f in range(n_fields):
                xs = []
                for p in range(panes):
                    part = slice(p * LANES, (p + 1) * LANES)
                    if f < layers:
                        kind = material[f, pl.ds(r, 8), part]
                        values = list(doubled)
                        bit = 1
                        while len(values) > 1:
                            odd = (kind & bit) != 0
                            values = [
                                jnp.where(odd, values[m + 1], values[m]) if m + 1 < len(values) else values[m]
                                for m in range(0, len(values), 2)
                            ]
                            bit *= 2
                        summed[p].append(values[0])
                        x = inverse(values[0])
                    elif f < 2 * layers:
                        x = source[f - layers, pl.ds(r, 8), part]
                    else:
                        x = heat_sink[pl.ds(r, 8), part]
                        summed[p].append(x)
                    field[f, p, pl.ds(TOP + r, 8), :] = x
                    xs.append(x)
                a, b = right_lane(f), left_lane(f)
                right = shift(xs[-1], HALO + a, 1)
                left = shift(xs[0], b, 1)
                edges = jnp.where((lane8 >= a) & (lane8 < a + HALO), right, edges)
                edges = jnp.where((lane8 >= b) & (lane8 < b + HALO), left, edges)
            packed[pl.ds(r, 8), :] = edges
            for p in range(panes):
                sums[pl.ds(r, 8), p * LANES : (p + 1) * LANES] = row_sums(summed[p])

    turned[...] = packed[...].T

    pl.semaphore_wait(barrier, count - 1)

    depth = from_side.shape[1]

    def halo_copy(k):
        dy, dx = DIRECTIONS[k]
        if k < 2:
            src = field.at[:, :, pl.ds(TOP if dy < 0 else height - TOP - 8, 8), :]
            dst = field.at[:, :, pl.ds(height - TOP if dy < 0 else TOP - 8, 8), :]
        elif dy == 0:
            src = turned.at[pl.ds(0 if dx > 0 else 64, depth), :]
            dst = from_side.at[0 if dx > 0 else 1]
        else:
            src = packed.at[pl.ds(0 if dy < 0 else rows - 8, 8), :]
            which = 2 if dx == 0 else (0 if dx > 0 else 1)
            dst = outer.at[which, pl.ds(0 if dy < 0 else LANES - 8, 8), :]
        return pltpu.make_async_remote_copy(
            src_ref=src, dst_ref=dst, send_sem=send_sem.at[k], recv_sem=recv_sem.at[k],
            device_id=(g + dy, t + dx), device_id_type=MESH,
        )

    def rough_copy(k, phase):
        dy, dx = DIRECTIONS[k]
        half = pl.ds(2 * phase, 2)
        if dy == 0 and phase == 1:
            src, dst = rim, rim_side.at[k - 2]
        elif dy == 0:
            src = rough.at[half]
            dst = rough_side.at[k - 2, half]
        else:
            src = rough.at[half, pl.ds(0 if dy < 0 else crows - 8, 8), :]
            dst = (rough_row.at[k, half] if dx == 0 else rough_corner.at[k - 4, half])
        s = len(DIRECTIONS) + N_ROUGH * phase + k
        return pltpu.make_async_remote_copy(
            src_ref=src, dst_ref=dst, send_sem=send_sem.at[s], recv_sem=recv_sem.at[s],
            device_id=(g + dy, t + dx), device_id_type=MESH,
        )

    def start_all(make, n):
        for k, (dy, dx) in enumerate(DIRECTIONS[:n]):
            pl.when(exists(dy, dx))(lambda k=k: make(k).start())

    def wait_all_recv(make, n):
        for k, (dy, dx) in enumerate(DIRECTIONS[:n]):
            pl.when(exists(-dy, -dx))(lambda k=k: make(k).wait_recv())

    def wait_all_send(make, n):
        for k, (dy, dx) in enumerate(DIRECTIONS[:n]):
            pl.when(exists(dy, dx))(lambda k=k: make(k).wait_send())

    start_all(halo_copy, len(DIRECTIONS))

    first8, last8 = lane8 == 0, lane8 == LANES - 1

    def from_right(xs, p, end):
        turn = shift(xs[p], -1, 1)
        if p < panes - 1:
            return jnp.where(last8, shift(xs[p + 1], -1, 1), turn)
        return turn if end is None else jnp.where(last8, end, turn)

    def from_left(xs, p, end):
        return jnp.where(first8, end if p == 0 else shift(xs[p - 1], 1, 1), shift(xs[p], 1, 1))

    def line_ends(line, l, q):
        return shift(line, -(8 * l + 2 * q + 1), 1)

    first_sub, last_sub = sub8 == 0, sub8 == 7

    def row_above(u, l, p, r, x):
        return shift(jnp.where(last_sub, u[l, p, pl.ds(r - 8, 8), :], x), 1, 0)

    def row_below(u, l, p, r, x):
        return shift(jnp.where(first_sub, u[l, p, pl.ds(r + 8, 8), :], x), -1, 0)

    early, late = TOP // 8 + 2, (height - TOP) // 8 - 1

    def across_down(r, l, p):
        k = field[l, p, pl.ds(r, 8), :]
        fx = inverse(k + row_below(field, l, p, r, k))
        zx[l, p, pl.ds(r, 8), :] = fx
        return fx

    def faces(i, line):
        r = pl.multiple_of(i * 8, 8)
        here = pl.ds(r, 8)
        ks = [[field[l, p, here, :] for p in range(panes)] for l in range(layers)]
        fxs = [[across_down(r, l, p) for p in range(panes)] for l in range(layers)]
        below = [None] * panes
        for l in range(layers):
            k = ks[l]
            ends = 0.0 if line is None else line_ends(line, l, 0)
            fys = [inverse(k[p] + from_right(k, p, None)) for p in range(panes)]
            fys[-1] = jnp.where(last8, ends, fys[-1])
            for p in range(panes):
                fy = fys[p]
                zy[l, p, here, :] = fy
                fu = row_above(zx, l, p, r, fxs[l][p])
                zu[l, p, here, :] = fu
                d = fxs[l][p] + fu + fy + from_left(fys, p, ends)
                d = d + (field[2 * layers, p, here, :] if l == 0 else below[p])
                if l < layers - 1:
                    below[p] = inverse(k[p] + ks[l + 1][p])
                    zz[l, p, here, :] = below[p]
                    d = d + below[p]
                diag[l, p, here, :] = d
                if line is not None:
                    first_sweep(here, l, p, d)

    def first_sweep(here, l, p, d):
        wt = guarded_weight(d)
        weight[l, p, here, :] = wt
        ua[l, p, here, :] = wt * field[layers + l, p, here, :]

    for l in range(layers):
        for p in range(panes):
            across_down((early - 1) * 8, l, p)

    @pl.loop(early, late, unroll=unroll_of(late - early))
    def _(i):
        faces(i, None)

    col_d = iota((8, LANES), 1)
    one, none = jnp.float32(1.0), jnp.float32(0.0)
    inner = jnp.where(col_d > 0, one, none) + jnp.where(col_d < edge - 1, one, none) + 1.0
    first_row = jnp.where(sub8 > 0, one, none)
    last_row = jnp.where(sub8 < 7, one, none)
    beside = (
        jnp.abs(iota((edge, edge), 0) - iota((edge, edge), 1)) == 1
    ).astype(jnp.float32)
    body = pl.ds(8, edge)
    tall = edge // 8

    def die_diagonal(c, b):
        tops = [c * (inner + first_row) + b, c * (inner + 1.0) + b, c * (inner + last_row) + b]
        ws = [guarded_weight(d) for d in tops]

        def full(x):
            return jnp.concatenate([x[0]] + [x[1]] * (tall - 2) + [x[2]], axis=0)

        return full(tops), full(ws)

    def around(n, s):
        v = dies[n, s, body, :]
        return (
            dies[n, s, pl.ds(7, edge), :] + dies[n, s, pl.ds(9, edge), :] + two_part_dot(v, beside)
        )

    rows_in = (iota((cell, edge), 0) == iota((cell, edge), 1) // RATIO).astype(jnp.bfloat16)
    rows_in = jnp.concatenate([rows_in, rows_in], axis=1)
    message = jnp.zeros((cell, LANES), jnp.float32)
    die_load.wait()
    params = jnp.full((8, LANES), -1.0, jnp.float32)
    for s in range(slots):
        c, b = die_conduct[s], bond[s]
        live = jnp.where(place[s] >= 0, 1.0, 0.0)
        p = die_power[s]
        d, wt = die_diagonal(c, b)
        dies[0, s, body, :] = wt * p
        dies[1, s, body, :] = (1.0 - RELAX) * dies[0, s, body, :] + wt * (p + c * around(0, s))
        resid = p + c * around(1, s) - d * dies[1, s, body, :]
        cols_in = (
            iota((edge, LANES), 0) // RATIO + cell * s == iota((edge, LANES), 1)
        ).astype(jnp.float32)
        by_row = jnp.dot(
            rows_in, jnp.concatenate(halves(resid), axis=0), preferred_element_type=jnp.float32
        )
        message = message + live * two_part_dot(by_row, cols_in)
        mine = lane8 // cell == s
        value = jnp.where(
            sub8 == 0, c, jnp.where(sub8 == 1, b * area, place[s].astype(jnp.float32))
        )
        params = jnp.where(mine, value, params)
    all_dies[me, 0:cell, :] = message
    all_dies[me, cell : cell + 8, :] = params

    def gather_start(phase):
        every = (all_dies, all_fixes)[phase]
        each_peer(
            lambda where: pltpu.make_async_remote_copy(
                src_ref=every.at[me], dst_ref=every.at[me],
                send_sem=gather_send.at[phase], recv_sem=gather_recv.at[phase],
                device_id=where, device_id_type=MESH,
            ).start()
        )

    def gather_wait(phase):
        others = (all_dies, all_fixes)[phase].at[pl.ds(0, count - 1)]
        for sem in (gather_send, gather_recv):
            pltpu.make_async_copy(others, others, sem.at[phase]).wait()

    def gathered(total, first_tile):
        pick = (iota((cols, LANES), 0) // RATIO == iota((cols, LANES), 1)).astype(jnp.float32)
        folded[...] = two_part_dot(sums[...], pick)
        for tile in range(2):
            result = jnp.zeros((crows, LANES), jnp.float32)
            for q in range(per):
                f = tile * per + q
                if f < total:
                    result = result + shift(folded[pl.ds(f, crows, stride=8), :], q * ccols, 1)
            rough[first_tile + tile] = result

    gathered(layers + 1, 0)

    wait_all_recv(halo_copy, len(DIRECTIONS))
    gather_start(0)
    start_all(lambda k: rough_copy(k, 0), N_ROUGH)
    extra = [outer[j].T for j in range(3)]

    def woven(near, far, f, first):
        size = near.shape[1]
        lower = iota((8, size), 0) < HALO
        m = f // 2 * 8
        a = (far if first else near)[m : m + 8]
        b = (near if first else far)[m : m + 8]
        return (
            jnp.where(lower, a, b) if f % 2 == 0 else shift(jnp.where(lower, b, a), HALO, 0)
        )

    for f in range(n_fields):
        for side in range(2):
            at = 64 if side == 0 else 0
            strip[side, f, :, 0:rows] = woven(
                turned[at : at + depth, :], from_side[side], f, side == 0
            )
            strip[side, f, :, rows:long] = woven(
                extra[2][at : at + depth], extra[side][64 - at : 64 - at + depth], f, side == 0
            )

    def strip_total(side, l, us):
        u, fx, fy = us[l], sx[side, l], sy[side, l]
        total = strip[side, layers + l] + fx * shift(u, -1, 1) + shift(fx * u, 1, 1)
        total = total + fy * shift(u, -1, 0) + shift(fy * u, 1, 0)
        if l > 0:
            total = total + sz[side, l - 1] * us[l - 1]
        if l < layers - 1:
            total = total + sz[side, l] * us[l + 1]
        return total

    def strip_sweep(side, us):
        return [
            (1.0 - RELAX) * us[l] + sw[side, l] * strip_total(side, l, us) for l in range(layers)
        ]

    def lay_lines(k, rows_of):
        x = jnp.concatenate(
            rows_of + [jnp.zeros((LANES - 8 * layers, long), jnp.float32)], axis=0
        ).T
        lines[k, TOP : TOP + rows + 8, :] = x[0 : rows + 8]
        lines[k, TOP - 8 : TOP, :] = x[long - 8 : long]

    sub_long = iota((8, long), 0)

    def line_rows(l, fields, has_face):
        parts = []
        if has_face:
            parts = [shift(sy[1, l], -3, 0), shift(sy[0, l], -2, 0)]
        for left, right in fields:
            q = len(parts)
            parts.append(shift(right[l], q - 4, 0))
            parts.append(shift(sy[0, l] * left[l], q - 2, 0))
        x = parts[0]
        for q in range(1, len(parts)):
            x = jnp.where(sub_long == q, parts[q], x)
        return x

    smooth = []
    for side in range(2):
        below = None
        us = []
        for l in range(layers):
            k = strip[side, l]
            fx = inverse(k + shift(k, -1, 1))
            fy = inverse(k + shift(k, -1, 0))
            sx[side, l] = fx
            sy[side, l] = fy
            d = fx + shift(fx, 1, 1) + fy + shift(fy, 1, 0)
            d = d + (strip[side, 2 * layers] if l == 0 else below)
            if l < layers - 1:
                below = inverse(k + strip[side, l + 1])
                sz[side, l] = below
                d = d + below
            wt = guarded_weight(d)
            sw[side, l] = wt
            us.append(wt * strip[side, layers + l])
        new = strip_sweep(side, us)
        for l in range(layers):
            su[side, l] = new[l]
        smooth.append((us, new))
    fields = list(zip(*smooth))
    lay_lines(0, [line_rows(l, fields, True) for l in range(layers)])

    def whole(i):
        faces(i, lines[0, pl.ds(pl.multiple_of(i * 8, 8), 8), :])

    pl.loop(1, early, unroll=early - 1)(whole)

    @pl.loop(early, late, unroll=unroll_of(late - early))
    def _(i):
        here = pl.ds(pl.multiple_of(i * 8, 8), 8)
        line = lines[0, here, :]
        for l in range(layers):
            ends = line_ends(line, l, 0)
            zy[l, panes - 1, here, :] = jnp.where(last8, ends, zy[l, panes - 1, here, :])
            for p in range(panes):
                d = diag[l, p, here, :]
                if p == 0:
                    d = d + jnp.where(first8, ends, 0.0)
                if p == panes - 1:
                    d = d + jnp.where(last8, ends, 0.0)
                if p in (0, panes - 1):
                    diag[l, p, here, :] = d
                first_sweep(here, l, p, d)

    pl.loop(late, height // 8 - 1, unroll=height // 8 - 1 - late)(whole)

    def pulled(u, r, l, us, line, q):
        here = pl.ds(r, 8)
        fys = [zy[l, p, here, :] for p in range(panes)]
        flows = [fys[p] * us[l][p] for p in range(panes)]
        ends = line_ends(line, l, q)
        totals = []
        for p in range(panes):
            total = field[layers + l, p, here, :]
            total = total + zx[l, p, here, :] * row_below(u, l, p, r, us[l][p])
            total = total + zu[l, p, here, :] * row_above(u, l, p, r, us[l][p])
            total = total + fys[p] * from_right(us[l], p, ends) + from_left(flows, p, ends)
            if l > 0:
                total = total + zz[l - 1, p, here, :] * us[l - 1][p]
            if l < layers - 1:
                total = total + zz[l, p, here, :] * us[l + 1][p]
            totals.append(total)
        return totals

    def layers_at(u, r):
        return [[u[l, p, pl.ds(r, 8), :] for p in range(panes)] for l in range(layers)]

    def sweep(u, store, first, last, k, q):
        @pl.loop(first, last, unroll=unroll_of(last - first))
        def _(i):
            r = pl.multiple_of(i * 8, 8)
            us = layers_at(u, r)
            line = lines[k, pl.ds(r, 8), :]
            for l in range(layers):
                totals = pulled(u, r, l, us, line, q)
                for p in range(panes):
                    store(
                        l, p, r,
                        (1.0 - RELAX) * us[l][p] + weight[l, p, pl.ds(r, 8), :] * totals[p],
                    )

    def into(ref):
        def store(l, p, r, new):
            ref[l, p, pl.ds(r, 8), :] = new

        return store

    sweep(ua, into(ub), 1, height // 8 - 1, 0, 1)

    @pl.loop(0, crows, unroll=unroll_of(crows))
    def _(i):
        r = pl.multiple_of(i * 8 + TOP, 8)
        us = layers_at(ub, r)
        line = lines[0, pl.ds(r, 8), :]
        resids = [[] for _ in range(panes)]
        for l in range(layers):
            totals = pulled(ub, r, l, us, line, 2)
            for p in range(panes):
                resids[p].append(totals[p] - diag[l, p, pl.ds(r, 8), :] * us[l][p])
        for p in range(panes):
            sums[pl.ds(pl.multiple_of(i * 8, 8), 8), p * LANES : (p + 1) * LANES] = row_sums(
                resids[p]
            )

    gathered(layers, 2)
    lane_r = iota((crows, LANES), 1) % ccols
    rim[...] = jnp.where(
        (lane_r < HALO) | (lane_r >= ccols - HALO),
        rough[2],
        jnp.where(lane_r < 2 * HALO, shift(rough[3], HALO, 1), shift(rough[3], -HALO, 1)),
    )
    start_all(lambda k: rough_copy(k, 1), N_ROUGH)

    chigh = crows + 16

    def side_of(n, phase, tile):
        if phase == 0:
            return rough_side[n, tile]
        return shift(rim_side[n], (tile - 2) * (HALO if n else -HALO), 1)

    def join(phase):
        wait_all_recv(lambda k: rough_copy(k, phase), N_ROUGH)
        for f in range(layers + 1 if phase == 0 else layers):
            tile, q = 2 * phase + f // per, f % per
            target = f if phase == 0 else layers + 1 + f

            def joined(left, middle, right, size):
                lane = iota((size, LANES), 1)
                x = shift(middle, 8 - ccols * q, 1)
                x = jnp.where((lane >= 8) & (lane < 8 + ccols), x, 0.0)
                x = jnp.where(lane < 8, shift(left, 8 - ccols - ccols * q, 1), x)
                return jnp.where(
                    (lane >= 8 + ccols) & (lane < 16 + ccols),
                    shift(right, 8 + ccols - ccols * q, 1),
                    x,
                )

            wide[target, 8 : 8 + crows, :] = joined(
                side_of(1, phase, tile), rough[tile], side_of(0, phase, tile), crows
            )
            wide[target, 0:8, :] = joined(
                rough_corner[3, tile], rough_row[1, tile], rough_corner[2, tile], 8
            )
            wide[target, 8 + crows : chigh, :] = joined(
                rough_corner[1, tile], rough_row[0, tile], rough_corner[0, tile], 8
            )

    join(0)
    kc = [wide[l] * (0.5 / area) for l in range(layers)]
    cx = [harmonic(k, shift(k, -1, 0)) for k in kc]
    cy = [harmonic(k, shift(k, -1, 1)) for k in kc]
    cz = [harmonic(kc[l], kc[l + 1]) * area for l in range(layers - 1)]
    sums_of = []
    for l in range(layers):
        d = cx[l] + shift(cx[l], 1, 0) + cy[l] + shift(cy[l], 1, 1)
        if l == 0:
            d = d + wide[layers]
        else:
            d = d + cz[l - 1]
        sums_of.append(d + cz[l] if l < layers - 1 else d)

    gather_wait(0)
    span = tile_count * across
    parts = cell + 8
    spots = [(a, b) for a in range(-1, down + 1) for b in range(-1, across + 1)]
    wanted = []
    for a, b in spots:
        pr, pc = g * down + a, t * across + b
        inside = (pr >= 0) & (pr < grp_count * down) & (pc >= 0) & (pc < span)
        wanted.append(jnp.where(inside, pr * span + pc, -2).astype(jnp.float32))

    for lo in range(0, len(spots), across + 2):

        def add(d, acc, lo=lo):
            block = all_dies[d]
            where = all_dies[d, pl.ds(cell + 2, 1), :]
            return tuple(
                jnp.where(where == wanted[lo + j], block, a) for j, a in enumerate(acc)
            )

        acc = lax.fori_loop(
            0, count, add, tuple(jnp.zeros((parts, LANES), jnp.float32) for _ in range(across + 2)),
            unroll=unroll_of(count, 8),
        )
        lane_p = iota((parts, LANES), 1)
        line = jnp.zeros((parts, LANES), jnp.float32)
        for j in range(across + 2):
            x = acc[j]
            step = LANES // 2
            while step >= cell:
                x = x + shift(x, step, 1)
                step //= 2
            line = jnp.where(lane_p // cell == j, x, line)
        line = shift(line, 8 - cell, 1)
        a = lo // (across + 2) - 1
        if a == -1:
            first, size, off = 0, 8, cell - 8
        elif a == down:
            first, size, off = 8 + crows, 8, 0
        else:
            first, size, off = 8 + a * cell, cell, 0
        n = 2 * layers + 1
        wide[n, first : first + size, :] = line[off : off + size]
        wide[n + 1, first : first + size, :] = jnp.broadcast_to(
            line[cell : cell + 1], (size, LANES)
        )
        wide[n + 2, first : first + size, :] = jnp.broadcast_to(
            line[cell + 1 : cell + 2], (size, LANES)
        )

    top_rhs, top_c, top_b = (wide[2 * layers + 1 + j] for j in range(3))
    weights = [guarded_weight(d) for d in sums_of[:-1]] + [guarded_weight(sums_of[-1] + top_b)]
    crow = (iota((chigh, LANES), 0) + (cell - 8)) % cell
    ccol = (iota((chigh, LANES), 1) + (cell - 8)) % cell
    low_x, high_x = crow != 0, crow != cell - 1
    low_y, high_y = ccol != 0, ccol != cell - 1
    near = sum(jnp.where(m, one, none) for m in (low_x, high_x, low_y, high_y))
    top_d = top_c * near + top_b
    top_w = guarded_weight(top_d)
    join(1)
    errors = [weights[l] * wide[layers + 1 + l] for l in range(layers)]
    top = top_w * top_rhs
    def next_errors(errors, top):
        new = []
        for l in range(layers):
            e = errors[l]
            total = wide[layers + 1 + l]
            total = total + cx[l] * shift(e, -1, 0) + shift(cx[l] * e, 1, 0)
            total = total + cy[l] * shift(e, -1, 1) + shift(cy[l] * e, 1, 1)
            if l > 0:
                total = total + cz[l - 1] * errors[l - 1]
            total = total + (cz[l] * errors[l + 1] if l < layers - 1 else top_b * top)
            new.append((1.0 - RELAX) * e + weights[l] * total)
        return new

    def next_top(errors, top):
        nearby = (
            jnp.where(low_x, shift(top, 1, 0), 0.0)
            + jnp.where(high_x, shift(top, -1, 0), 0.0)
            + jnp.where(low_y, shift(top, 1, 1), 0.0)
            + jnp.where(high_y, shift(top, -1, 1), 0.0)
        )
        return top + top_w * (
            top_rhs + top_b * errors[layers - 1] + top_c * nearby - top_d * top
        )

    for _ in range(NC - 2):
        errors, top = next_errors(errors, top), next_top(errors, top)
    last_top, top = top, next_top(errors, top)

    lane_c = iota((cell, LANES), 1)
    fix = jnp.zeros((cell, LANES), jnp.float32)
    for a in range(down):
        piece = shift(top[8 + a * cell : 8 + (a + 1) * cell], a * ccols - 8, 1)
        fix = jnp.where(lane_c // ccols == a, piece, fix)
    row_f = iota((cell, LANES), 0)
    blocks = down * across
    short = all_fixes.shape[1]
    rest = cell - short
    stacks = short // rest if rest else 1

    def stored(j):
        return blocks + j // stacks, j % stacks

    if rest:
        for j in range(blocks):
            at, stack = stored(j)
            moved = shift(shift(fix, rest * stack - short, 0), cell * (at - j), 1)
            fix = jnp.where((lane_c // cell == at) & (row_f // rest == stack), moved, fix)
    all_fixes[me] = fix[:short]
    gather_start(1)
    errors = next_errors(errors, last_top)

    pick = (iota((LANES, cols), 0) == 8 + iota((LANES, cols), 1) // RATIO).astype(jnp.float32)
    fine = two_part_dot(jnp.concatenate(errors, axis=0), pick)
    for l in range(layers):
        for p in range(panes):
            spread[l, p] = fine[l * chigh : (l + 1) * chigh, p * LANES : (p + 1) * LANES]
    lane_s = iota((LANES, LANES), 1)
    wanted_lane = jnp.where(lane_s % 8 < HALO, 7, 8) + jnp.where(lane_s % 16 < 8, 0, ccols)
    wanted_lane = jnp.where(
        iota((LANES, LANES), 0) == wanted_lane, lane_s // 16, -1
    )
    sides_of = jnp.zeros((chigh, LANES), jnp.float32)
    for l in range(layers):
        sides_of = sides_of + two_part_dot(errors[l], (wanted_lane == l).astype(jnp.float32))
    along = iota((chigh, long), 1)
    coarse_row = jnp.where(along < rows + 64, along // RATIO + 8, 7)
    side_fix = two_part_dot(
        sides_of.T, (iota((chigh, long), 0) == coarse_row).astype(jnp.float32)
    )
    smooth = []
    for side in range(2):
        us = []
        for l in range(layers):
            at = 16 * l + 8 * side
            us.append(su[side, l] + side_fix[at : at + 8])
        smooth.append((us, strip_sweep(side, us)))
    fields = list(zip(*smooth))
    lay_lines(1, [line_rows(l, fields, False) for l in range(layers)])

    @pl.loop(1, height // 8 - 1)
    def _(i):
        r = pl.multiple_of(i * 8, 8)
        for l in range(layers):
            for p in range(panes):
                ub[l, p, pl.ds(r, 8), :] = ub[l, p, pl.ds(r, 8), :] + spread[l, p, pl.ds(i + 6, 1), :]

    sweep(ub, into(ua), 1, height // 8 - 1, 1, 0)

    def finish(l, p, r, new):
        out[l, pl.ds(r - TOP, 8), p * LANES : (p + 1) * LANES] = new

    sweep(ua, finish, TOP // 8, (height - TOP) // 8, 1, 1)

    gather_wait(1)
    group = lane_c // cell
    cols_out = (iota((LANES, edge), 0) == iota((LANES, edge), 1) // RATIO).astype(jnp.float32)
    for s in range(slots):
        spot = jnp.maximum(place[s], 0)
        pr, pc = spot // span, lax.rem(spot, span)
        target = (pr // down) * tile_count + pc // across
        local = lax.rem(pr, down) * across + lax.rem(pc, across)
        block = all_fixes[target]
        if rest:
            block = jnp.concatenate([block, jnp.zeros((rest, LANES), jnp.float32)], axis=0)
            tail = jnp.where(
                (group == blocks + local // stacks) & (row_f // rest == lax.rem(local, stacks)),
                block, 0.0,
            )
            tail = sum(shift(tail, short - rest * n, 0) for n in range(stacks))
            x = jnp.where(row_f < short, jnp.where(group == local, block, 0.0), tail)
        else:
            x = jnp.where(group == local, block, 0.0)
        step = LANES // 2
        while step >= cell:
            x = x + shift(x, step, 1)
            step //= 2
        c, b = die_conduct[s], bond[s]
        live = jnp.where(place[s] >= 0, 1.0, 0.0)
        p = die_power[s]
        wt = die_diagonal(c, b)[1]
        fixed[s] = live * two_part_dot(x, cols_out)
        for k in range(tall):
            dies[0, s, pl.ds(8 + 8 * k, 8), :] = (
                dies[1, s, pl.ds(8 + 8 * k, 8), :] + fixed[s, pl.ds(k, 1), :]
            )
        for n in range(NU):
            v = (1.0 - RELAX) * dies[n % 2, s, body, :] + wt * (p + c * around(n % 2, s))
            if n < NU - 1:
                dies[(n + 1) % 2, s, body, :] = v
        die_out[s] = live * v

    wait_all_send(halo_copy, len(DIRECTIONS))
    for phase in range(2):
        wait_all_send(lambda k: rough_copy(k, phase), N_ROUGH)


def per_device(grp_count, tile_count, *args):
    material, die_power = args[0], args[4]
    layers, rows, cols = material.shape
    slots, edge, _ = die_power.shape
    cell = edge // RATIO
    crows = rows // RATIO
    panes, long, height = cols // LANES, rows + LANES, rows + 2 * TOP
    count = grp_count * tile_count
    n_fields = 2 * layers + 1
    depth = -(-n_fields * HALO // 8) * 8
    vmem = pl.BlockSpec(memory_space=pltpu.VMEM)
    smem = pl.BlockSpec(memory_space=pltpu.SMEM)
    far = pl.BlockSpec(memory_space=pl.ANY)
    f32 = jnp.float32

    def scratch(*shape):
        return pltpu.VMEM(shape, f32)

    grid = (layers, panes, height, LANES)
    return pl.pallas_call(
        functools.partial(kernel, grp_count, tile_count),
        out_shape=(
            pltpu.VMEM((layers, rows, cols), f32),
            pltpu.VMEM((slots, edge, edge), f32),
        ),
        in_specs=[far, smem, far, far, far, smem, smem, smem],
        out_specs=(vmem, vmem),
        scratch_shapes=[
            pltpu.VMEM(material.shape, material.dtype),
            scratch(rows, cols),
            scratch(layers, rows, cols),
            scratch(slots, edge, edge),
            scratch(n_fields, panes, height, LANES),
            scratch(*grid),
            scratch(*grid),
            scratch(*grid),
            scratch(layers - 1, panes, height, LANES),
            scratch(*grid),
            scratch(*grid),
            scratch(*grid),
            scratch(*grid),
            scratch(rows, LANES),
            scratch(LANES, rows),
            scratch(2, depth, rows),
            scratch(3, LANES, LANES),
            scratch(2, n_fields, 8, long),
            scratch(2, layers, 8, long),
            scratch(2, layers, 8, long),
            scratch(2, layers - 1, 8, long),
            scratch(2, layers, 8, long),
            scratch(2, layers, 8, long),
            scratch(2, height, LANES),
            scratch(rows, cols),
            scratch(rows, LANES),
            scratch(4, crows, LANES),
            scratch(2, 4, crows, LANES),
            scratch(2, 4, 8, LANES),
            scratch(4, 4, 8, LANES),
            scratch(crows, LANES),
            scratch(2, crows, LANES),
            scratch(2, slots, edge + 16, edge),
            scratch(slots, cell, edge),
            scratch(count, cell + 8, LANES),
            scratch(count, cell * cell * (rows // edge) * (cols // edge) // LANES, LANES),
            scratch(n_fields + 3, crows + 16, LANES),
            scratch(layers, panes, crows + 16, LANES),
            pltpu.SemaphoreType.DMA((len(DIRECTIONS) + 2 * N_ROUGH,)),
            pltpu.SemaphoreType.DMA((len(DIRECTIONS) + 2 * N_ROUGH,)),
            pltpu.SemaphoreType.DMA((2,)),
            pltpu.SemaphoreType.DMA((2,)),
            pltpu.SemaphoreType.DMA((3, unroll_of(rows // 8, 4))),
            pltpu.SemaphoreType.DMA,
        ],
        compiler_params=pltpu.CompilerParams(
            collective_id=0, has_side_effects=True, vmem_limit_bytes=60 * 1024 * 1024
        ),
    )(*args)


def solution(mesh):
    placed = (
        P(None, "grp", "tile"),
        P(),
        P("grp", "tile"),
        P(None, "grp", "tile"),
        P(("grp", "tile"), None, None),
        P(("grp", "tile")),
        P(("grp", "tile")),
        P(("grp", "tile")),
    )
    return jax.shard_map(
        functools.partial(per_device, mesh.shape["grp"], mesh.shape["tile"]),
        mesh=mesh,
        in_specs=placed,
        out_specs=(P(None, "grp", "tile"), P(("grp", "tile"), None, None)),
        check_vma=False,
    )
```

```python
import functools
import jax
import jax.numpy as jnp
from jax import lax
from jax.experimental import pallas as pl
from jax.experimental.pallas import tpu as pltpu
from jax.sharding import PartitionSpec as P

RATIO = 8
NU = 2
NC = 4
RELAX = 0.8
HALO = 4
TOP = 16
LANES = 128
FAR = 1e30
TINY = 1e-25
UNROLL = 5
MESH = pl.DeviceIdType.MESH
DIRECTIONS = ((-1, 0), (1, 0), (0, -1), (0, 1), (-1, -1), (-1, 1), (1, -1), (1, 1), (-1, 0), (1, 0))
N_ROUGH = 8


def inverse(x):
    return pltpu.reciprocal(x, approx=True)


def harmonic(a, b):
    total = a + b
    return 2.0 * a * b * inverse(jnp.where(total > 0, total, 1.0))


def guarded_weight(d):
    return RELAX * inverse(jnp.where(d > TINY, d, 1.0))


def unroll_of(n, most=UNROLL):
    return max(u for u in range(1, most + 1) if n % u == 0)


def iota(shape, dim):
    return lax.broadcasted_iota(jnp.int32, shape, dim)


def shift(x, amount, axis):
    return pltpu.roll(x, amount % x.shape[axis], axis)


def row_sums(fields):
    shape = fields[0].shape
    row = lax.broadcasted_iota(jnp.int32, shape, 0)
    xs = list(fields) + [jnp.zeros(shape, jnp.float32)] * (8 - len(fields))

    def merge(x, y, start, run):
        first = ((row - start + 8) % 8) % (2 * run) < run
        return jnp.where(first, x, y) + shift(jnp.where(first, y, x), -run, 0)

    z = [merge(xs[j], xs[j + 4], j, 4) for j in range(4)]
    y = [merge(z[j], z[j + 2], j, 2) for j in range(2)]
    return merge(y[0], y[1], 0, 1)


def halves(a):
    high = a.astype(jnp.bfloat16)
    return high, (a - high.astype(jnp.float32)).astype(jnp.bfloat16)


def two_part_dot(a, b):
    b = b.astype(jnp.bfloat16)
    return jnp.dot(
        jnp.concatenate(halves(a), axis=1),
        jnp.concatenate([b, b], axis=0),
        preferred_element_type=jnp.float32,
    )


def die_diagonal(c, b, edge):
    col, row = iota((8, edge), 1), iota((8, edge), 0)
    inner = jnp.where(col > 0, 1.0, 0.0) + jnp.where(col < edge - 1, 1.0, 0.0) + 1.0
    ds = [
        c * (inner + jnp.where(row > 0, 1.0, 0.0)) + b,
        c * (inner + 1.0) + b,
        c * (inner + jnp.where(row < 7, 1.0, 0.0)) + b,
    ]

    def full(x):
        return jnp.concatenate([x[0]] + [x[1]] * (edge // 8 - 2) + [x[2]], axis=0)

    return full(ds), full([guarded_weight(d) for d in ds])


def around(ref):
    edge = ref.shape[1]
    beside = jnp.abs(iota((edge, edge), 0) - iota((edge, edge), 1)) == 1
    v = ref[pl.ds(8, edge), :]
    return (
        ref[pl.ds(7, edge), :]
        + ref[pl.ds(9, edge), :]
        + two_part_dot(v, beside.astype(jnp.float32))
    )


def kernel(
    grp_count,
    tile_count,
    material_far,
    table,
    heat_sink_far,
    source_far,
    die_power_far,
    die_conduct,
    bond,
    place,
    out,
    dies,
    fixed,
    die_power,
    material,
    heat_sink,
    source,
    field,
    zx,
    zu,
    zy,
    zz,
    diag,
    weight,
    ua,
    ub,
    packed,
    turned,
    from_side,
    outer,
    strip,
    sx,
    sy,
    sz,
    sw,
    su,
    lines,
    sums,
    folded,
    rough,
    rough_side,
    rough_row,
    rough_corner,
    rim,
    rim_side,
    all_dies,
    all_fixes,
    wide,
    spread,
    send_sem,
    recv_sem,
    gather_send,
    gather_recv,
    load_sem,
    die_sem,
):
    layers, rows, cols = material.shape
    slots, edge, _ = die_power.shape
    cell = edge // RATIO
    down, across = rows // edge, cols // edge
    crows, ccols = rows // RATIO, cols // RATIO
    panes = cols // LANES
    long = rows + LANES
    height = rows + 2 * TOP
    n_fields = 2 * layers + 1
    area = float(RATIO * RATIO)
    per = LANES // ccols
    count = grp_count * tile_count
    g = lax.axis_index("grp")
    t = lax.axis_index("tile")
    me = g * tile_count + t

    def each_peer(act):
        for dg in range(grp_count):
            for dt in range(tile_count):
                if dg or dt:
                    act((lax.rem(g + dg, grp_count), lax.rem(t + dt, tile_count)))

    def exists(dy, dx):
        ok = jnp.bool_(True)
        if dy:
            ok = jnp.logical_and(ok, g > 0 if dy < 0 else g < grp_count - 1)
        if dx:
            ok = jnp.logical_and(ok, t > 0 if dx < 0 else t < tile_count - 1)
        return ok

    pieces = unroll_of(rows // 8, 4)
    piece = rows // pieces

    def loads(n):
        some = pl.ds(pl.multiple_of(n * piece, 8), piece)
        pairs = (
            (material_far.at[:, some, :], material.at[:, some, :]),
            (source_far.at[:, some, :], source.at[:, some, :]),
            (heat_sink_far.at[some, :], heat_sink.at[some, :]),
        )
        return [
            pltpu.make_async_copy(a, b, load_sem.at[j, n]) for j, (a, b) in enumerate(pairs)
        ]

    die_load = pltpu.make_async_copy(die_power_far, die_power, die_sem)
    for n in range(pieces):
        for load in loads(n):
            load.start()
    die_load.start()

    for top in (0, height - TOP):
        field[0:layers, :, top : top + TOP, :] = jnp.full((layers, panes, TOP, LANES), FAR, jnp.float32)
        field[layers:n_fields, :, top : top + TOP, :] = jnp.zeros(
            (n_fields - layers, panes, TOP, LANES), jnp.float32
        )
    cut = HALO * layers
    from_side[:, 0:cut, :] = jnp.full((2, cut, rows), FAR, jnp.float32)
    from_side[:, cut:, :] = jnp.zeros((2, from_side.shape[1] - cut, rows), jnp.float32)
    outer[...] = jnp.where(iota(outer.shape, 2) % 64 < cut, FAR, 0.0)
    for n in range(2):
        for at in (0, edge + 8):
            dies[n, :, pl.ds(at, 8), :] = jnp.zeros((slots, 8, edge), jnp.float32)
    rough_side[...] = jnp.zeros_like(rough_side)
    rim_side[...] = jnp.zeros_like(rim_side)
    rough_row[...] = jnp.zeros_like(rough_row)
    rough_corner[...] = jnp.zeros_like(rough_corner)
    zx[:, :, 0:8, :] = jnp.zeros((layers, panes, 8, LANES), jnp.float32)

    barrier = pltpu.get_barrier_semaphore()

    each_peer(
        lambda where: pl.semaphore_signal(barrier, inc=1, device_id=where, device_id_type=MESH)
    )

    lane8 = iota((8, LANES), 1)
    sub8 = iota((8, LANES), 0)

    def right_lane(f):
        return HALO * f

    def left_lane(f):
        return 64 + 8 * (f // 2) + HALO * (1 - f % 2)

    kinds = table.shape[0]
    doubled = [2.0 * table[m] for m in range(kinds)]
    listed = jnp.zeros((8, LANES), jnp.float32)
    for m in range(min(kinds, 8)):
        listed = jnp.where(sub8 == m, doubled[m], listed)

    @pl.loop(0, pieces)
    def _(n):
        for load in loads(n):
            load.wait()

        @pl.loop(0, piece // 8, unroll=unroll_of(piece // 8, 4))
        def _(i):
            r = pl.multiple_of(n * piece + i * 8, 8)
            edges = jnp.zeros((8, LANES), jnp.float32)
            summed = [[] for _ in range(panes)]
            for f in range(n_fields):
                xs = []
                for p in range(panes):
                    part = slice(p * LANES, (p + 1) * LANES)
                    if f < layers:
                        kind = material[f, pl.ds(r, 8), part]
                        k2 = jnp.take_along_axis(listed, kind, axis=0)
                        summed[p].append(k2)
                        x = inverse(k2)
                    elif f < 2 * layers:
                        x = source[f - layers, pl.ds(r, 8), part]
                    else:
                        x = heat_sink[pl.ds(r, 8), part]
                        summed[p].append(x)
                    field[f, p, pl.ds(TOP + r, 8), :] = x
                    xs.append(x)
                a, b = right_lane(f), left_lane(f)
                right = shift(xs[-1], HALO + a, 1)
                left = shift(xs[0], b, 1)
                edges = jnp.where((lane8 >= a) & (lane8 < a + HALO), right, edges)
                edges = jnp.where((lane8 >= b) & (lane8 < b + HALO), left, edges)
            packed[pl.ds(r, 8), :] = edges
            for p in range(panes):
                sums[pl.ds(r, 8), p * LANES : (p + 1) * LANES] = row_sums(summed[p])

    turned[...] = packed[...].T

    pl.semaphore_wait(barrier, count - 1)

    depth = from_side.shape[1]

    def halo_copy(k):
        dy, dx = DIRECTIONS[k]
        if k < 2:
            src = field.at[:, :, pl.ds(TOP if dy < 0 else height - TOP - 8, 8), :]
            dst = field.at[:, :, pl.ds(height - TOP if dy < 0 else TOP - 8, 8), :]
        elif dy == 0:
            src = turned.at[pl.ds(0 if dx > 0 else 64, depth), :]
            dst = from_side.at[0 if dx > 0 else 1]
        else:
            src = packed.at[pl.ds(0 if dy < 0 else rows - 8, 8), :]
            which = 2 if dx == 0 else (0 if dx > 0 else 1)
            dst = outer.at[which, pl.ds(0 if dy < 0 else LANES - 8, 8), :]
        return pltpu.make_async_remote_copy(
            src_ref=src, dst_ref=dst, send_sem=send_sem.at[k], recv_sem=recv_sem.at[k],
            device_id=(g + dy, t + dx), device_id_type=MESH,
        )

    def rough_copy(k, phase):
        dy, dx = DIRECTIONS[k]
        half = pl.ds(2 * phase, 2)
        if dy == 0 and phase == 1:
            src, dst = rim, rim_side.at[k - 2]
        elif dy == 0:
            src = rough.at[half]
            dst = rough_side.at[k - 2, half]
        else:
            src = rough.at[half, pl.ds(0 if dy < 0 else crows - 8, 8), :]
            dst = (rough_row.at[k, half] if dx == 0 else rough_corner.at[k - 4, half])
        s = len(DIRECTIONS) + N_ROUGH * phase + k
        return pltpu.make_async_remote_copy(
            src_ref=src, dst_ref=dst, send_sem=send_sem.at[s], recv_sem=recv_sem.at[s],
            device_id=(g + dy, t + dx), device_id_type=MESH,
        )

    def start_all(make, n):
        for k, (dy, dx) in enumerate(DIRECTIONS[:n]):
            pl.when(exists(dy, dx))(lambda k=k: make(k).start())

    def wait_all_recv(make, n):
        for k, (dy, dx) in enumerate(DIRECTIONS[:n]):
            pl.when(exists(-dy, -dx))(lambda k=k: make(k).wait_recv())

    def wait_all_send(make, n):
        for k, (dy, dx) in enumerate(DIRECTIONS[:n]):
            pl.when(exists(dy, dx))(lambda k=k: make(k).wait_send())

    start_all(halo_copy, len(DIRECTIONS))

    first8, last8 = lane8 == 0, lane8 == LANES - 1

    def from_right(xs, p, end):
        turn = shift(xs[p], -1, 1)
        if p < panes - 1:
            return jnp.where(last8, shift(xs[p + 1], -1, 1), turn)
        return turn if end is None else jnp.where(last8, end, turn)

    def from_left(xs, p, end):
        return jnp.where(first8, end if p == 0 else shift(xs[p - 1], 1, 1), shift(xs[p], 1, 1))

    def line_ends(line, l, q):
        return shift(line, -(8 * l + 2 * q + 1), 1)

    first_sub, last_sub = sub8 == 0, sub8 == 7

    def row_above(u, l, p, r, x):
        return shift(jnp.where(last_sub, u[l, p, pl.ds(r - 8, 8), :], x), 1, 0)

    def row_below(u, l, p, r, x):
        return shift(jnp.where(first_sub, u[l, p, pl.ds(r + 8, 8), :], x), -1, 0)

    early, late = TOP // 8 + 2, (height - TOP) // 8 - 1

    def across_down(r, l, p):
        k = field[l, p, pl.ds(r, 8), :]
        fx = inverse(k + row_below(field, l, p, r, k))
        zx[l, p, pl.ds(r, 8), :] = fx
        return fx

    def faces(i, line):
        r = pl.multiple_of(i * 8, 8)
        here = pl.ds(r, 8)
        ks = [[field[l, p, here, :] for p in range(panes)] for l in range(layers)]
        fxs = [[across_down(r, l, p) for p in range(panes)] for l in range(layers)]
        below = [None] * panes
        for l in range(layers):
            k = ks[l]
            ends = 0.0 if line is None else line_ends(line, l, 0)
            fys = [inverse(k[p] + from_right(k, p, None)) for p in range(panes)]
            fys[-1] = jnp.where(last8, ends, fys[-1])
            for p in range(panes):
                fy = fys[p]
                zy[l, p, here, :] = fy
                fu = row_above(zx, l, p, r, fxs[l][p])
                zu[l, p, here, :] = fu
                d = fxs[l][p] + fu + fy + from_left(fys, p, ends)
                d = d + (field[2 * layers, p, here, :] if l == 0 else below[p])
                if l < layers - 1:
                    below[p] = inverse(k[p] + ks[l + 1][p])
                    zz[l, p, here, :] = below[p]
                    d = d + below[p]
                diag[l, p, here, :] = d
                if line is not None:
                    first_sweep(here, l, p, d)

    def first_sweep(here, l, p, d):
        wt = guarded_weight(d)
        weight[l, p, here, :] = wt
        ua[l, p, here, :] = wt * field[layers + l, p, here, :]

    for l in range(layers):
        for p in range(panes):
            across_down((early - 1) * 8, l, p)

    @pl.loop(early, late, unroll=unroll_of(late - early))
    def _(i):
        faces(i, None)

    col_d = iota((8, LANES), 1)
    one, none = jnp.float32(1.0), jnp.float32(0.0)
    body = pl.ds(8, edge)

    rows_in = (iota((cell, edge), 0) == iota((cell, edge), 1) // RATIO).astype(jnp.bfloat16)
    rows_in = jnp.concatenate([rows_in, rows_in], axis=1)
    message = jnp.zeros((cell, LANES), jnp.float32)
    die_load.wait()
    params = jnp.full((8, LANES), -1.0, jnp.float32)
    for s in range(slots):
        c, b = die_conduct[s], bond[s]
        live = jnp.where(place[s] >= 0, 1.0, 0.0)
        p = die_power[s]
        d, wt = die_diagonal(c, b, edge)
        dies[0, s, body, :] = wt * p
        dies[1, s, body, :] = (1.0 - RELAX) * dies[0, s, body, :] + wt * (p + c * around(dies.at[0, s]))
        resid = p + c * around(dies.at[1, s]) - d * dies[1, s, body, :]
        cols_in = (
            iota((edge, LANES), 0) // RATIO + cell * s == iota((edge, LANES), 1)
        ).astype(jnp.float32)
        by_row = jnp.dot(
            rows_in, jnp.concatenate(halves(resid), axis=0), preferred_element_type=jnp.float32
        )
        message = message + live * two_part_dot(by_row, cols_in)
        mine = lane8 // cell == s
        value = jnp.where(
            sub8 == 0, c, jnp.where(sub8 == 1, b * area, place[s].astype(jnp.float32))
        )
        params = jnp.where(mine, value, params)
    all_dies[me, 0:cell, :] = message
    all_dies[me, cell : cell + 8, :] = params

    def gather_start(phase):
        every = (all_dies, all_fixes)[phase]
        each_peer(
            lambda where: pltpu.make_async_remote_copy(
                src_ref=every.at[me], dst_ref=every.at[me],
                send_sem=gather_send.at[phase], recv_sem=gather_recv.at[phase],
                device_id=where, device_id_type=MESH,
            ).start()
        )

    def gather_wait(phase):
        others = (all_dies, all_fixes)[phase].at[pl.ds(0, count - 1)]
        for sem in (gather_send, gather_recv):
            pltpu.make_async_copy(others, others, sem.at[phase]).wait()

    def gathered(total, first_tile):
        pick = (iota((cols, LANES), 0) // RATIO == iota((cols, LANES), 1)).astype(jnp.float32)
        folded[...] = two_part_dot(sums[...], pick)
        for tile in range(2):
            result = jnp.zeros((crows, LANES), jnp.float32)
            for q in range(per):
                f = tile * per + q
                if f < total:
                    result = result + shift(folded[pl.ds(f, crows, stride=8), :], q * ccols, 1)
            rough[first_tile + tile] = result

    gathered(layers + 1, 0)

    wait_all_recv(halo_copy, len(DIRECTIONS))
    gather_start(0)
    start_all(lambda k: rough_copy(k, 0), N_ROUGH)
    extra = [outer[j].T for j in range(3)]

    def woven(near, far, f, first):
        size = near.shape[1]
        lower = iota((8, size), 0) < HALO
        m = f // 2 * 8
        a = (far if first else near)[m : m + 8]
        b = (near if first else far)[m : m + 8]
        return (
            jnp.where(lower, a, b) if f % 2 == 0 else shift(jnp.where(lower, b, a), HALO, 0)
        )

    for f in range(n_fields):
        for side in range(2):
            at = 64 if side == 0 else 0
            strip[side, f, :, 0:rows] = woven(
                turned[at : at + depth, :], from_side[side], f, side == 0
            )
            strip[side, f, :, rows:long] = woven(
                extra[2][at : at + depth], extra[side][64 - at : 64 - at + depth], f, side == 0
            )

    def strip_total(side, l, us):
        u, fx, fy = us[l], sx[side, l], sy[side, l]
        total = strip[side, layers + l] + fx * shift(u, -1, 1) + shift(fx * u, 1, 1)
        total = total + fy * shift(u, -1, 0) + shift(fy * u, 1, 0)
        if l > 0:
            total = total + sz[side, l - 1] * us[l - 1]
        if l < layers - 1:
            total = total + sz[side, l] * us[l + 1]
        return total

    def strip_sweep(side, us):
        return [
            (1.0 - RELAX) * us[l] + sw[side, l] * strip_total(side, l, us) for l in range(layers)
        ]

    def lay_lines(k, rows_of):
        x = jnp.concatenate(
            rows_of + [jnp.zeros((LANES - 8 * layers, long), jnp.float32)], axis=0
        ).T
        lines[k, TOP : TOP + rows + 8, :] = x[0 : rows + 8]
        lines[k, TOP - 8 : TOP, :] = x[long - 8 : long]

    sub_long = iota((8, long), 0)

    def line_rows(l, fields, has_face):
        parts = []
        if has_face:
            parts = [shift(sy[1, l], -3, 0), shift(sy[0, l], -2, 0)]
        for left, right in fields:
            q = len(parts)
            parts.append(shift(right[l], q - 4, 0))
            parts.append(shift(sy[0, l] * left[l], q - 2, 0))
        x = parts[0]
        for q in range(1, len(parts)):
            x = jnp.where(sub_long == q, parts[q], x)
        return x

    smooth = []
    for side in range(2):
        below = None
        us = []
        for l in range(layers):
            k = strip[side, l]
            fx = inverse(k + shift(k, -1, 1))
            fy = inverse(k + shift(k, -1, 0))
            sx[side, l] = fx
            sy[side, l] = fy
            d = fx + shift(fx, 1, 1) + fy + shift(fy, 1, 0)
            d = d + (strip[side, 2 * layers] if l == 0 else below)
            if l < layers - 1:
                below = inverse(k + strip[side, l + 1])
                sz[side, l] = below
                d = d + below
            wt = guarded_weight(d)
            sw[side, l] = wt
            us.append(wt * strip[side, layers + l])
        new = strip_sweep(side, us)
        for l in range(layers):
            su[side, l] = new[l]
        smooth.append((us, new))
    fields = list(zip(*smooth))
    lay_lines(0, [line_rows(l, fields, True) for l in range(layers)])

    def whole(i):
        faces(i, lines[0, pl.ds(pl.multiple_of(i * 8, 8), 8), :])

    pl.loop(1, early, unroll=early - 1)(whole)

    @pl.loop(early, late, unroll=unroll_of(late - early))
    def _(i):
        here = pl.ds(pl.multiple_of(i * 8, 8), 8)
        line = lines[0, here, :]
        for l in range(layers):
            ends = line_ends(line, l, 0)
            zy[l, panes - 1, here, :] = jnp.where(last8, ends, zy[l, panes - 1, here, :])
            for p in range(panes):
                d = diag[l, p, here, :]
                if p == 0:
                    d = d + jnp.where(first8, ends, 0.0)
                if p == panes - 1:
                    d = d + jnp.where(last8, ends, 0.0)
                if p in (0, panes - 1):
                    diag[l, p, here, :] = d
                first_sweep(here, l, p, d)

    pl.loop(late, height // 8 - 1, unroll=height // 8 - 1 - late)(whole)

    def pulled(u, r, l, us, line, q):
        here = pl.ds(r, 8)
        fys = [zy[l, p, here, :] for p in range(panes)]
        flows = [fys[p] * us[l][p] for p in range(panes)]
        ends = line_ends(line, l, q)
        totals = []
        for p in range(panes):
            total = field[layers + l, p, here, :]
            total = total + zx[l, p, here, :] * row_below(u, l, p, r, us[l][p])
            total = total + zu[l, p, here, :] * row_above(u, l, p, r, us[l][p])
            total = total + fys[p] * from_right(us[l], p, ends) + from_left(flows, p, ends)
            if l > 0:
                total = total + zz[l - 1, p, here, :] * us[l - 1][p]
            if l < layers - 1:
                total = total + zz[l, p, here, :] * us[l + 1][p]
            totals.append(total)
        return totals

    def layers_at(u, r):
        return [[u[l, p, pl.ds(r, 8), :] for p in range(panes)] for l in range(layers)]

    def sweep(u, store, first, last, k, q):
        @pl.loop(first, last, unroll=unroll_of(last - first))
        def _(i):
            r = pl.multiple_of(i * 8, 8)
            us = layers_at(u, r)
            line = lines[k, pl.ds(r, 8), :]
            for l in range(layers):
                totals = pulled(u, r, l, us, line, q)
                for p in range(panes):
                    store(
                        l, p, r,
                        (1.0 - RELAX) * us[l][p] + weight[l, p, pl.ds(r, 8), :] * totals[p],
                    )

    def into(ref):
        def store(l, p, r, new):
            ref[l, p, pl.ds(r, 8), :] = new

        return store

    sweep(ua, into(ub), 1, height // 8 - 1, 0, 1)

    @pl.loop(0, crows, unroll=unroll_of(crows))
    def _(i):
        r = pl.multiple_of(i * 8 + TOP, 8)
        us = layers_at(ub, r)
        line = lines[0, pl.ds(r, 8), :]
        resids = [[] for _ in range(panes)]
        for l in range(layers):
            totals = pulled(ub, r, l, us, line, 2)
            for p in range(panes):
                resids[p].append(totals[p] - diag[l, p, pl.ds(r, 8), :] * us[l][p])
        for p in range(panes):
            sums[pl.ds(pl.multiple_of(i * 8, 8), 8), p * LANES : (p + 1) * LANES] = row_sums(
                resids[p]
            )

    gathered(layers, 2)
    lane_r = iota((crows, LANES), 1) % ccols
    rim[...] = jnp.where(
        (lane_r < HALO) | (lane_r >= ccols - HALO),
        rough[2],
        jnp.where(lane_r < 2 * HALO, shift(rough[3], HALO, 1), shift(rough[3], -HALO, 1)),
    )
    start_all(lambda k: rough_copy(k, 1), N_ROUGH)

    chigh = crows + 16

    def side_of(n, phase, tile):
        if phase == 0:
            return rough_side[n, tile]
        return shift(rim_side[n], (tile - 2) * (HALO if n else -HALO), 1)

    def join(phase):
        wait_all_recv(lambda k: rough_copy(k, phase), N_ROUGH)
        for f in range(layers + 1 if phase == 0 else layers):
            tile, q = 2 * phase + f // per, f % per
            target = f if phase == 0 else layers + 1 + f

            def joined(left, middle, right, size):
                lane = iota((size, LANES), 1)
                x = shift(middle, 8 - ccols * q, 1)
                x = jnp.where((lane >= 8) & (lane < 8 + ccols), x, 0.0)
                x = jnp.where(lane < 8, shift(left, 8 - ccols - ccols * q, 1), x)
                return jnp.where(
                    (lane >= 8 + ccols) & (lane < 16 + ccols),
                    shift(right, 8 + ccols - ccols * q, 1),
                    x,
                )

            wide[target, 8 : 8 + crows, :] = joined(
                side_of(1, phase, tile), rough[tile], side_of(0, phase, tile), crows
            )
            wide[target, 0:8, :] = joined(
                rough_corner[3, tile], rough_row[1, tile], rough_corner[2, tile], 8
            )
            wide[target, 8 + crows : chigh, :] = joined(
                rough_corner[1, tile], rough_row[0, tile], rough_corner[0, tile], 8
            )

    join(0)
    kc = [wide[l] * (0.5 / area) for l in range(layers)]
    cx = [harmonic(k, shift(k, -1, 0)) for k in kc]
    cy = [harmonic(k, shift(k, -1, 1)) for k in kc]
    cz = [harmonic(kc[l], kc[l + 1]) * area for l in range(layers - 1)]
    sums_of = []
    for l in range(layers):
        d = cx[l] + shift(cx[l], 1, 0) + cy[l] + shift(cy[l], 1, 1)
        if l == 0:
            d = d + wide[layers]
        else:
            d = d + cz[l - 1]
        sums_of.append(d + cz[l] if l < layers - 1 else d)

    gather_wait(0)
    span = tile_count * across
    parts = cell + 8
    spots = [(a, b) for a in range(-1, down + 1) for b in range(-1, across + 1)]
    wanted = []
    for a, b in spots:
        pr, pc = g * down + a, t * across + b
        inside = (pr >= 0) & (pr < grp_count * down) & (pc >= 0) & (pc < span)
        wanted.append(jnp.where(inside, pr * span + pc, -2).astype(jnp.float32))

    for lo in range(0, len(spots), across + 2):

        def add(d, acc, lo=lo):
            block = all_dies[d]
            where = all_dies[d, pl.ds(cell + 2, 1), :]
            return tuple(
                jnp.where(where == wanted[lo + j], block, a) for j, a in enumerate(acc)
            )

        acc = lax.fori_loop(
            0, count, add, tuple(jnp.zeros((parts, LANES), jnp.float32) for _ in range(across + 2)),
            unroll=unroll_of(count, 8),
        )
        lane_p = iota((parts, LANES), 1)
        line = jnp.zeros((parts, LANES), jnp.float32)
        for j in range(across + 2):
            x = acc[j]
            step = LANES // 2
            while step >= cell:
                x = x + shift(x, step, 1)
                step //= 2
            line = jnp.where(lane_p // cell == j, x, line)
        line = shift(line, 8 - cell, 1)
        a = lo // (across + 2) - 1
        if a == -1:
            first, size, off = 0, 8, cell - 8
        elif a == down:
            first, size, off = 8 + crows, 8, 0
        else:
            first, size, off = 8 + a * cell, cell, 0
        n = 2 * layers + 1
        wide[n, first : first + size, :] = line[off : off + size]
        wide[n + 1, first : first + size, :] = jnp.broadcast_to(
            line[cell : cell + 1], (size, LANES)
        )
        wide[n + 2, first : first + size, :] = jnp.broadcast_to(
            line[cell + 1 : cell + 2], (size, LANES)
        )

    top_rhs, top_c, top_b = (wide[2 * layers + 1 + j] for j in range(3))
    weights = [guarded_weight(d) for d in sums_of[:-1]] + [guarded_weight(sums_of[-1] + top_b)]
    crow = (iota((chigh, LANES), 0) + (cell - 8)) % cell
    ccol = (iota((chigh, LANES), 1) + (cell - 8)) % cell
    low_x, high_x = crow != 0, crow != cell - 1
    low_y, high_y = ccol != 0, ccol != cell - 1
    near = sum(jnp.where(m, one, none) for m in (low_x, high_x, low_y, high_y))
    top_d = top_c * near + top_b
    top_w = guarded_weight(top_d)
    join(1)
    errors = [weights[l] * wide[layers + 1 + l] for l in range(layers)]
    top = top_w * top_rhs
    def next_errors(errors, top):
        new = []
        for l in range(layers):
            e = errors[l]
            total = wide[layers + 1 + l]
            total = total + cx[l] * shift(e, -1, 0) + shift(cx[l] * e, 1, 0)
            total = total + cy[l] * shift(e, -1, 1) + shift(cy[l] * e, 1, 1)
            if l > 0:
                total = total + cz[l - 1] * errors[l - 1]
            total = total + (cz[l] * errors[l + 1] if l < layers - 1 else top_b * top)
            new.append((1.0 - RELAX) * e + weights[l] * total)
        return new

    def next_top(errors, top):
        nearby = (
            jnp.where(low_x, shift(top, 1, 0), 0.0)
            + jnp.where(high_x, shift(top, -1, 0), 0.0)
            + jnp.where(low_y, shift(top, 1, 1), 0.0)
            + jnp.where(high_y, shift(top, -1, 1), 0.0)
        )
        return top + top_w * (
            top_rhs + top_b * errors[layers - 1] + top_c * nearby - top_d * top
        )

    for _ in range(NC - 2):
        errors, top = next_errors(errors, top), next_top(errors, top)
    last_top, top = top, next_top(errors, top)

    lane_c = iota((cell, LANES), 1)
    fix = jnp.zeros((cell, LANES), jnp.float32)
    for a in range(down):
        piece = shift(top[8 + a * cell : 8 + (a + 1) * cell], a * ccols - 8, 1)
        fix = jnp.where(lane_c // ccols == a, piece, fix)
    row_f = iota((cell, LANES), 0)
    blocks = down * across
    short = all_fixes.shape[1]
    rest = cell - short
    stacks = short // rest if rest else 1

    def stored(j):
        return blocks + j // stacks, j % stacks

    if rest:
        for j in range(blocks):
            at, stack = stored(j)
            moved = shift(shift(fix, rest * stack - short, 0), cell * (at - j), 1)
            fix = jnp.where((lane_c // cell == at) & (row_f // rest == stack), moved, fix)
    all_fixes[me] = fix[:short]
    gather_start(1)
    errors = next_errors(errors, last_top)

    pick = (iota((LANES, cols), 0) == 8 + iota((LANES, cols), 1) // RATIO).astype(jnp.float32)
    fine = two_part_dot(jnp.concatenate(errors, axis=0), pick)
    for l in range(layers):
        for p in range(panes):
            spread[l, p] = fine[l * chigh : (l + 1) * chigh, p * LANES : (p + 1) * LANES]
    lane_s = iota((LANES, LANES), 1)
    wanted_lane = jnp.where(lane_s % 8 < HALO, 7, 8) + jnp.where(lane_s % 16 < 8, 0, ccols)
    wanted_lane = jnp.where(
        iota((LANES, LANES), 0) == wanted_lane, lane_s // 16, -1
    )
    sides_of = jnp.zeros((chigh, LANES), jnp.float32)
    for l in range(layers):
        sides_of = sides_of + two_part_dot(errors[l], (wanted_lane == l).astype(jnp.float32))
    along = iota((chigh, long), 1)
    coarse_row = jnp.where(along < rows + 64, along // RATIO + 8, 7)
    side_fix = two_part_dot(
        sides_of.T, (iota((chigh, long), 0) == coarse_row).astype(jnp.float32)
    )
    smooth = []
    for side in range(2):
        us = []
        for l in range(layers):
            at = 16 * l + 8 * side
            us.append(su[side, l] + side_fix[at : at + 8])
        smooth.append((us, strip_sweep(side, us)))
    fields = list(zip(*smooth))
    lay_lines(1, [line_rows(l, fields, False) for l in range(layers)])

    @pl.loop(1, height // 8 - 1)
    def _(i):
        r = pl.multiple_of(i * 8, 8)
        for l in range(layers):
            for p in range(panes):
                ub[l, p, pl.ds(r, 8), :] = ub[l, p, pl.ds(r, 8), :] + spread[l, p, pl.ds(i + 6, 1), :]

    sweep(ub, into(ua), 1, height // 8 - 1, 1, 0)

    def finish(l, p, r, new):
        out[l, pl.ds(r - TOP, 8), p * LANES : (p + 1) * LANES] = new

    sweep(ua, finish, TOP // 8, (height - TOP) // 8, 1, 1)

    gather_wait(1)
    group = lane_c // cell
    cols_out = (iota((LANES, edge), 0) == iota((LANES, edge), 1) // RATIO).astype(jnp.float32)
    for s in range(slots):
        spot = jnp.maximum(place[s], 0)
        pr, pc = spot // span, lax.rem(spot, span)
        target = (pr // down) * tile_count + pc // across
        local = lax.rem(pr, down) * across + lax.rem(pc, across)
        block = all_fixes[target]
        if rest:
            block = jnp.concatenate([block, jnp.zeros((rest, LANES), jnp.float32)], axis=0)
            tail = jnp.where(
                (group == blocks + local // stacks) & (row_f // rest == lax.rem(local, stacks)),
                block, 0.0,
            )
            tail = sum(shift(tail, short - rest * n, 0) for n in range(stacks))
            x = jnp.where(row_f < short, jnp.where(group == local, block, 0.0), tail)
        else:
            x = jnp.where(group == local, block, 0.0)
        step = LANES // 2
        while step >= cell:
            x = x + shift(x, step, 1)
            step //= 2
        live = jnp.where(place[s] >= 0, 1.0, 0.0)
        fixed[s] = live * two_part_dot(x, cols_out)

    wait_all_send(halo_copy, len(DIRECTIONS))
    for phase in range(2):
        wait_all_send(lambda k: rough_copy(k, phase), N_ROUGH)


def per_device(grp_count, tile_count, *args):
    material, die_power = args[0], args[4]
    layers, rows, cols = material.shape
    slots, edge, _ = die_power.shape
    cell = edge // RATIO
    crows = rows // RATIO
    panes, long, height = cols // LANES, rows + LANES, rows + 2 * TOP
    count = grp_count * tile_count
    n_fields = 2 * layers + 1
    depth = -(-n_fields * HALO // 8) * 8
    vmem = pl.BlockSpec(memory_space=pltpu.VMEM)
    smem = pl.BlockSpec(memory_space=pltpu.SMEM)
    far = pl.BlockSpec(memory_space=pl.ANY)
    f32 = jnp.float32

    def scratch(*shape):
        return pltpu.VMEM(shape, f32)

    grid = (layers, panes, height, LANES)
    heats = pl.pallas_call(
        functools.partial(kernel, grp_count, tile_count),
        out_shape=(
            pltpu.VMEM((layers, rows, cols), f32),
            pltpu.VMEM((2, slots, edge + 16, edge), f32),
            pltpu.VMEM((slots, cell, edge), f32),
            pltpu.VMEM((slots, edge, edge), f32),
        ),
        in_specs=[far, smem, far, far, far, smem, smem, smem],
        out_specs=(vmem,) * 4,
        scratch_shapes=[
            pltpu.VMEM(material.shape, material.dtype),
            scratch(rows, cols),
            scratch(layers, rows, cols),
            scratch(n_fields, panes, height, LANES),
            scratch(*grid),
            scratch(*grid),
            scratch(*grid),
            scratch(layers - 1, panes, height, LANES),
            scratch(*grid),
            scratch(*grid),
            scratch(*grid),
            scratch(*grid),
            scratch(rows, LANES),
            scratch(LANES, rows),
            scratch(2, depth, rows),
            scratch(3, LANES, LANES),
            scratch(2, n_fields, 8, long),
            scratch(2, layers, 8, long),
            scratch(2, layers, 8, long),
            scratch(2, layers - 1, 8, long),
            scratch(2, layers, 8, long),
            scratch(2, layers, 8, long),
            scratch(2, height, LANES),
            scratch(rows, cols),
            scratch(rows, LANES),
            scratch(4, crows, LANES),
            scratch(2, 4, crows, LANES),
            scratch(2, 4, 8, LANES),
            scratch(4, 4, 8, LANES),
            scratch(crows, LANES),
            scratch(2, crows, LANES),
            scratch(count, cell + 8, LANES),
            scratch(count, cell * cell * (rows // edge) * (cols // edge) // LANES, LANES),
            scratch(n_fields + 3, crows + 16, LANES),
            scratch(layers, panes, crows + 16, LANES),
            pltpu.SemaphoreType.DMA((len(DIRECTIONS) + 2 * N_ROUGH,)),
            pltpu.SemaphoreType.DMA((len(DIRECTIONS) + 2 * N_ROUGH,)),
            pltpu.SemaphoreType.DMA((2,)),
            pltpu.SemaphoreType.DMA((2,)),
            pltpu.SemaphoreType.DMA((3, unroll_of(rows // 8, 4))),
            pltpu.SemaphoreType.DMA,
        ],
        compiler_params=pltpu.CompilerParams(
            collective_id=0, has_side_effects=True, vmem_limit_bytes=60 * 1024 * 1024
        ),
    )(*args)

    return finish_dies(*heats, args[5], args[6], args[7])


def finish_kernel(
    heat, dies, fixed, die_power, die_conduct, bond, place, heat_out, die_out, work, done,
    heat_sem, die_sem,
):
    slots, edge, _ = die_power.shape
    body = pl.ds(8, edge)
    move = pltpu.make_async_copy(heat, heat_out, heat_sem)
    move.start()
    moves = []
    for at in (0, edge + 8):
        work[:, :, pl.ds(at, 8), :] = jnp.zeros((2, slots, 8, edge), jnp.float32)
    for s in range(slots):
        c, b = die_conduct[s], bond[s]
        live = jnp.where(place[s] >= 0, 1.0, 0.0)
        p = die_power[s]
        wt = die_diagonal(c, b, edge)[1]
        for k in range(edge // 8):
            work[0, s, pl.ds(8 + 8 * k, 8), :] = (
                dies[1, s, pl.ds(8 + 8 * k, 8), :] + fixed[s, pl.ds(k, 1), :]
            )
        for n in range(NU):
            now = work.at[n % 2, s]
            v = (1.0 - RELAX) * now[body, :] + wt * (p + c * around(now))
            if n < NU - 1:
                work[(n + 1) % 2, s, body, :] = v
        done[s] = live * v
    for s in range(slots):
        moves.append(pltpu.make_async_copy(done.at[s], die_out.at[s], die_sem.at[s]))
        moves[-1].start()
    for each in moves:
        each.wait()
    move.wait()


def finish_dies(heat, dies, fixed, die_power, *params):
    slots, edge, _ = die_power.shape
    near = [pltpu.with_memory_space_constraint(x, pltpu.VMEM) for x in (dies, fixed, die_power)]
    anywhere = pl.BlockSpec(memory_space=pl.ANY)
    vmem = pl.BlockSpec(memory_space=pltpu.VMEM)
    smem = pl.BlockSpec(memory_space=pltpu.SMEM)
    return pl.pallas_call(
        finish_kernel,
        out_shape=(
            jax.ShapeDtypeStruct(heat.shape, heat.dtype),
            jax.ShapeDtypeStruct(die_power.shape, die_power.dtype),
        ),
        in_specs=[anywhere] + [vmem] * 3 + [smem] * 3,
        out_specs=(anywhere, anywhere),
        scratch_shapes=[
            pltpu.VMEM(dies.shape, jnp.float32),
            pltpu.VMEM(die_power.shape, jnp.float32),
            pltpu.SemaphoreType.DMA,
            pltpu.SemaphoreType.DMA((slots,)),
        ],
        compiler_params=pltpu.CompilerParams(vmem_limit_bytes=8 * 1024 * 1024),
    )(heat, *near, *params)


def solution(mesh):
    placed = (
        P(None, "grp", "tile"),
        P(),
        P("grp", "tile"),
        P(None, "grp", "tile"),
        P(("grp", "tile"), None, None),
        P(("grp", "tile")),
        P(("grp", "tile")),
        P(("grp", "tile")),
    )
    return jax.shard_map(
        functools.partial(per_device, mesh.shape["grp"], mesh.shape["tile"]),
        mesh=mesh,
        in_specs=placed,
        out_specs=(P(None, "grp", "tile"), P(("grp", "tile"), None, None)),
        check_vma=False,
    )
```

```python
import functools
import jax
import jax.numpy as jnp
from jax import lax
from jax.experimental import pallas as pl
from jax.experimental.pallas import tpu as pltpu
from jax.sharding import PartitionSpec as P

RATIO = 8
NU = 2
NC = 4
RELAX = 0.8
HALO = 4
TOP = 16
LANES = 128
FAR = 1e30
TINY = 1e-25
UNROLL = 6
MESH = pl.DeviceIdType.MESH
DIRECTIONS = ((-1, 0), (1, 0), (0, -1), (0, 1), (-1, -1), (-1, 1), (1, -1), (1, 1), (-1, 0), (1, 0))
N_ROUGH = 8


def inverse(x):
    return pltpu.reciprocal(x, approx=True)


def harmonic(a, b):
    total = a + b
    return 2.0 * a * b * inverse(jnp.where(total > 0, total, 1.0))


def guarded_weight(d):
    return RELAX * inverse(jnp.where(d > TINY, d, 1.0))


def unroll_of(n, most=UNROLL):
    return max(u for u in range(1, most + 1) if n % u == 0)


def iota(shape, dim):
    return lax.broadcasted_iota(jnp.int32, shape, dim)


def shift(x, amount, axis):
    return pltpu.roll(x, amount % x.shape[axis], axis)


def row_sums(fields):
    shape = fields[0].shape
    row = lax.broadcasted_iota(jnp.int32, shape, 0)
    xs = list(fields) + [jnp.zeros(shape, jnp.float32)] * (8 - len(fields))

    def merge(x, y, start, run):
        first = ((row - start + 8) % 8) % (2 * run) < run
        return jnp.where(first, x, y) + shift(jnp.where(first, y, x), -run, 0)

    z = [merge(xs[j], xs[j + 4], j, 4) for j in range(4)]
    y = [merge(z[j], z[j + 2], j, 2) for j in range(2)]
    return merge(y[0], y[1], 0, 1)


def halves(a):
    high = a.astype(jnp.bfloat16)
    return high, (a - high.astype(jnp.float32)).astype(jnp.bfloat16)


def two_part_dot(a, b):
    b = b.astype(jnp.bfloat16)
    return jnp.dot(
        jnp.concatenate(halves(a), axis=1),
        jnp.concatenate([b, b], axis=0),
        preferred_element_type=jnp.float32,
    )


def die_diagonal(c, b, edge):
    col, row = iota((8, edge), 1), iota((8, edge), 0)
    inner = jnp.where(col > 0, 1.0, 0.0) + jnp.where(col < edge - 1, 1.0, 0.0) + 1.0
    ds = [
        c * (inner + jnp.where(row > 0, 1.0, 0.0)) + b,
        c * (inner + 1.0) + b,
        c * (inner + jnp.where(row < 7, 1.0, 0.0)) + b,
    ]

    def full(x):
        return jnp.concatenate([x[0]] + [x[1]] * (edge // 8 - 2) + [x[2]], axis=0)

    return full(ds), full([guarded_weight(d) for d in ds])


def around(ref):
    edge = ref.shape[1]
    beside = jnp.abs(iota((edge, edge), 0) - iota((edge, edge), 1)) == 1
    v = ref[pl.ds(8, edge), :]
    return (
        ref[pl.ds(7, edge), :]
        + ref[pl.ds(9, edge), :]
        + two_part_dot(v, beside.astype(jnp.float32))
    )


def kernel(
    grp_count,
    tile_count,
    material_far,
    table,
    heat_sink_far,
    source_far,
    die_power_far,
    die_conduct,
    bond,
    place,
    out,
    dies,
    fixed,
    die_power,
    material,
    heat_sink,
    source,
    field,
    zx,
    zu,
    zy,
    zz,
    diag,
    weight,
    ua,
    ub,
    packed,
    turned,
    from_side,
    outer,
    strip,
    sx,
    sy,
    sz,
    sw,
    su,
    lines,
    sums,
    folded,
    rough,
    rough_side,
    rough_row,
    rough_corner,
    rim,
    rim_side,
    all_dies,
    all_fixes,
    wide,
    spread,
    send_sem,
    recv_sem,
    gather_send,
    gather_recv,
    load_sem,
    die_sem,
):
    layers, rows, cols = material.shape
    slots, edge, _ = die_power.shape
    cell = edge // RATIO
    down, across = rows // edge, cols // edge
    crows, ccols = rows // RATIO, cols // RATIO
    panes = cols // LANES
    long = rows + LANES
    height = rows + 2 * TOP
    n_fields = 2 * layers + 1
    area = float(RATIO * RATIO)
    per = LANES // ccols
    count = grp_count * tile_count
    g = lax.axis_index("grp")
    t = lax.axis_index("tile")
    me = g * tile_count + t

    def each_peer(act):
        for dg in range(grp_count):
            for dt in range(tile_count):
                if dg or dt:
                    act((lax.rem(g + dg, grp_count), lax.rem(t + dt, tile_count)))

    def exists(dy, dx):
        ok = jnp.bool_(True)
        if dy:
            ok = jnp.logical_and(ok, g > 0 if dy < 0 else g < grp_count - 1)
        if dx:
            ok = jnp.logical_and(ok, t > 0 if dx < 0 else t < tile_count - 1)
        return ok

    pieces = unroll_of(rows // 8, 4)
    piece = rows // pieces

    def loads(n):
        some = pl.ds(pl.multiple_of(n * piece, 8), piece)
        pairs = (
            (material_far.at[:, some, :], material.at[:, some, :]),
            (source_far.at[:, some, :], source.at[:, some, :]),
            (heat_sink_far.at[some, :], heat_sink.at[some, :]),
        )
        return [
            pltpu.make_async_copy(a, b, load_sem.at[j, n]) for j, (a, b) in enumerate(pairs)
        ]

    die_load = pltpu.make_async_copy(die_power_far, die_power, die_sem)
    for n in range(pieces):
        for load in loads(n):
            load.start()
    die_load.start()

    for top in (0, height - TOP):
        field[0:layers, :, top : top + TOP, :] = jnp.full((layers, panes, TOP, LANES), FAR, jnp.float32)
        field[layers:n_fields, :, top : top + TOP, :] = jnp.zeros(
            (n_fields - layers, panes, TOP, LANES), jnp.float32
        )
    cut = HALO * layers
    from_side[:, 0:cut, :] = jnp.full((2, cut, rows), FAR, jnp.float32)
    from_side[:, cut:, :] = jnp.zeros((2, from_side.shape[1] - cut, rows), jnp.float32)
    outer[...] = jnp.where(iota(outer.shape, 2) % 64 < cut, FAR, 0.0)
    for n in range(2):
        for at in (0, edge + 8):
            dies[n, :, pl.ds(at, 8), :] = jnp.zeros((slots, 8, edge), jnp.float32)
    rough_side[...] = jnp.zeros_like(rough_side)
    rim_side[...] = jnp.zeros_like(rim_side)
    rough_row[...] = jnp.zeros_like(rough_row)
    rough_corner[...] = jnp.zeros_like(rough_corner)
    zx[:, :, 0:8, :] = jnp.zeros((layers, panes, 8, LANES), jnp.float32)

    barrier = pltpu.get_barrier_semaphore()

    each_peer(
        lambda where: pl.semaphore_signal(barrier, inc=1, device_id=where, device_id_type=MESH)
    )

    lane8 = iota((8, LANES), 1)
    sub8 = iota((8, LANES), 0)

    kinds = table.shape[0]
    doubled = [2.0 * table[m] for m in range(kinds)]
    listed = jnp.zeros((8, LANES), jnp.float32)
    for m in range(min(kinds, 8)):
        listed = jnp.where(sub8 == m, doubled[m], listed)

    @pl.loop(0, pieces)
    def _(n):
        for load in loads(n):
            load.wait()

        @pl.loop(0, piece // 8, unroll=unroll_of(piece // 8, 4))
        def _(i):
            r = pl.multiple_of(n * piece + i * 8, 8)
            kept = [jnp.zeros((8, LANES), jnp.float32)] * 2
            summed = [[] for _ in range(panes)]
            for f in range(n_fields):
                xs = []
                for p in range(panes):
                    part = slice(p * LANES, (p + 1) * LANES)
                    if f < layers:
                        kind = material[f, pl.ds(r, 8), part]
                        k2 = jnp.take_along_axis(listed, kind, axis=0)
                        summed[p].append(k2)
                        x = inverse(k2)
                    elif f < 2 * layers:
                        x = source[f - layers, pl.ds(r, 8), part]
                    else:
                        x = heat_sink[pl.ds(r, 8), part]
                        summed[p].append(x)
                    field[f, p, pl.ds(TOP + r, 8), :] = x
                    xs.append(x)
                at = 8 * (f // 2) + HALO * (f % 2)
                both = shift(jnp.where(lane8 < HALO, xs[0], xs[-1]), HALO + at, 1)
                kept[f % 2] = jnp.where((lane8 >= at) & (lane8 < at + 8), both, kept[f % 2])
            even, odd = kept
            edges = jnp.where(
                lane8 < 64,
                jnp.where(lane8 % 8 < HALO, even, odd),
                jnp.where(lane8 % 8 < HALO, shift(odd, 56, 1), shift(even, 64, 1)),
            )
            packed[pl.ds(r, 8), :] = edges
            for p in range(panes):
                sums[pl.ds(r, 8), p * LANES : (p + 1) * LANES] = row_sums(summed[p])

    turned[...] = packed[...].T

    pl.semaphore_wait(barrier, count - 1)

    depth = from_side.shape[1]

    def halo_copy(k):
        dy, dx = DIRECTIONS[k]
        if k < 2:
            src = field.at[:, :, pl.ds(TOP if dy < 0 else height - TOP - 8, 8), :]
            dst = field.at[:, :, pl.ds(height - TOP if dy < 0 else TOP - 8, 8), :]
        elif dy == 0:
            src = turned.at[pl.ds(0 if dx > 0 else 64, depth), :]
            dst = from_side.at[0 if dx > 0 else 1]
        else:
            src = packed.at[pl.ds(0 if dy < 0 else rows - 8, 8), :]
            which = 2 if dx == 0 else (0 if dx > 0 else 1)
            dst = outer.at[which, pl.ds(0 if dy < 0 else LANES - 8, 8), :]
        return pltpu.make_async_remote_copy(
            src_ref=src, dst_ref=dst, send_sem=send_sem.at[k], recv_sem=recv_sem.at[k],
            device_id=(g + dy, t + dx), device_id_type=MESH,
        )

    def rough_copy(k, phase):
        dy, dx = DIRECTIONS[k]
        half = pl.ds(2 * phase, 2)
        if dy == 0 and phase == 1:
            src, dst = rim, rim_side.at[k - 2]
        elif dy == 0:
            src = rough.at[half]
            dst = rough_side.at[k - 2, half]
        else:
            src = rough.at[half, pl.ds(0 if dy < 0 else crows - 8, 8), :]
            dst = (rough_row.at[k, half] if dx == 0 else rough_corner.at[k - 4, half])
        s = len(DIRECTIONS) + N_ROUGH * phase + k
        return pltpu.make_async_remote_copy(
            src_ref=src, dst_ref=dst, send_sem=send_sem.at[s], recv_sem=recv_sem.at[s],
            device_id=(g + dy, t + dx), device_id_type=MESH,
        )

    def start_all(make, n):
        for k, (dy, dx) in enumerate(DIRECTIONS[:n]):
            pl.when(exists(dy, dx))(lambda k=k: make(k).start())

    def wait_all_recv(make, n):
        for k, (dy, dx) in enumerate(DIRECTIONS[:n]):
            pl.when(exists(-dy, -dx))(lambda k=k: make(k).wait_recv())

    def wait_all_send(make, n):
        for k, (dy, dx) in enumerate(DIRECTIONS[:n]):
            pl.when(exists(dy, dx))(lambda k=k: make(k).wait_send())

    start_all(halo_copy, len(DIRECTIONS))

    first8, last8 = lane8 == 0, lane8 == LANES - 1

    def from_right(xs, p, end):
        turn = shift(xs[p], -1, 1)
        if p < panes - 1:
            return jnp.where(last8, shift(xs[p + 1], -1, 1), turn)
        return turn if end is None else jnp.where(last8, end, turn)

    def from_left(xs, p, end):
        return jnp.where(first8, end if p == 0 else shift(xs[p - 1], 1, 1), shift(xs[p], 1, 1))

    def line_ends(line, l, q):
        return shift(line, -(8 * l + 2 * q + 1), 1)

    first_sub, last_sub = sub8 == 0, sub8 == 7

    def row_above(u, l, p, r, x):
        return shift(jnp.where(last_sub, u[l, p, pl.ds(r - 8, 8), :], x), 1, 0)

    def row_below(u, l, p, r, x):
        return shift(jnp.where(first_sub, u[l, p, pl.ds(r + 8, 8), :], x), -1, 0)

    early, late = TOP // 8 + 2, (height - TOP) // 8 - 1

    def across_down(r, l, p):
        k = field[l, p, pl.ds(r, 8), :]
        fx = inverse(k + row_below(field, l, p, r, k))
        zx[l, p, pl.ds(r, 8), :] = fx
        return fx

    def faces(i, line):
        r = pl.multiple_of(i * 8, 8)
        here = pl.ds(r, 8)
        ks = [[field[l, p, here, :] for p in range(panes)] for l in range(layers)]
        fxs = [[across_down(r, l, p) for p in range(panes)] for l in range(layers)]
        below = [None] * panes
        for l in range(layers):
            k = ks[l]
            ends = 0.0 if line is None else line_ends(line, l, 0)
            fys = [inverse(k[p] + from_right(k, p, None)) for p in range(panes)]
            fys[-1] = jnp.where(last8, ends, fys[-1])
            for p in range(panes):
                fy = fys[p]
                zy[l, p, here, :] = fy
                fu = row_above(zx, l, p, r, fxs[l][p])
                zu[l, p, here, :] = fu
                d = fxs[l][p] + fu + fy + from_left(fys, p, ends)
                d = d + (field[2 * layers, p, here, :] if l == 0 else below[p])
                if l < layers - 1:
                    below[p] = inverse(k[p] + ks[l + 1][p])
                    zz[l, p, here, :] = below[p]
                    d = d + below[p]
                diag[l, p, here, :] = d
                if line is not None:
                    first_sweep(here, l, p, d)

    def first_sweep(here, l, p, d):
        wt = guarded_weight(d)
        weight[l, p, here, :] = wt
        ua[l, p, here, :] = wt * field[layers + l, p, here, :]

    for l in range(layers):
        for p in range(panes):
            across_down((early - 1) * 8, l, p)

    @pl.loop(early, late, unroll=unroll_of(late - early))
    def _(i):
        faces(i, None)

    col_d = iota((8, LANES), 1)
    one, none = jnp.float32(1.0), jnp.float32(0.0)
    body = pl.ds(8, edge)

    rows_in = (iota((cell, edge), 0) == iota((cell, edge), 1) // RATIO).astype(jnp.bfloat16)
    rows_in = jnp.concatenate([rows_in, rows_in], axis=1)
    message = jnp.zeros((cell, LANES), jnp.float32)
    die_load.wait()
    params = jnp.full((8, LANES), -1.0, jnp.float32)
    for s in range(slots):
        c, b = die_conduct[s], bond[s]
        live = jnp.where(place[s] >= 0, 1.0, 0.0)
        p = die_power[s]
        d, wt = die_diagonal(c, b, edge)
        dies[0, s, body, :] = wt * p
        dies[1, s, body, :] = (1.0 - RELAX) * dies[0, s, body, :] + wt * (p + c * around(dies.at[0, s]))
        resid = p + c * around(dies.at[1, s]) - d * dies[1, s, body, :]
        cols_in = (
            iota((edge, LANES), 0) // RATIO + cell * s == iota((edge, LANES), 1)
        ).astype(jnp.float32)
        by_row = jnp.dot(
            rows_in, jnp.concatenate(halves(resid), axis=0), preferred_element_type=jnp.float32
        )
        message = message + live * two_part_dot(by_row, cols_in)
        mine = lane8 // cell == s
        value = jnp.where(
            sub8 == 0, c, jnp.where(sub8 == 1, b * area, place[s].astype(jnp.float32))
        )
        params = jnp.where(mine, value, params)
    all_dies[me, 0:cell, :] = message
    all_dies[me, cell : cell + 8, :] = params

    def gather_start(phase):
        every = (all_dies, all_fixes)[phase]
        each_peer(
            lambda where: pltpu.make_async_remote_copy(
                src_ref=every.at[me], dst_ref=every.at[me],
                send_sem=gather_send.at[phase], recv_sem=gather_recv.at[phase],
                device_id=where, device_id_type=MESH,
            ).start()
        )

    def gather_wait(phase):
        others = (all_dies, all_fixes)[phase].at[pl.ds(0, count - 1)]
        for sem in (gather_send, gather_recv):
            pltpu.make_async_copy(others, others, sem.at[phase]).wait()

    def gathered(total, first_tile):
        pick = (iota((cols, LANES), 0) // RATIO == iota((cols, LANES), 1)).astype(jnp.float32)
        folded[...] = two_part_dot(sums[...], pick)
        for tile in range(2):
            result = jnp.zeros((crows, LANES), jnp.float32)
            for q in range(per):
                f = tile * per + q
                if f < total:
                    result = result + shift(folded[pl.ds(f, crows, stride=8), :], q * ccols, 1)
            rough[first_tile + tile] = result

    gathered(layers + 1, 0)

    wait_all_recv(halo_copy, len(DIRECTIONS))
    gather_start(0)
    start_all(lambda k: rough_copy(k, 0), N_ROUGH)
    extra = [outer[j].T for j in range(3)]

    def woven(near, far, f, first):
        size = near.shape[1]
        lower = iota((8, size), 0) < HALO
        m = f // 2 * 8
        a = (far if first else near)[m : m + 8]
        b = (near if first else far)[m : m + 8]
        return (
            jnp.where(lower, a, b) if f % 2 == 0 else shift(jnp.where(lower, b, a), HALO, 0)
        )

    for f in range(n_fields):
        for side in range(2):
            at = 64 if side == 0 else 0
            strip[side, f, :, 0:rows] = woven(
                turned[at : at + depth, :], from_side[side], f, side == 0
            )
            strip[side, f, :, rows:long] = woven(
                extra[2][at : at + depth], extra[side][64 - at : 64 - at + depth], f, side == 0
            )

    def strip_total(side, l, us):
        u, fx, fy = us[l], sx[side, l], sy[side, l]
        total = strip[side, layers + l] + fx * shift(u, -1, 1) + shift(fx * u, 1, 1)
        total = total + fy * shift(u, -1, 0) + shift(fy * u, 1, 0)
        if l > 0:
            total = total + sz[side, l - 1] * us[l - 1]
        if l < layers - 1:
            total = total + sz[side, l] * us[l + 1]
        return total

    def strip_sweep(side, us):
        return [
            (1.0 - RELAX) * us[l] + sw[side, l] * strip_total(side, l, us) for l in range(layers)
        ]

    def lay_lines(k, rows_of):
        x = jnp.concatenate(
            rows_of + [jnp.zeros((LANES - 8 * layers, long), jnp.float32)], axis=0
        ).T
        lines[k, TOP : TOP + rows + 8, :] = x[0 : rows + 8]
        lines[k, TOP - 8 : TOP, :] = x[long - 8 : long]

    sub_long = iota((8, long), 0)

    def line_rows(l, fields, has_face):
        parts = []
        if has_face:
            parts = [shift(sy[1, l], -3, 0), shift(sy[0, l], -2, 0)]
        for left, right in fields:
            q = len(parts)
            parts.append(shift(right[l], q - 4, 0))
            parts.append(shift(sy[0, l] * left[l], q - 2, 0))
        x = parts[0]
        for q in range(1, len(parts)):
            x = jnp.where(sub_long == q, parts[q], x)
        return x

    smooth = []
    for side in range(2):
        below = None
        us = []
        for l in range(layers):
            k = strip[side, l]
            fx = inverse(k + shift(k, -1, 1))
            fy = inverse(k + shift(k, -1, 0))
            sx[side, l] = fx
            sy[side, l] = fy
            d = fx + shift(fx, 1, 1) + fy + shift(fy, 1, 0)
            d = d + (strip[side, 2 * layers] if l == 0 else below)
            if l < layers - 1:
                below = inverse(k + strip[side, l + 1])
                sz[side, l] = below
                d = d + below
            wt = guarded_weight(d)
            sw[side, l] = wt
            us.append(wt * strip[side, layers + l])
        new = strip_sweep(side, us)
        for l in range(layers):
            su[side, l] = new[l]
        smooth.append((us, new))
    fields = list(zip(*smooth))
    lay_lines(0, [line_rows(l, fields, True) for l in range(layers)])

    def whole(i):
        faces(i, lines[0, pl.ds(pl.multiple_of(i * 8, 8), 8), :])

    pl.loop(1, early, unroll=early - 1)(whole)

    @pl.loop(early, late, unroll=unroll_of(late - early))
    def _(i):
        here = pl.ds(pl.multiple_of(i * 8, 8), 8)
        line = lines[0, here, :]
        for l in range(layers):
            ends = line_ends(line, l, 0)
            zy[l, panes - 1, here, :] = jnp.where(last8, ends, zy[l, panes - 1, here, :])
            for p in range(panes):
                d = diag[l, p, here, :]
                if p == 0:
                    d = d + jnp.where(first8, ends, 0.0)
                if p == panes - 1:
                    d = d + jnp.where(last8, ends, 0.0)
                if p in (0, panes - 1):
                    diag[l, p, here, :] = d
                first_sweep(here, l, p, d)

    pl.loop(late, height // 8 - 1, unroll=height // 8 - 1 - late)(whole)

    def pulled(u, r, l, us, line, q):
        here = pl.ds(r, 8)
        fys = [zy[l, p, here, :] for p in range(panes)]
        flows = [fys[p] * us[l][p] for p in range(panes)]
        ends = line_ends(line, l, q)
        totals = []
        for p in range(panes):
            total = field[layers + l, p, here, :]
            total = total + zx[l, p, here, :] * row_below(u, l, p, r, us[l][p])
            total = total + zu[l, p, here, :] * row_above(u, l, p, r, us[l][p])
            total = total + fys[p] * from_right(us[l], p, ends) + from_left(flows, p, ends)
            if l > 0:
                total = total + zz[l - 1, p, here, :] * us[l - 1][p]
            if l < layers - 1:
                total = total + zz[l, p, here, :] * us[l + 1][p]
            totals.append(total)
        return totals

    def layers_at(u, r):
        return [[u[l, p, pl.ds(r, 8), :] for p in range(panes)] for l in range(layers)]

    def sweep(u, store, first, last, k, q):
        @pl.loop(first, last, unroll=unroll_of(last - first))
        def _(i):
            r = pl.multiple_of(i * 8, 8)
            us = layers_at(u, r)
            line = lines[k, pl.ds(r, 8), :]
            for l in range(layers):
                totals = pulled(u, r, l, us, line, q)
                for p in range(panes):
                    store(
                        l, p, r,
                        (1.0 - RELAX) * us[l][p] + weight[l, p, pl.ds(r, 8), :] * totals[p],
                    )

    def into(ref):
        def store(l, p, r, new):
            ref[l, p, pl.ds(r, 8), :] = new

        return store

    sweep(ua, into(ub), 1, height // 8 - 1, 0, 1)

    @pl.loop(0, crows, unroll=unroll_of(crows))
    def _(i):
        r = pl.multiple_of(i * 8 + TOP, 8)
        us = layers_at(ub, r)
        line = lines[0, pl.ds(r, 8), :]
        resids = [[] for _ in range(panes)]
        for l in range(layers):
            totals = pulled(ub, r, l, us, line, 2)
            for p in range(panes):
                resids[p].append(totals[p] - diag[l, p, pl.ds(r, 8), :] * us[l][p])
        for p in range(panes):
            sums[pl.ds(pl.multiple_of(i * 8, 8), 8), p * LANES : (p + 1) * LANES] = row_sums(
                resids[p]
            )

    gathered(layers, 2)
    lane_r = iota((crows, LANES), 1) % ccols
    rim[...] = jnp.where(
        (lane_r < HALO) | (lane_r >= ccols - HALO),
        rough[2],
        jnp.where(lane_r < 2 * HALO, shift(rough[3], HALO, 1), shift(rough[3], -HALO, 1)),
    )
    start_all(lambda k: rough_copy(k, 1), N_ROUGH)

    chigh = crows + 16

    def side_of(n, phase, tile):
        if phase == 0:
            return rough_side[n, tile]
        return shift(rim_side[n], (tile - 2) * (HALO if n else -HALO), 1)

    def join(phase):
        wait_all_recv(lambda k: rough_copy(k, phase), N_ROUGH)
        for f in range(layers + 1 if phase == 0 else layers):
            tile, q = 2 * phase + f // per, f % per
            target = f if phase == 0 else layers + 1 + f

            def joined(left, middle, right, size):
                lane = iota((size, LANES), 1)
                x = shift(middle, 8 - ccols * q, 1)
                x = jnp.where((lane >= 8) & (lane < 8 + ccols), x, 0.0)
                x = jnp.where(lane < 8, shift(left, 8 - ccols - ccols * q, 1), x)
                return jnp.where(
                    (lane >= 8 + ccols) & (lane < 16 + ccols),
                    shift(right, 8 + ccols - ccols * q, 1),
                    x,
                )

            wide[target, 8 : 8 + crows, :] = joined(
                side_of(1, phase, tile), rough[tile], side_of(0, phase, tile), crows
            )
            wide[target, 0:8, :] = joined(
                rough_corner[3, tile], rough_row[1, tile], rough_corner[2, tile], 8
            )
            wide[target, 8 + crows : chigh, :] = joined(
                rough_corner[1, tile], rough_row[0, tile], rough_corner[0, tile], 8
            )

    join(0)
    kc = [wide[l] * (0.5 / area) for l in range(layers)]
    cx = [harmonic(k, shift(k, -1, 0)) for k in kc]
    cy = [harmonic(k, shift(k, -1, 1)) for k in kc]
    cz = [harmonic(kc[l], kc[l + 1]) * area for l in range(layers - 1)]
    sums_of = []
    for l in range(layers):
        d = cx[l] + shift(cx[l], 1, 0) + cy[l] + shift(cy[l], 1, 1)
        if l == 0:
            d = d + wide[layers]
        else:
            d = d + cz[l - 1]
        sums_of.append(d + cz[l] if l < layers - 1 else d)

    gather_wait(0)
    span = tile_count * across
    parts = cell + 8
    spots = [(a, b) for a in range(-1, down + 1) for b in range(-1, across + 1)]
    wanted = []
    for a, b in spots:
        pr, pc = g * down + a, t * across + b
        inside = (pr >= 0) & (pr < grp_count * down) & (pc >= 0) & (pc < span)
        wanted.append(jnp.where(inside, pr * span + pc, -2).astype(jnp.float32))

    for lo in range(0, len(spots), across + 2):

        def add(d, acc, lo=lo):
            block = all_dies[d]
            where = all_dies[d, pl.ds(cell + 2, 1), :]
            return tuple(
                jnp.where(where == wanted[lo + j], block, a) for j, a in enumerate(acc)
            )

        acc = lax.fori_loop(
            0, count, add, tuple(jnp.zeros((parts, LANES), jnp.float32) for _ in range(across + 2)),
            unroll=unroll_of(count, 8),
        )
        lane_p = iota((parts, LANES), 1)
        line = jnp.zeros((parts, LANES), jnp.float32)
        for j in range(across + 2):
            x = acc[j]
            step = LANES // 2
            while step >= cell:
                x = x + shift(x, step, 1)
                step //= 2
            line = jnp.where(lane_p // cell == j, x, line)
        line = shift(line, 8 - cell, 1)
        a = lo // (across + 2) - 1
        if a == -1:
            first, size, off = 0, 8, cell - 8
        elif a == down:
            first, size, off = 8 + crows, 8, 0
        else:
            first, size, off = 8 + a * cell, cell, 0
        n = 2 * layers + 1
        wide[n, first : first + size, :] = line[off : off + size]
        wide[n + 1, first : first + size, :] = jnp.broadcast_to(
            line[cell : cell + 1], (size, LANES)
        )
        wide[n + 2, first : first + size, :] = jnp.broadcast_to(
            line[cell + 1 : cell + 2], (size, LANES)
        )

    top_rhs, top_c, top_b = (wide[2 * layers + 1 + j] for j in range(3))
    weights = [guarded_weight(d) for d in sums_of[:-1]] + [guarded_weight(sums_of[-1] + top_b)]
    crow = (iota((chigh, LANES), 0) + (cell - 8)) % cell
    ccol = (iota((chigh, LANES), 1) + (cell - 8)) % cell
    low_x, high_x = crow != 0, crow != cell - 1
    low_y, high_y = ccol != 0, ccol != cell - 1
    near = sum(jnp.where(m, one, none) for m in (low_x, high_x, low_y, high_y))
    top_d = top_c * near + top_b
    top_w = guarded_weight(top_d)
    join(1)
    errors = [weights[l] * wide[layers + 1 + l] for l in range(layers)]
    top = top_w * top_rhs
    def next_errors(errors, top):
        new = []
        for l in range(layers):
            e = errors[l]
            total = wide[layers + 1 + l]
            total = total + cx[l] * shift(e, -1, 0) + shift(cx[l] * e, 1, 0)
            total = total + cy[l] * shift(e, -1, 1) + shift(cy[l] * e, 1, 1)
            if l > 0:
                total = total + cz[l - 1] * errors[l - 1]
            total = total + (cz[l] * errors[l + 1] if l < layers - 1 else top_b * top)
            new.append((1.0 - RELAX) * e + weights[l] * total)
        return new

    def next_top(errors, top):
        nearby = (
            jnp.where(low_x, shift(top, 1, 0), 0.0)
            + jnp.where(high_x, shift(top, -1, 0), 0.0)
            + jnp.where(low_y, shift(top, 1, 1), 0.0)
            + jnp.where(high_y, shift(top, -1, 1), 0.0)
        )
        return top + top_w * (
            top_rhs + top_b * errors[layers - 1] + top_c * nearby - top_d * top
        )

    for _ in range(NC - 2):
        errors, top = next_errors(errors, top), next_top(errors, top)
    last_top, top = top, next_top(errors, top)

    lane_c = iota((cell, LANES), 1)
    fix = jnp.zeros((cell, LANES), jnp.float32)
    for a in range(down):
        piece = shift(top[8 + a * cell : 8 + (a + 1) * cell], a * ccols - 8, 1)
        fix = jnp.where(lane_c // ccols == a, piece, fix)
    row_f = iota((cell, LANES), 0)
    blocks = down * across
    short = all_fixes.shape[1]
    rest = cell - short
    stacks = short // rest if rest else 1

    def stored(j):
        return blocks + j // stacks, j % stacks

    if rest:
        for j in range(blocks):
            at, stack = stored(j)
            moved = shift(shift(fix, rest * stack - short, 0), cell * (at - j), 1)
            fix = jnp.where((lane_c // cell == at) & (row_f // rest == stack), moved, fix)
    all_fixes[me] = fix[:short]
    gather_start(1)
    errors = next_errors(errors, last_top)

    pick = (iota((LANES, cols), 0) == 8 + iota((LANES, cols), 1) // RATIO).astype(jnp.float32)
    fine = two_part_dot(jnp.concatenate(errors, axis=0), pick)
    for l in range(layers):
        for p in range(panes):
            spread[l, p] = fine[l * chigh : (l + 1) * chigh, p * LANES : (p + 1) * LANES]
    lane_s = iota((LANES, LANES), 1)
    wanted_lane = jnp.where(lane_s % 8 < HALO, 7, 8) + jnp.where(lane_s % 16 < 8, 0, ccols)
    wanted_lane = jnp.where(
        iota((LANES, LANES), 0) == wanted_lane, lane_s // 16, -1
    )
    sides_of = jnp.zeros((chigh, LANES), jnp.float32)
    for l in range(layers):
        sides_of = sides_of + two_part_dot(errors[l], (wanted_lane == l).astype(jnp.float32))
    along = iota((chigh, long), 1)
    coarse_row = jnp.where(along < rows + 64, along // RATIO + 8, 7)
    side_fix = two_part_dot(
        sides_of.T, (iota((chigh, long), 0) == coarse_row).astype(jnp.float32)
    )
    smooth = []
    for side in range(2):
        us = []
        for l in range(layers):
            at = 16 * l + 8 * side
            us.append(su[side, l] + side_fix[at : at + 8])
        smooth.append((us, strip_sweep(side, us)))
    fields = list(zip(*smooth))
    lay_lines(1, [line_rows(l, fields, False) for l in range(layers)])

    @pl.loop(1, height // 8 - 1)
    def _(i):
        r = pl.multiple_of(i * 8, 8)
        for l in range(layers):
            for p in range(panes):
                ub[l, p, pl.ds(r, 8), :] = ub[l, p, pl.ds(r, 8), :] + spread[l, p, pl.ds(i + 6, 1), :]

    sweep(ub, into(ua), 1, height // 8 - 1, 1, 0)

    def finish(l, p, r, new):
        out[l, pl.ds(r - TOP, 8), p * LANES : (p + 1) * LANES] = new

    sweep(ua, finish, TOP // 8, (height - TOP) // 8, 1, 1)

    wait_all_send(halo_copy, len(DIRECTIONS))
    for phase in range(2):
        wait_all_send(lambda k: rough_copy(k, phase), N_ROUGH)
    homes = []
    for s in range(slots):
        spot = jnp.maximum(place[s], 0)
        pr, pc = spot // span, lax.rem(spot, span)
        target = (pr // down) * tile_count + pc // across
        local = lax.rem(pr, down) * across + lax.rem(pc, across)
        homes.append((target, local))
    gather_wait(1)
    group = lane_c // cell
    cols_out = (iota((LANES, edge), 0) == iota((LANES, edge), 1) // RATIO).astype(jnp.float32)
    for s in range(slots):
        target, local = homes[s]
        block = all_fixes[target]
        if rest:
            block = jnp.concatenate([block, jnp.zeros((rest, LANES), jnp.float32)], axis=0)
            tail = jnp.where(
                (group == blocks + local // stacks) & (row_f // rest == lax.rem(local, stacks)),
                block, 0.0,
            )
            tail = sum(shift(tail, short - rest * n, 0) for n in range(stacks))
            x = jnp.where(row_f < short, jnp.where(group == local, block, 0.0), tail)
        else:
            x = jnp.where(group == local, block, 0.0)
        step = LANES // 2
        while step >= cell:
            x = x + shift(x, step, 1)
            step //= 2
        live = jnp.where(place[s] >= 0, 1.0, 0.0)
        fixed[s] = live * two_part_dot(x, cols_out)


def per_device(grp_count, tile_count, *args):
    material, die_power = args[0], args[4]
    layers, rows, cols = material.shape
    slots, edge, _ = die_power.shape
    cell = edge // RATIO
    crows = rows // RATIO
    panes, long, height = cols // LANES, rows + LANES, rows + 2 * TOP
    count = grp_count * tile_count
    n_fields = 2 * layers + 1
    depth = -(-n_fields * HALO // 8) * 8
    vmem = pl.BlockSpec(memory_space=pltpu.VMEM)
    smem = pl.BlockSpec(memory_space=pltpu.SMEM)
    far = pl.BlockSpec(memory_space=pl.ANY)
    f32 = jnp.float32

    def scratch(*shape):
        return pltpu.VMEM(shape, f32)

    grid = (layers, panes, height, LANES)
    heats = pl.pallas_call(
        functools.partial(kernel, grp_count, tile_count),
        out_shape=(
            pltpu.VMEM((layers, rows, cols), f32),
            pltpu.VMEM((2, slots, edge + 16, edge), f32),
            pltpu.VMEM((slots, cell, edge), f32),
            pltpu.VMEM((slots, edge, edge), f32),
        ),
        in_specs=[far, smem, far, far, far, smem, smem, smem],
        out_specs=(vmem,) * 4,
        scratch_shapes=[
            pltpu.VMEM(material.shape, material.dtype),
            scratch(rows, cols),
            scratch(layers, rows, cols),
            scratch(n_fields, panes, height, LANES),
            scratch(*grid),
            scratch(*grid),
            scratch(*grid),
            scratch(layers - 1, panes, height, LANES),
            scratch(*grid),
            scratch(*grid),
            scratch(*grid),
            scratch(*grid),
            scratch(rows, LANES),
            scratch(LANES, rows),
            scratch(2, depth, rows),
            scratch(3, LANES, LANES),
            scratch(2, n_fields, 8, long),
            scratch(2, layers, 8, long),
            scratch(2, layers, 8, long),
            scratch(2, layers - 1, 8, long),
            scratch(2, layers, 8, long),
            scratch(2, layers, 8, long),
            scratch(2, height, LANES),
            scratch(rows, cols),
            scratch(rows, LANES),
            scratch(4, crows, LANES),
            scratch(2, 4, crows, LANES),
            scratch(2, 4, 8, LANES),
            scratch(4, 4, 8, LANES),
            scratch(crows, LANES),
            scratch(2, crows, LANES),
            scratch(count, cell + 8, LANES),
            scratch(count, cell * cell * (rows // edge) * (cols // edge) // LANES, LANES),
            scratch(n_fields + 3, crows + 16, LANES),
            scratch(layers, panes, crows + 16, LANES),
            pltpu.SemaphoreType.DMA((len(DIRECTIONS) + 2 * N_ROUGH,)),
            pltpu.SemaphoreType.DMA((len(DIRECTIONS) + 2 * N_ROUGH,)),
            pltpu.SemaphoreType.DMA((2,)),
            pltpu.SemaphoreType.DMA((2,)),
            pltpu.SemaphoreType.DMA((3, unroll_of(rows // 8, 4))),
            pltpu.SemaphoreType.DMA,
        ],
        compiler_params=pltpu.CompilerParams(
            collective_id=0, has_side_effects=True, vmem_limit_bytes=60 * 1024 * 1024
        ),
    )(*args)

    return finish_dies(*heats, args[5], args[6], args[7])


def finish_kernel(
    heat, dies, fixed, die_power, die_conduct, bond, place, heat_out, die_out, work, done,
    heat_sem, die_sem,
):
    slots, edge, _ = die_power.shape
    body = pl.ds(8, edge)
    move = pltpu.make_async_copy(heat, heat_out, heat_sem)
    move.start()
    moves = []
    for at in (0, edge + 8):
        work[:, :, pl.ds(at, 8), :] = jnp.zeros((2, slots, 8, edge), jnp.float32)
    for s in range(slots):
        c, b = die_conduct[s], bond[s]
        live = jnp.where(place[s] >= 0, 1.0, 0.0)
        p = die_power[s]
        wt = die_diagonal(c, b, edge)[1]
        for k in range(edge // 8):
            work[0, s, pl.ds(8 + 8 * k, 8), :] = (
                dies[1, s, pl.ds(8 + 8 * k, 8), :] + fixed[s, pl.ds(k, 1), :]
            )
        for n in range(NU):
            now = work.at[n % 2, s]
            v = (1.0 - RELAX) * now[body, :] + wt * (p + c * around(now))
            if n < NU - 1:
                work[(n + 1) % 2, s, body, :] = v
        done[s] = live * v
    for s in range(slots):
        moves.append(pltpu.make_async_copy(done.at[s], die_out.at[s], die_sem.at[s]))
        moves[-1].start()
    for each in moves:
        each.wait()
    move.wait()


def finish_dies(heat, dies, fixed, die_power, *params):
    slots, edge, _ = die_power.shape
    near = [pltpu.with_memory_space_constraint(x, pltpu.VMEM) for x in (dies, fixed, die_power)]
    anywhere = pl.BlockSpec(memory_space=pl.ANY)
    vmem = pl.BlockSpec(memory_space=pltpu.VMEM)
    smem = pl.BlockSpec(memory_space=pltpu.SMEM)
    return pl.pallas_call(
        finish_kernel,
        out_shape=(
            jax.ShapeDtypeStruct(heat.shape, heat.dtype),
            jax.ShapeDtypeStruct(die_power.shape, die_power.dtype),
        ),
        in_specs=[anywhere] + [vmem] * 3 + [smem] * 3,
        out_specs=(anywhere, anywhere),
        scratch_shapes=[
            pltpu.VMEM(dies.shape, jnp.float32),
            pltpu.VMEM(die_power.shape, jnp.float32),
            pltpu.SemaphoreType.DMA,
            pltpu.SemaphoreType.DMA((slots,)),
        ],
        compiler_params=pltpu.CompilerParams(vmem_limit_bytes=8 * 1024 * 1024),
    )(heat, *near, *params)


def solution(mesh):
    placed = (
        P(None, "grp", "tile"),
        P(),
        P("grp", "tile"),
        P(None, "grp", "tile"),
        P(("grp", "tile"), None, None),
        P(("grp", "tile")),
        P(("grp", "tile")),
        P(("grp", "tile")),
    )
    return jax.shard_map(
        functools.partial(per_device, mesh.shape["grp"], mesh.shape["tile"]),
        mesh=mesh,
        in_specs=placed,
        out_specs=(P(None, "grp", "tile"), P(("grp", "tile"), None, None)),
        check_vma=False,
    )
```

```python
import functools
import jax
import jax.numpy as jnp
from jax import lax
from jax.experimental import pallas as pl
from jax.experimental.pallas import tpu as pltpu
from jax.sharding import PartitionSpec as P

RATIO = 8
NU = 2
NC = 4
RELAX = 0.8
HALO = 4
TOP = 16
LANES = 128
FAR = 1e30
TINY = 1e-25
UNROLL = 6
MESH = pl.DeviceIdType.MESH
DIRECTIONS = ((-1, 0), (1, 0), (0, -1), (0, 1), (-1, -1), (-1, 1), (1, -1), (1, 1), (-1, 0), (1, 0))
N_ROUGH = 8


def inverse(x):
    return pltpu.reciprocal(x, approx=True)


def harmonic(a, b):
    total = a + b
    return 2.0 * a * b * inverse(jnp.where(total > 0, total, 1.0))


def guarded_weight(d):
    return RELAX * inverse(jnp.where(d > TINY, d, 1.0))


def unroll_of(n, most=UNROLL):
    return max(u for u in range(1, most + 1) if n % u == 0)


def iota(shape, dim):
    return lax.broadcasted_iota(jnp.int32, shape, dim)


def shift(x, amount, axis):
    return pltpu.roll(x, amount % x.shape[axis], axis)


def row_sums(fields):
    shape = fields[0].shape
    row = lax.broadcasted_iota(jnp.int32, shape, 0)
    xs = list(fields) + [jnp.zeros(shape, jnp.float32)] * (8 - len(fields))

    def merge(x, y, start, run):
        first = ((row - start + 8) % 8) % (2 * run) < run
        return jnp.where(first, x, y) + shift(jnp.where(first, y, x), -run, 0)

    z = [merge(xs[j], xs[j + 4], j, 4) for j in range(4)]
    y = [merge(z[j], z[j + 2], j, 2) for j in range(2)]
    return merge(y[0], y[1], 0, 1)


def halves(a):
    high = a.astype(jnp.bfloat16)
    return high, (a - high.astype(jnp.float32)).astype(jnp.bfloat16)


def two_part_dot(a, b):
    b = b.astype(jnp.bfloat16)
    return jnp.dot(
        jnp.concatenate(halves(a), axis=1),
        jnp.concatenate([b, b], axis=0),
        preferred_element_type=jnp.float32,
    )


def die_diagonal(c, b, edge):
    col, row = iota((8, edge), 1), iota((8, edge), 0)
    inner = jnp.where(col > 0, 1.0, 0.0) + jnp.where(col < edge - 1, 1.0, 0.0) + 1.0
    ds = [
        c * (inner + jnp.where(row > 0, 1.0, 0.0)) + b,
        c * (inner + 1.0) + b,
        c * (inner + jnp.where(row < 7, 1.0, 0.0)) + b,
    ]

    def full(x):
        return jnp.concatenate([x[0]] + [x[1]] * (edge // 8 - 2) + [x[2]], axis=0)

    return full(ds), full([guarded_weight(d) for d in ds])


def around(ref):
    edge = ref.shape[1]
    beside = jnp.abs(iota((edge, edge), 0) - iota((edge, edge), 1)) == 1
    v = ref[pl.ds(8, edge), :]
    return (
        ref[pl.ds(7, edge), :]
        + ref[pl.ds(9, edge), :]
        + two_part_dot(v, beside.astype(jnp.float32))
    )


def kernel(
    grp_count,
    tile_count,
    material_far,
    table,
    heat_sink_far,
    source_far,
    die_power_far,
    die_conduct,
    bond,
    place,
    out,
    dies,
    fixed,
    die_power,
    material,
    heat_sink,
    source,
    field,
    zx,
    zu,
    zy,
    zz,
    diag,
    weight,
    ua,
    ub,
    packed,
    turned,
    from_side,
    outer,
    strip,
    sx,
    sy,
    sz,
    sw,
    su,
    lines,
    sums,
    folded,
    rough,
    rough_side,
    rough_row,
    rough_corner,
    rim,
    rim_side,
    all_dies,
    all_fixes,
    wide,
    spread,
    send_sem,
    recv_sem,
    gather_send,
    gather_recv,
    load_sem,
    die_sem,
):
    layers, rows, cols = material.shape
    slots, edge, _ = die_power.shape
    cell = edge // RATIO
    down, across = rows // edge, cols // edge
    crows, ccols = rows // RATIO, cols // RATIO
    panes = cols // LANES
    long = rows + LANES
    height = rows + 2 * TOP
    n_fields = 2 * layers + 1
    area = float(RATIO * RATIO)
    per = LANES // ccols
    count = grp_count * tile_count
    g = lax.axis_index("grp")
    t = lax.axis_index("tile")
    me = g * tile_count + t

    def each_peer(act):
        for dg in range(grp_count):
            for dt in range(tile_count):
                if dg or dt:
                    act((lax.rem(g + dg, grp_count), lax.rem(t + dt, tile_count)))

    def exists(dy, dx):
        ok = jnp.bool_(True)
        if dy:
            ok = jnp.logical_and(ok, g > 0 if dy < 0 else g < grp_count - 1)
        if dx:
            ok = jnp.logical_and(ok, t > 0 if dx < 0 else t < tile_count - 1)
        return ok

    pieces = unroll_of(rows // 8, 4)
    piece = rows // pieces

    def loads(n):
        some = pl.ds(pl.multiple_of(n * piece, 8), piece)
        pairs = (
            (material_far.at[:, some, :], material.at[:, some, :]),
            (source_far.at[:, some, :], source.at[:, some, :]),
            (heat_sink_far.at[some, :], heat_sink.at[some, :]),
        )
        return [
            pltpu.make_async_copy(a, b, load_sem.at[j, n]) for j, (a, b) in enumerate(pairs)
        ]

    die_load = pltpu.make_async_copy(die_power_far, die_power, die_sem)
    for n in range(pieces):
        for load in loads(n):
            load.start()
    die_load.start()

    for top in (0, height - TOP):
        field[0:layers, :, top : top + TOP, :] = jnp.full((layers, panes, TOP, LANES), FAR, jnp.float32)
        field[layers:n_fields, :, top : top + TOP, :] = jnp.zeros(
            (n_fields - layers, panes, TOP, LANES), jnp.float32
        )
    cut = HALO * layers
    from_side[:, 0:cut, :] = jnp.full((2, cut, rows), FAR, jnp.float32)
    from_side[:, cut:, :] = jnp.zeros((2, from_side.shape[1] - cut, rows), jnp.float32)
    outer[...] = jnp.where(iota(outer.shape, 2) % 64 < cut, FAR, 0.0)
    for n in range(2):
        for at in (0, edge + 8):
            dies[n, :, pl.ds(at, 8), :] = jnp.zeros((slots, 8, edge), jnp.float32)
    rough_side[...] = jnp.zeros_like(rough_side)
    rim_side[...] = jnp.zeros_like(rim_side)
    rough_row[...] = jnp.zeros_like(rough_row)
    rough_corner[...] = jnp.zeros_like(rough_corner)
    zx[:, :, 0:8, :] = jnp.zeros((layers, panes, 8, LANES), jnp.float32)

    barrier = pltpu.get_barrier_semaphore()

    each_peer(
        lambda where: pl.semaphore_signal(barrier, inc=1, device_id=where, device_id_type=MESH)
    )

    lane8 = iota((8, LANES), 1)
    sub8 = iota((8, LANES), 0)

    kinds = table.shape[0]
    doubled = [2.0 * table[m] for m in range(kinds)]
    listed = jnp.zeros((8, LANES), jnp.float32)
    for m in range(min(kinds, 8)):
        listed = jnp.where(sub8 == m, doubled[m], listed)

    @pl.loop(0, pieces)
    def _(n):
        for load in loads(n):
            load.wait()

        @pl.loop(0, piece // 8, unroll=unroll_of(piece // 8, 4))
        def _(i):
            r = pl.multiple_of(n * piece + i * 8, 8)
            kept = [jnp.zeros((8, LANES), jnp.float32)] * 2
            summed = [[] for _ in range(panes)]
            for f in range(n_fields):
                xs = []
                for p in range(panes):
                    part = slice(p * LANES, (p + 1) * LANES)
                    if f < layers:
                        kind = material[f, pl.ds(r, 8), part]
                        k2 = jnp.take_along_axis(listed, kind, axis=0)
                        summed[p].append(k2)
                        x = inverse(k2)
                    elif f < 2 * layers:
                        x = source[f - layers, pl.ds(r, 8), part]
                    else:
                        x = heat_sink[pl.ds(r, 8), part]
                        summed[p].append(x)
                    field[f, p, pl.ds(TOP + r, 8), :] = x
                    xs.append(x)
                at = 8 * (f // 2) + HALO * (f % 2)
                both = shift(jnp.where(lane8 < HALO, xs[0], xs[-1]), HALO + at, 1)
                kept[f % 2] = jnp.where((lane8 >= at) & (lane8 < at + 8), both, kept[f % 2])
            even, odd = kept
            edges = jnp.where(
                lane8 < 64,
                jnp.where(lane8 % 8 < HALO, even, odd),
                jnp.where(lane8 % 8 < HALO, shift(odd, 56, 1), shift(even, 64, 1)),
            )
            packed[pl.ds(r, 8), :] = edges
            for p in range(panes):
                sums[pl.ds(r, 8), p * LANES : (p + 1) * LANES] = row_sums(summed[p])

    turned[...] = packed[...].T

    pl.semaphore_wait(barrier, count - 1)

    depth = from_side.shape[1]

    def halo_copy(k):
        dy, dx = DIRECTIONS[k]
        if k < 2:
            src = field.at[:, :, pl.ds(TOP if dy < 0 else height - TOP - 8, 8), :]
            dst = field.at[:, :, pl.ds(height - TOP if dy < 0 else TOP - 8, 8), :]
        elif dy == 0:
            src = turned.at[pl.ds(0 if dx > 0 else 64, depth), :]
            dst = from_side.at[0 if dx > 0 else 1]
        else:
            src = packed.at[pl.ds(0 if dy < 0 else rows - 8, 8), :]
            which = 2 if dx == 0 else (0 if dx > 0 else 1)
            dst = outer.at[which, pl.ds(0 if dy < 0 else LANES - 8, 8), :]
        return pltpu.make_async_remote_copy(
            src_ref=src, dst_ref=dst, send_sem=send_sem.at[k], recv_sem=recv_sem.at[k],
            device_id=(g + dy, t + dx), device_id_type=MESH,
        )

    def rough_copy(k, phase):
        dy, dx = DIRECTIONS[k]
        half = pl.ds(2 * phase, 2)
        if dy == 0 and phase == 1:
            src, dst = rim, rim_side.at[k - 2]
        elif dy == 0:
            src = rough.at[half]
            dst = rough_side.at[k - 2, half]
        else:
            src = rough.at[half, pl.ds(0 if dy < 0 else crows - 8, 8), :]
            dst = (rough_row.at[k, half] if dx == 0 else rough_corner.at[k - 4, half])
        s = len(DIRECTIONS) + N_ROUGH * phase + k
        return pltpu.make_async_remote_copy(
            src_ref=src, dst_ref=dst, send_sem=send_sem.at[s], recv_sem=recv_sem.at[s],
            device_id=(g + dy, t + dx), device_id_type=MESH,
        )

    def start_all(make, n):
        for k, (dy, dx) in enumerate(DIRECTIONS[:n]):
            pl.when(exists(dy, dx))(lambda k=k: make(k).start())

    def wait_all_recv(make, n):
        for k, (dy, dx) in enumerate(DIRECTIONS[:n]):
            pl.when(exists(-dy, -dx))(lambda k=k: make(k).wait_recv())

    def wait_all_send(make, n):
        for k, (dy, dx) in enumerate(DIRECTIONS[:n]):
            pl.when(exists(dy, dx))(lambda k=k: make(k).wait_send())

    start_all(halo_copy, len(DIRECTIONS))

    first8, last8 = lane8 == 0, lane8 == LANES - 1

    def from_right(xs, p, end):
        turn = shift(xs[p], -1, 1)
        if p < panes - 1:
            return jnp.where(last8, shift(xs[p + 1], -1, 1), turn)
        return turn if end is None else jnp.where(last8, end, turn)

    def from_left(xs, p, end):
        return jnp.where(first8, end if p == 0 else shift(xs[p - 1], 1, 1), shift(xs[p], 1, 1))

    def line_ends(line, l, q):
        return shift(line, -(8 * l + 2 * q + 1), 1)

    first_sub, last_sub = sub8 == 0, sub8 == 7

    def row_above(u, l, p, r, x):
        return shift(jnp.where(last_sub, u[l, p, pl.ds(r - 8, 8), :], x), 1, 0)

    def row_below(u, l, p, r, x):
        return shift(jnp.where(first_sub, u[l, p, pl.ds(r + 8, 8), :], x), -1, 0)

    early, late = TOP // 8 + 2, (height - TOP) // 8 - 1

    def across_down(r, l, p):
        k = field[l, p, pl.ds(r, 8), :]
        fx = inverse(k + row_below(field, l, p, r, k))
        zx[l, p, pl.ds(r, 8), :] = fx
        return fx

    def faces(i, line):
        r = pl.multiple_of(i * 8, 8)
        here = pl.ds(r, 8)
        ks = [[field[l, p, here, :] for p in range(panes)] for l in range(layers)]
        fxs = [[across_down(r, l, p) for p in range(panes)] for l in range(layers)]
        below = [None] * panes
        for l in range(layers):
            k = ks[l]
            ends = 0.0 if line is None else line_ends(line, l, 0)
            fys = [inverse(k[p] + from_right(k, p, None)) for p in range(panes)]
            fys[-1] = jnp.where(last8, ends, fys[-1])
            for p in range(panes):
                fy = fys[p]
                zy[l, p, here, :] = fy
                fu = row_above(zx, l, p, r, fxs[l][p])
                zu[l, p, here, :] = fu
                d = fxs[l][p] + fu + fy + from_left(fys, p, ends)
                d = d + (field[2 * layers, p, here, :] if l == 0 else below[p])
                if l < layers - 1:
                    below[p] = inverse(k[p] + ks[l + 1][p])
                    zz[l, p, here, :] = below[p]
                    d = d + below[p]
                diag[l, p, here, :] = d
                if line is not None:
                    first_sweep(here, l, p, d)

    def first_sweep(here, l, p, d):
        wt = guarded_weight(d)
        weight[l, p, here, :] = wt
        ua[l, p, here, :] = wt * field[layers + l, p, here, :]

    for l in range(layers):
        for p in range(panes):
            across_down((early - 1) * 8, l, p)

    @pl.loop(early, late, unroll=unroll_of(late - early))
    def _(i):
        faces(i, None)

    col_d = iota((8, LANES), 1)
    one, none = jnp.float32(1.0), jnp.float32(0.0)
    body = pl.ds(8, edge)

    rows_in = (iota((cell, edge), 0) == iota((cell, edge), 1) // RATIO).astype(jnp.bfloat16)
    rows_in = jnp.concatenate([rows_in, rows_in], axis=1)
    message = jnp.zeros((cell, LANES), jnp.float32)
    die_load.wait()
    params = jnp.full((8, LANES), -1.0, jnp.float32)
    for s in range(slots):
        c, b = die_conduct[s], bond[s]
        live = jnp.where(place[s] >= 0, 1.0, 0.0)
        p = die_power[s]
        d, wt = die_diagonal(c, b, edge)
        dies[0, s, body, :] = wt * p
        dies[1, s, body, :] = (1.0 - RELAX) * dies[0, s, body, :] + wt * (p + c * around(dies.at[0, s]))
        resid = p + c * around(dies.at[1, s]) - d * dies[1, s, body, :]
        cols_in = (
            iota((edge, LANES), 0) // RATIO + cell * s == iota((edge, LANES), 1)
        ).astype(jnp.float32)
        by_row = jnp.dot(
            rows_in, jnp.concatenate(halves(resid), axis=0), preferred_element_type=jnp.float32
        )
        message = message + live * two_part_dot(by_row, cols_in)
        mine = lane8 // cell == s
        value = jnp.where(
            sub8 == 0, c, jnp.where(sub8 == 1, b * area, place[s].astype(jnp.float32))
        )
        params = jnp.where(mine, value, params)
    all_dies[me, 0:cell, :] = message
    all_dies[me, cell : cell + 8, :] = params

    def gather_start(phase):
        every = (all_dies, all_fixes)[phase]
        each_peer(
            lambda where: pltpu.make_async_remote_copy(
                src_ref=every.at[me], dst_ref=every.at[me],
                send_sem=gather_send.at[phase], recv_sem=gather_recv.at[phase],
                device_id=where, device_id_type=MESH,
            ).start()
        )

    def gather_wait(phase):
        others = (all_dies, all_fixes)[phase].at[pl.ds(0, count - 1)]
        for sem in (gather_send, gather_recv):
            pltpu.make_async_copy(others, others, sem.at[phase]).wait()

    def gathered(total, first_tile):
        pick = (iota((cols, LANES), 0) // RATIO == iota((cols, LANES), 1)).astype(jnp.float32)
        folded[...] = two_part_dot(sums[...], pick)
        for tile in range(2):
            result = jnp.zeros((crows, LANES), jnp.float32)
            for q in range(per):
                f = tile * per + q
                if f < total:
                    result = result + shift(folded[pl.ds(f, crows, stride=8), :], q * ccols, 1)
            rough[first_tile + tile] = result

    gathered(layers + 1, 0)

    wait_all_recv(halo_copy, len(DIRECTIONS))
    gather_start(0)
    start_all(lambda k: rough_copy(k, 0), N_ROUGH)
    extra = [outer[j].T for j in range(3)]

    def woven(near, far, f, first):
        size = near.shape[1]
        lower = iota((8, size), 0) < HALO
        m = f // 2 * 8
        a = (far if first else near)[m : m + 8]
        b = (near if first else far)[m : m + 8]
        return (
            jnp.where(lower, a, b) if f % 2 == 0 else shift(jnp.where(lower, b, a), HALO, 0)
        )

    for f in range(n_fields):
        for side in range(2):
            at = 64 if side == 0 else 0
            strip[side, f, :, 0:rows] = woven(
                turned[at : at + depth, :], from_side[side], f, side == 0
            )
            strip[side, f, :, rows:long] = woven(
                extra[2][at : at + depth], extra[side][64 - at : 64 - at + depth], f, side == 0
            )

    def strip_total(side, l, us):
        u, fx, fy = us[l], sx[side, l], sy[side, l]
        total = strip[side, layers + l] + fx * shift(u, -1, 1) + shift(fx * u, 1, 1)
        total = total + fy * shift(u, -1, 0) + shift(fy * u, 1, 0)
        if l > 0:
            total = total + sz[side, l - 1] * us[l - 1]
        if l < layers - 1:
            total = total + sz[side, l] * us[l + 1]
        return total

    def strip_sweep(side, us):
        return [
            (1.0 - RELAX) * us[l] + sw[side, l] * strip_total(side, l, us) for l in range(layers)
        ]

    def lay_lines(k, rows_of):
        x = jnp.concatenate(
            rows_of + [jnp.zeros((LANES - 8 * layers, long), jnp.float32)], axis=0
        ).T
        lines[k, TOP : TOP + rows + 8, :] = x[0 : rows + 8]
        lines[k, TOP - 8 : TOP, :] = x[long - 8 : long]

    sub_long = iota((8, long), 0)

    def line_rows(l, fields, has_face):
        parts = []
        if has_face:
            parts = [shift(sy[1, l], -3, 0), shift(sy[0, l], -2, 0)]
        for left, right in fields:
            q = len(parts)
            parts.append(shift(right[l], q - 4, 0))
            parts.append(shift(sy[0, l] * left[l], q - 2, 0))
        x = parts[0]
        for q in range(1, len(parts)):
            x = jnp.where(sub_long == q, parts[q], x)
        return x

    smooth = []
    for side in range(2):
        below = None
        us = []
        for l in range(layers):
            k = strip[side, l]
            fx = inverse(k + shift(k, -1, 1))
            fy = inverse(k + shift(k, -1, 0))
            sx[side, l] = fx
            sy[side, l] = fy
            d = fx + shift(fx, 1, 1) + fy + shift(fy, 1, 0)
            d = d + (strip[side, 2 * layers] if l == 0 else below)
            if l < layers - 1:
                below = inverse(k + strip[side, l + 1])
                sz[side, l] = below
                d = d + below
            wt = guarded_weight(d)
            sw[side, l] = wt
            us.append(wt * strip[side, layers + l])
        new = strip_sweep(side, us)
        for l in range(layers):
            su[side, l] = new[l]
        smooth.append((us, new))
    fields = list(zip(*smooth))
    lay_lines(0, [line_rows(l, fields, True) for l in range(layers)])

    def whole(i):
        faces(i, lines[0, pl.ds(pl.multiple_of(i * 8, 8), 8), :])

    pl.loop(1, early, unroll=early - 1)(whole)

    @pl.loop(early, late, unroll=unroll_of(late - early))
    def _(i):
        here = pl.ds(pl.multiple_of(i * 8, 8), 8)
        line = lines[0, here, :]
        for l in range(layers):
            ends = line_ends(line, l, 0)
            zy[l, panes - 1, here, :] = jnp.where(last8, ends, zy[l, panes - 1, here, :])
            for p in range(panes):
                d = diag[l, p, here, :]
                if p == 0:
                    d = d + jnp.where(first8, ends, 0.0)
                if p == panes - 1:
                    d = d + jnp.where(last8, ends, 0.0)
                if p in (0, panes - 1):
                    diag[l, p, here, :] = d
                first_sweep(here, l, p, d)

    pl.loop(late, height // 8 - 1, unroll=height // 8 - 1 - late)(whole)

    def pulled(u, r, l, us, line, q):
        here = pl.ds(r, 8)
        fys = [zy[l, p, here, :] for p in range(panes)]
        flows = [fys[p] * us[l][p] for p in range(panes)]
        ends = line_ends(line, l, q)
        totals = []
        for p in range(panes):
            total = field[layers + l, p, here, :]
            total = total + zx[l, p, here, :] * row_below(u, l, p, r, us[l][p])
            total = total + zu[l, p, here, :] * row_above(u, l, p, r, us[l][p])
            total = total + fys[p] * from_right(us[l], p, ends) + from_left(flows, p, ends)
            if l > 0:
                total = total + zz[l - 1, p, here, :] * us[l - 1][p]
            if l < layers - 1:
                total = total + zz[l, p, here, :] * us[l + 1][p]
            totals.append(total)
        return totals

    def layers_at(u, r):
        return [[u[l, p, pl.ds(r, 8), :] for p in range(panes)] for l in range(layers)]

    def sweep(u, store, first, last, k, q):
        @pl.loop(first, last, unroll=unroll_of(last - first))
        def _(i):
            r = pl.multiple_of(i * 8, 8)
            us = layers_at(u, r)
            line = lines[k, pl.ds(r, 8), :]
            for l in range(layers):
                totals = pulled(u, r, l, us, line, q)
                for p in range(panes):
                    store(
                        l, p, r,
                        (1.0 - RELAX) * us[l][p] + weight[l, p, pl.ds(r, 8), :] * totals[p],
                    )

    def into(ref):
        def store(l, p, r, new):
            ref[l, p, pl.ds(r, 8), :] = new

        return store

    sweep(ua, into(ub), 1, height // 8 - 1, 0, 1)

    @pl.loop(0, crows, unroll=unroll_of(crows))
    def _(i):
        r = pl.multiple_of(i * 8 + TOP, 8)
        us = layers_at(ub, r)
        line = lines[0, pl.ds(r, 8), :]
        resids = [[] for _ in range(panes)]
        for l in range(layers):
            totals = pulled(ub, r, l, us, line, 2)
            for p in range(panes):
                resids[p].append(totals[p] - diag[l, p, pl.ds(r, 8), :] * us[l][p])
        for p in range(panes):
            sums[pl.ds(pl.multiple_of(i * 8, 8), 8), p * LANES : (p + 1) * LANES] = row_sums(
                resids[p]
            )

    gathered(layers, 2)
    lane_r = iota((crows, LANES), 1) % ccols
    rim[...] = jnp.where(
        (lane_r < HALO) | (lane_r >= ccols - HALO),
        rough[2],
        jnp.where(lane_r < 2 * HALO, shift(rough[3], HALO, 1), shift(rough[3], -HALO, 1)),
    )
    start_all(lambda k: rough_copy(k, 1), N_ROUGH)

    chigh = crows + 16

    def side_of(n, phase, tile):
        if phase == 0:
            return rough_side[n, tile]
        return shift(rim_side[n], (tile - 2) * (HALO if n else -HALO), 1)

    def join(phase):
        wait_all_recv(lambda k: rough_copy(k, phase), N_ROUGH)
        for f in range(layers + 1 if phase == 0 else layers):
            tile, q = 2 * phase + f // per, f % per
            target = f if phase == 0 else layers + 1 + f

            def joined(left, middle, right, size):
                lane = iota((size, LANES), 1)
                x = shift(middle, 8 - ccols * q, 1)
                x = jnp.where((lane >= 8) & (lane < 8 + ccols), x, 0.0)
                x = jnp.where(lane < 8, shift(left, 8 - ccols - ccols * q, 1), x)
                return jnp.where(
                    (lane >= 8 + ccols) & (lane < 16 + ccols),
                    shift(right, 8 + ccols - ccols * q, 1),
                    x,
                )

            wide[target, 8 : 8 + crows, :] = joined(
                side_of(1, phase, tile), rough[tile], side_of(0, phase, tile), crows
            )
            wide[target, 0:8, :] = joined(
                rough_corner[3, tile], rough_row[1, tile], rough_corner[2, tile], 8
            )
            wide[target, 8 + crows : chigh, :] = joined(
                rough_corner[1, tile], rough_row[0, tile], rough_corner[0, tile], 8
            )

    join(0)
    kc = [wide[l] * (0.5 / area) for l in range(layers)]
    cx = [harmonic(k, shift(k, -1, 0)) for k in kc]
    cy = [harmonic(k, shift(k, -1, 1)) for k in kc]
    cz = [harmonic(kc[l], kc[l + 1]) * area for l in range(layers - 1)]
    sums_of = []
    for l in range(layers):
        d = cx[l] + shift(cx[l], 1, 0) + cy[l] + shift(cy[l], 1, 1)
        if l == 0:
            d = d + wide[layers]
        else:
            d = d + cz[l - 1]
        sums_of.append(d + cz[l] if l < layers - 1 else d)

    gather_wait(0)
    span = tile_count * across
    parts = cell + 8
    spots = [(a, b) for a in range(-1, down + 1) for b in range(-1, across + 1)]
    wanted = []
    for a, b in spots:
        pr, pc = g * down + a, t * across + b
        inside = (pr >= 0) & (pr < grp_count * down) & (pc >= 0) & (pc < span)
        wanted.append(jnp.where(inside, pr * span + pc, -2).astype(jnp.float32))

    for lo in range(0, len(spots), across + 2):

        def add(d, acc, lo=lo):
            block = all_dies[d]
            where = all_dies[d, pl.ds(cell + 2, 1), :]
            return tuple(
                jnp.where(where == wanted[lo + j], block, a) for j, a in enumerate(acc)
            )

        acc = lax.fori_loop(
            0, count, add, tuple(jnp.zeros((parts, LANES), jnp.float32) for _ in range(across + 2)),
            unroll=unroll_of(count, 8),
        )
        lane_p = iota((parts, LANES), 1)
        line = jnp.zeros((parts, LANES), jnp.float32)
        for j in range(across + 2):
            x = acc[j]
            step = LANES // 2
            while step >= cell:
                x = x + shift(x, step, 1)
                step //= 2
            line = jnp.where(lane_p // cell == j, x, line)
        line = shift(line, 8 - cell, 1)
        a = lo // (across + 2) - 1
        if a == -1:
            first, size, off = 0, 8, cell - 8
        elif a == down:
            first, size, off = 8 + crows, 8, 0
        else:
            first, size, off = 8 + a * cell, cell, 0
        n = 2 * layers + 1
        wide[n, first : first + size, :] = line[off : off + size]
        wide[n + 1, first : first + size, :] = jnp.broadcast_to(
            line[cell : cell + 1], (size, LANES)
        )
        wide[n + 2, first : first + size, :] = jnp.broadcast_to(
            line[cell + 1 : cell + 2], (size, LANES)
        )

    top_rhs, top_c, top_b = (wide[2 * layers + 1 + j] for j in range(3))
    weights = [guarded_weight(d) for d in sums_of[:-1]] + [guarded_weight(sums_of[-1] + top_b)]
    crow = (iota((chigh, LANES), 0) + (cell - 8)) % cell
    ccol = (iota((chigh, LANES), 1) + (cell - 8)) % cell
    low_x, high_x = crow != 0, crow != cell - 1
    low_y, high_y = ccol != 0, ccol != cell - 1
    near = sum(jnp.where(m, one, none) for m in (low_x, high_x, low_y, high_y))
    top_d = top_c * near + top_b
    top_w = guarded_weight(top_d)
    join(1)
    errors = [weights[l] * wide[layers + 1 + l] for l in range(layers)]
    top = top_w * top_rhs
    def next_errors(errors, top):
        new = []
        for l in range(layers):
            e = errors[l]
            total = wide[layers + 1 + l]
            total = total + cx[l] * shift(e, -1, 0) + shift(cx[l] * e, 1, 0)
            total = total + cy[l] * shift(e, -1, 1) + shift(cy[l] * e, 1, 1)
            if l > 0:
                total = total + cz[l - 1] * errors[l - 1]
            total = total + (cz[l] * errors[l + 1] if l < layers - 1 else top_b * top)
            new.append((1.0 - RELAX) * e + weights[l] * total)
        return new

    def next_top(errors, top):
        nearby = (
            jnp.where(low_x, shift(top, 1, 0), 0.0)
            + jnp.where(high_x, shift(top, -1, 0), 0.0)
            + jnp.where(low_y, shift(top, 1, 1), 0.0)
            + jnp.where(high_y, shift(top, -1, 1), 0.0)
        )
        return top + top_w * (
            top_rhs + top_b * errors[layers - 1] + top_c * nearby - top_d * top
        )

    for _ in range(NC - 2):
        errors, top = next_errors(errors, top), next_top(errors, top)
    last_top, top = top, next_top(errors, top)

    lane_c = iota((cell, LANES), 1)
    fix = jnp.zeros((cell, LANES), jnp.float32)
    for a in range(down):
        piece = shift(top[8 + a * cell : 8 + (a + 1) * cell], a * ccols - 8, 1)
        fix = jnp.where(lane_c // ccols == a, piece, fix)
    row_f = iota((cell, LANES), 0)
    blocks = down * across
    short = all_fixes.shape[1]
    rest = cell - short
    stacks = short // rest if rest else 1

    def stored(j):
        return blocks + j // stacks, j % stacks

    if rest:
        for j in range(blocks):
            at, stack = stored(j)
            moved = shift(shift(fix, rest * stack - short, 0), cell * (at - j), 1)
            fix = jnp.where((lane_c // cell == at) & (row_f // rest == stack), moved, fix)
    all_fixes[me] = fix[:short]
    gather_start(1)
    errors = next_errors(errors, last_top)

    pick = (iota((LANES, cols), 0) == 8 + iota((LANES, cols), 1) // RATIO).astype(jnp.float32)
    fine = two_part_dot(jnp.concatenate(errors, axis=0), pick)
    for l in range(layers):
        for p in range(panes):
            spread[l, p] = fine[l * chigh : (l + 1) * chigh, p * LANES : (p + 1) * LANES]
    lane_s = iota((LANES, LANES), 1)
    wanted_lane = jnp.where(lane_s % 8 < HALO, 7, 8) + jnp.where(lane_s % 16 < 8, 0, ccols)
    wanted_lane = jnp.where(
        iota((LANES, LANES), 0) == wanted_lane, lane_s // 16, -1
    )
    sides_of = jnp.zeros((chigh, LANES), jnp.float32)
    for l in range(layers):
        sides_of = sides_of + two_part_dot(errors[l], (wanted_lane == l).astype(jnp.float32))
    along = iota((chigh, long), 1)
    coarse_row = jnp.where(along < rows + 64, along // RATIO + 8, 7)
    side_fix = two_part_dot(
        sides_of.T, (iota((chigh, long), 0) == coarse_row).astype(jnp.float32)
    )
    smooth = []
    for side in range(2):
        us = []
        for l in range(layers):
            at = 16 * l + 8 * side
            us.append(su[side, l] + side_fix[at : at + 8])
        smooth.append((us, strip_sweep(side, us)))
    fields = list(zip(*smooth))
    lay_lines(1, [line_rows(l, fields, False) for l in range(layers)])

    @pl.loop(1, height // 8 - 1)
    def _(i):
        r = pl.multiple_of(i * 8, 8)
        for l in range(layers):
            for p in range(panes):
                ub[l, p, pl.ds(r, 8), :] = ub[l, p, pl.ds(r, 8), :] + spread[l, p, pl.ds(i + 6, 1), :]

    sweep(ub, into(ua), 1, height // 8 - 1, 1, 0)

    def finish(l, p, r, new):
        out[l, pl.ds(r - TOP, 8), p * LANES : (p + 1) * LANES] = new

    sweep(ua, finish, TOP // 8, (height - TOP) // 8, 1, 1)

    wait_all_send(halo_copy, len(DIRECTIONS))
    for phase in range(2):
        wait_all_send(lambda k: rough_copy(k, phase), N_ROUGH)
    homes = []
    for s in range(slots):
        spot = jnp.maximum(place[s], 0)
        pr, pc = spot // span, lax.rem(spot, span)
        target = (pr // down) * tile_count + pc // across
        local = lax.rem(pr, down) * across + lax.rem(pc, across)
        homes.append((target, local))
    gather_wait(1)
    group = lane_c // cell
    cols_out = (iota((LANES, edge), 0) == iota((LANES, edge), 1) // RATIO).astype(jnp.float32)
    for s in range(slots):
        target, local = homes[s]
        block = all_fixes[target]
        if rest:
            block = jnp.concatenate([block, jnp.zeros((rest, LANES), jnp.float32)], axis=0)
            tail = jnp.where(
                (group == blocks + local // stacks) & (row_f // rest == lax.rem(local, stacks)),
                block, 0.0,
            )
            tail = sum(shift(tail, short - rest * n, 0) for n in range(stacks))
            x = jnp.where(row_f < short, jnp.where(group == local, block, 0.0), tail)
        else:
            x = jnp.where(group == local, block, 0.0)
        step = LANES // 2
        while step >= cell:
            x = x + shift(x, step, 1)
            step //= 2
        live = jnp.where(place[s] >= 0, 1.0, 0.0)
        fixed[s] = live * two_part_dot(x, cols_out)


def per_device(grp_count, tile_count, *args):
    material, die_power = args[0], args[4]
    layers, rows, cols = material.shape
    slots, edge, _ = die_power.shape
    cell = edge // RATIO
    crows = rows // RATIO
    panes, long, height = cols // LANES, rows + LANES, rows + 2 * TOP
    count = grp_count * tile_count
    n_fields = 2 * layers + 1
    depth = -(-n_fields * HALO // 8) * 8
    vmem = pl.BlockSpec(memory_space=pltpu.VMEM)
    smem = pl.BlockSpec(memory_space=pltpu.SMEM)
    far = pl.BlockSpec(memory_space=pl.ANY)
    f32 = jnp.float32

    def scratch(*shape):
        return pltpu.VMEM(shape, f32)

    grid = (layers, panes, height, LANES)
    heats = pl.pallas_call(
        functools.partial(kernel, grp_count, tile_count),
        out_shape=(
            pltpu.VMEM((layers, rows, cols), f32),
            pltpu.VMEM((2, slots, edge + 16, edge), f32),
            pltpu.VMEM((slots, cell, edge), f32),
            pltpu.VMEM((slots, edge, edge), f32),
        ),
        in_specs=[far, smem, far, far, far, smem, smem, smem],
        out_specs=(vmem,) * 4,
        scratch_shapes=[
            pltpu.VMEM(material.shape, material.dtype),
            scratch(rows, cols),
            scratch(layers, rows, cols),
            scratch(n_fields, panes, height, LANES),
            scratch(*grid),
            scratch(*grid),
            scratch(*grid),
            scratch(layers - 1, panes, height, LANES),
            scratch(*grid),
            scratch(*grid),
            scratch(*grid),
            scratch(*grid),
            scratch(rows, LANES),
            scratch(LANES, rows),
            scratch(2, depth, rows),
            scratch(3, LANES, LANES),
            scratch(2, n_fields, 8, long),
            scratch(2, layers, 8, long),
            scratch(2, layers, 8, long),
            scratch(2, layers - 1, 8, long),
            scratch(2, layers, 8, long),
            scratch(2, layers, 8, long),
            scratch(2, height, LANES),
            scratch(rows, cols),
            scratch(rows, LANES),
            scratch(4, crows, LANES),
            scratch(2, 4, crows, LANES),
            scratch(2, 4, 8, LANES),
            scratch(4, 4, 8, LANES),
            scratch(crows, LANES),
            scratch(2, crows, LANES),
            scratch(count, cell + 8, LANES),
            scratch(count, cell * cell * (rows // edge) * (cols // edge) // LANES, LANES),
            scratch(n_fields + 3, crows + 16, LANES),
            scratch(layers, panes, crows + 16, LANES),
            pltpu.SemaphoreType.DMA((len(DIRECTIONS) + 2 * N_ROUGH,)),
            pltpu.SemaphoreType.DMA((len(DIRECTIONS) + 2 * N_ROUGH,)),
            pltpu.SemaphoreType.DMA((2,)),
            pltpu.SemaphoreType.DMA((2,)),
            pltpu.SemaphoreType.DMA((3, unroll_of(rows // 8, 4))),
            pltpu.SemaphoreType.DMA,
        ],
        compiler_params=pltpu.CompilerParams(
            collective_id=0, has_side_effects=True, vmem_limit_bytes=60 * 1024 * 1024
        ),
    )(*args)

    return finish_dies(*heats, args[5], args[6], args[7])


def finish_kernel(
    heat, dies, fixed, die_power, die_conduct, bond, place, heat_out, die_out, work, done,
    heat_sem, die_sem,
):
    slots, edge, _ = die_power.shape
    body = pl.ds(8, edge)
    move = pltpu.make_async_copy(heat, heat_out, heat_sem)
    move.start()
    moves = []
    for at in (0, edge + 8):
        work[:, :, pl.ds(at, 8), :] = jnp.zeros((2, slots, 8, edge), jnp.float32)
    for s in range(slots):
        c, b = die_conduct[s], bond[s]
        live = jnp.where(place[s] >= 0, 1.0, 0.0)
        p = die_power[s]
        wt = die_diagonal(c, b, edge)[1]
        for k in range(edge // 8):
            work[0, s, pl.ds(8 + 8 * k, 8), :] = (
                dies[1, s, pl.ds(8 + 8 * k, 8), :] + fixed[s, pl.ds(k, 1), :]
            )
        for n in range(NU):
            now = work.at[n % 2, s]
            v = (1.0 - RELAX) * now[body, :] + wt * (p + c * around(now))
            if n < NU - 1:
                work[(n + 1) % 2, s, body, :] = v
        done[s] = live * v
        if s in (slots // 2 - 1, slots - 1):
            for ready in range(len(moves), s + 1):
                moves.append(
                    pltpu.make_async_copy(done.at[ready], die_out.at[ready], die_sem.at[ready])
                )
                moves[-1].start()
    for each in moves:
        each.wait()
    move.wait()


def finish_dies(heat, dies, fixed, die_power, *params):
    slots, edge, _ = die_power.shape
    near = [pltpu.with_memory_space_constraint(x, pltpu.VMEM) for x in (dies, fixed, die_power)]
    anywhere = pl.BlockSpec(memory_space=pl.ANY)
    vmem = pl.BlockSpec(memory_space=pltpu.VMEM)
    smem = pl.BlockSpec(memory_space=pltpu.SMEM)
    return pl.pallas_call(
        finish_kernel,
        out_shape=(
            jax.ShapeDtypeStruct(heat.shape, heat.dtype),
            jax.ShapeDtypeStruct(die_power.shape, die_power.dtype),
        ),
        in_specs=[anywhere] + [vmem] * 3 + [smem] * 3,
        out_specs=(anywhere, anywhere),
        scratch_shapes=[
            pltpu.VMEM(dies.shape, jnp.float32),
            pltpu.VMEM(die_power.shape, jnp.float32),
            pltpu.SemaphoreType.DMA,
            pltpu.SemaphoreType.DMA((slots,)),
        ],
        compiler_params=pltpu.CompilerParams(vmem_limit_bytes=8 * 1024 * 1024),
    )(heat, *near, *params)


def solution(mesh):
    placed = (
        P(None, "grp", "tile"),
        P(),
        P("grp", "tile"),
        P(None, "grp", "tile"),
        P(("grp", "tile"), None, None),
        P(("grp", "tile")),
        P(("grp", "tile")),
        P(("grp", "tile")),
    )
    return jax.shard_map(
        functools.partial(per_device, mesh.shape["grp"], mesh.shape["tile"]),
        mesh=mesh,
        in_specs=placed,
        out_specs=(P(None, "grp", "tile"), P(("grp", "tile"), None, None)),
        check_vma=False,
    )
```
